256 devices in a mesh: row: 16 (over x, y), col: 16 (over z, core).
Axes of the slice: x: 4, y: 4, z: 8, core: 2. Of those that a mesh axis runs over, the one named last changes fastest.
Arguments:
- src_points: float32 [73728, 64], P('row'), may hold values from -1.2 to 1.2
- dst_points: float32 [73728, 64], P(('col', 'row')), may hold values from -1.2 to 1.2
- dst_potential: float32 [73728], P(('col', 'row')), may hold values from -1.2 to 25.3
- partners: int32 [288, 28], P('row'), may hold values from 0 to 287, as said below
- partner_count: int32 [288], P('row'), may hold values from 14 to 28
- src_count: int32 [288], P('row'), may hold values from 64 to 256
- dst_count: int32 [288], P('col'), may hold values from 64 to 256
Outputs:
- src_potential: float32 [73728], P('row')
- dst_new: float32 [73728], P(('col', 'row'))
The draws below stay inside these ranges and needn't reach their ends.
Inputs may be any that keep to these rules, and one draw needn't show every extreme that they name: `partners`: row s holds 28 different tiles, each within 28 tiles of tile s * 1, counted around the end of the range, except that for even s slot 0 holds tile (s * 1 + 288 // 2) mod 288.
All inputs are finite; a program needn't handle non-finite values.
Results may differ from the reference program's by a relative error of at most 0.00029.
Values sent between devices are 32-bit elements; how exact they have to be, the bound alone decides.
No kernel may reach another device: no remote copies, remote signals or barrier semaphores. Data moves between devices by JAX's collectives and lax.ppermute only.
A program may use at most 128 MiB of HBM per device.

```python
import math
import jax
import jax.numpy as jnp
from jax import lax

D = 64
TILE = 256
KMAX = 28
ST = 288
TT = 288
NS = 73728
NT = 73728


def forced_counts(key, length, lowest, highest):
    first, second = jax.random.split(key)
    counts = jax.random.randint(first, (length,), lowest, highest + 1, dtype=jnp.int32)
    order = jax.random.permutation(second, length)
    counts = counts.at[order[0]].set(highest)
    counts = counts.at[order[1]].set(lowest)
    return counts.astype(jnp.int32)


def draw_partners(key, part):
    key = jax.random.fold_in(key, 11)
    lonely_key, pick_key = jax.random.split(key)
    lonely = 2 * jax.random.permutation(lonely_key, TT // 2)[:KMAX // 4].astype(jnp.int32) + 1
    barred = jnp.zeros((TT,), jnp.int32).at[lonely].set(1)
    window = 2 * KMAX + 1
    offsets = jnp.arange(window, dtype=jnp.int32) - KMAX
    sources = jnp.arange(ST, dtype=jnp.int32)
    centre = sources * TT // ST
    row_keys = jax.random.split(pick_key, ST)

    def one_row(single, middle, source):
        nearby = (middle + offsets + TT) % TT
        shuffled = jax.random.permutation(single, window).astype(jnp.int32)
        ranked = jnp.argsort(shuffled + window * barred[nearby], stable=True)
        near = nearby[ranked[:KMAX]]
        antipode = ((middle + TT // 2) % TT).astype(jnp.int32)
        with_far = jnp.concatenate([antipode[None], near[:KMAX - 1]])
        return jnp.where(source % 2 == 0, with_far, near)
    return jax.vmap(one_row)(row_keys, centre, sources).astype(jnp.int32)


def draw_partner_count(key, part):
    key = jax.random.fold_in(key, 23)
    return forced_counts(key, ST, KMAX // 2, KMAX)


def draw_src_count(key, part):
    key = jax.random.fold_in(key, 31)
    return forced_counts(key, ST, TILE // 4, TILE)


def draw_dst_count(key, part):
    key = jax.random.fold_in(key, 37)
    return forced_counts(key, TT, TILE // 4, TILE)


def draw_dst_potential(key, part):
    key = jax.random.fold_in(key, 41)
    return 0.3 * jnp.clip(jax.random.normal(key, (NT,), jnp.float32), -4.0, 4.0)


def levels(key, shape, pieces, smallest, top_value):
    factor_of, own = 1.0, jax.random.fold_in(key, 6)
    for axis_at, blocks in pieces:
        draws = jnp.exp(jax.random.uniform(jax.random.fold_in(own, axis_at), (blocks,), jnp.float32, smallest / len(pieces), top_value / len(pieces)))
        factor_of = factor_of * jnp.repeat(draws, shape[axis_at] // blocks).reshape([-1 if axis == axis_at else 1 for axis in range(len(shape))])
    return factor_of


def bell_draw(key, extent, scale, reach, shards=(), kind=jnp.bfloat16):
    values = jax.random.normal(key, extent, jnp.float32) * scale
    if len(shards) > 0:
        values = levels(key, extent, shards, -0.22, 0.18) * values
    return jnp.clip(values, min=-reach, max=reach).astype(kind)


def setup_inputs(seed: int = 0) -> dict:
    arg_keys = jax.random.split(jax.random.key(seed), 8)
    src_points = bell_draw(arg_keys[0], (NS, D), 0.2, 1.2, ((0, 16),), jnp.float32)
    dst_points = bell_draw(arg_keys[1], (NT, D), 0.2, 1.2, ((0, 256),), jnp.float32)
    dst_potential = draw_dst_potential(jax.random.fold_in(arg_keys[7], 71), 0)
    partners = draw_partners(jax.random.fold_in(arg_keys[7], 71), 0)
    partner_count = draw_partner_count(jax.random.fold_in(arg_keys[7], 71), 0)
    src_count = draw_src_count(jax.random.fold_in(arg_keys[7], 71), 0)
    dst_count = draw_dst_count(jax.random.fold_in(arg_keys[7], 71), 0)
    return {"src_points": src_points, "dst_points": dst_points, "dst_potential": dst_potential, "partners": partners, "partner_count": partner_count, "src_count": src_count, "dst_count": dst_count}


entropy = 0.1
masked_score = -1e30


def point_valid(counts):
    places = jnp.arange(TILE, dtype=jnp.int32)
    return places[None, :] < counts[:, None]


def reference(src_points, dst_points, dst_potential, partners, partner_count, src_count, dst_count):
    src_tiles = src_points.reshape(ST, TILE, D)
    dst_tiles = dst_points.reshape(TT, TILE, D)
    dst_values = dst_potential.reshape(TT, TILE)
    src_valid = point_valid(src_count)
    dst_valid = point_valid(dst_count)
    src_half = 0.5 * jnp.sum(src_tiles * src_tiles, axis=2)
    dst_half = 0.5 * jnp.sum(dst_tiles * dst_tiles, axis=2)
    slot_on = jnp.arange(KMAX, dtype=jnp.int32)[None, :] < partner_count[:, None]

    def tile_cost(index):
        chosen = partners[index]
        cross = jnp.einsum("id,kjd->kij", src_tiles[index], dst_tiles[chosen], precision=lax.Precision.HIGHEST)
        return (src_half[index][None, :, None] + dst_half[chosen][:, None, :]) - cross, chosen

    def source_pass(index):
        cost, chosen = tile_cost(index)
        live = slot_on[index][:, None, None] & dst_valid[chosen][:, None, :]
        score = jnp.where(live, (dst_values[chosen][:, None, :] - cost) / entropy, masked_score)
        highest = jnp.max(score, axis=(0, 2))
        summed = jnp.sum(jnp.where(live, jnp.exp(score - highest[None, :, None]), 0.0), axis=(0, 2))
        return highest, summed

    row_high, row_total = lax.map(source_pass, jnp.arange(ST, dtype=jnp.int32))
    src_mass = -jnp.log(src_count.astype(jnp.float32))[:, None] - math.log(ST)
    src_new = jnp.where(src_valid, entropy * (src_mass - (row_high + jnp.log(row_total))), 0.0)

    def target_pass(index):
        cost, chosen = tile_cost(index)
        live = slot_on[index][:, None, None] & src_valid[index][None, :, None]
        score = jnp.where(live, (src_new[index][None, :, None] - cost) / entropy, masked_score)
        highest = jnp.max(score, axis=1)
        summed = jnp.sum(jnp.where(live, jnp.exp(score - highest[:, None, :]), 0.0), axis=1)
        return highest, summed

    part_high, part_total = lax.map(target_pass, jnp.arange(ST, dtype=jnp.int32))
    segment = jnp.where(slot_on, partners, TT).reshape(-1).astype(jnp.int32)
    flat_high = part_high.reshape(ST * KMAX, TILE)
    flat_total = part_total.reshape(ST * KMAX, TILE)
    col_high = jax.ops.segment_max(flat_high, segment, num_segments=TT + 1)
    col_high = jnp.maximum(col_high, masked_score)
    scaled = flat_total * jnp.exp(flat_high - col_high[segment])
    col_total = jax.ops.segment_sum(scaled, segment, num_segments=TT + 1)[:TT]
    col_high = col_high[:TT]
    dst_mass = -jnp.log(dst_count.astype(jnp.float32))[:, None] - math.log(TT)
    col_lse = col_high + jnp.log(jnp.maximum(col_total, 1.0))
    dst_new = jnp.where(dst_valid & (col_total > 0.0), entropy * (dst_mass - col_lse), 0.0)
    return src_new.reshape(NS), dst_new.reshape(NT)
```

```python
import functools
import math

import jax
import jax.numpy as jnp
from jax import lax
from jax.experimental import pallas as pl
from jax.experimental.pallas import tpu as pltpu
from jax.sharding import PartitionSpec as P

entropy = 0.1
scale = math.log2(math.e) / entropy
ln2 = math.log(2.0)
nothing = -1e30
floor = -1e25
half = 128
wire_rows = 152
f32 = jnp.float32
bf16 = jnp.bfloat16


def pieces(a):
    first = a.astype(bf16).astype(f32)
    rest = a - first
    second = rest.astype(bf16).astype(f32)
    return first, second, rest - second


def extra_rows(bias):
    place = lax.broadcasted_iota(jnp.int32, (64, bias.shape[1]), 0)
    first, second, third = pieces(bias)
    block = jnp.where(place < 3, 1.0, 0.0)
    for k, piece in enumerate((first, second, third)):
        block = jnp.where(place == 3 + k, piece, block)
    return block.astype(bf16)


def prepare_sources(points_ref, main_ref, bias_ref):
    tiles, depth, tile = main_ref.shape
    for s in range(tiles):
        x = points_ref[:, s * tile : (s + 1) * tile]
        high = x.astype(bf16)
        low = (x - high.astype(f32)).astype(bf16)
        bias = (-0.5 * scale) * jnp.sum(x * x, axis=0, keepdims=True)
        main_ref[s, 0:64, :] = high
        main_ref[s, 64:128, :] = high
        main_ref[s, 128:192, :] = low
        main_ref[s, 192:256, :] = extra_rows(bias)
        bias_ref[s : s + 1, :] = bias


def unpack_targets(wire_ref, operand_ref):
    shards_held = wire_ref.shape[0]
    lane = lax.broadcasted_iota(jnp.int32, (144, 128), 1)
    front = lane < 64
    sublane = lax.broadcasted_iota(jnp.int32, (16, 256), 0)
    pick = (
        lax.broadcasted_iota(jnp.int32, (16, 128), 1)
        == lax.broadcasted_iota(jnp.int32, (16, 128), 0) + 64
    ) & (lax.broadcasted_iota(jnp.int32, (16, 128), 0) < 6)
    pick = jnp.where(pick, 1.0, 0.0).astype(bf16)

    def columns(row):
        first, second, third = pieces(row)
        stacked = jnp.where(sublane < 6, 1.0, 0.0)
        for k, piece in enumerate((first, second, third)):
            stacked = jnp.where(sublane == k, piece, stacked)
        return lax.dot_general(
            stacked.astype(bf16), pick, (((0,), (0,)), ((), ())), preferred_element_type=f32
        )[0:144]

    def one(m, carry):
        both = wire_ref[m, 0:144, :]
        high = both.astype(bf16).astype(f32)
        low = both - high
        high_back = pltpu.roll(high, 64, 1)
        low_back = pltpu.roll(low, 64, 1)
        tail = wire_ref[m, 144:152, :]
        extra_a = columns(jnp.concatenate([tail[0:1], tail[1:2]], axis=1))
        extra_b = columns(jnp.concatenate([tail[2:3], tail[3:4]], axis=1))
        start = pl.multiple_of(m * 288, 16)
        after = pl.multiple_of(m * 288 + 144, 16)
        operand_ref[pl.ds(start, 144), 0:128] = jnp.where(front, high, low_back).astype(bf16)
        operand_ref[pl.ds(start, 144), 128:256] = jnp.where(front, high, extra_a).astype(bf16)
        operand_ref[pl.ds(after, 144), 0:128] = jnp.where(front, high_back, low).astype(bf16)
        operand_ref[pl.ds(after, 144), 128:256] = jnp.where(front, high_back, extra_b).astype(bf16)
        return carry

    lax.fori_loop(0, shards_held, one, 0)
    rows = shards_held * 288
    dummy_lane = lax.broadcasted_iota(jnp.int32, (half, 256), 1)
    operand_ref[rows : rows + half, :] = jnp.where(dummy_lane == 192, nothing, 0.0).astype(bf16)


def row_pass(count_ref, list_ref, wire_ref, main_ref, lse_ref, operand_ref):
    tiles, depth, tile = main_ref.shape
    unpack_targets(wire_ref, operand_ref)

    def one_tile(s, carry):
        weights = main_ref[s]

        def score(unit):
            rows = operand_ref[pl.ds(pl.multiple_of(unit * half, half), half), :]
            return jnp.dot(rows, weights, preferred_element_type=f32).reshape(half // 8, 8, tile)

        def step(i, state):
            high, total = state
            one = score(list_ref[s, 2 * i])
            two = score(list_ref[s, 2 * i + 1])
            new = jnp.maximum(high, jnp.maximum(jnp.max(one, axis=0), jnp.max(two, axis=0)))
            total = total * jnp.exp2(high - new)
            total = total + jnp.sum(jnp.exp2(one - new[None]), axis=0)
            total = total + jnp.sum(jnp.exp2(two - new[None]), axis=0)
            return new, total

        start = (jnp.full((8, tile), floor, f32), jnp.zeros((8, tile), f32))
        high, total = lax.fori_loop(0, (count_ref[s] + 1) // 2, step, start)
        top = jnp.max(high, axis=0, keepdims=True)
        total = jnp.sum(total * jnp.exp2(high - top), axis=0, keepdims=True)
        lse_ref[pl.ds(s, 1), :] = jnp.where(
            total > 0.0, top + jnp.log2(jnp.maximum(total, 1e-30)), nothing
        )
        return carry

    lax.fori_loop(0, tiles, one_tile, 0)


def column_pass(
    count_ref, list_ref, live_ref, main_ref, operand_ref, bias_ref, out_ref,
    weights_ref, total_ref, high_ref, seen_ref,
):
    tiles, depth, tile = main_ref.shape
    units = out_ref.shape[0]

    def clear(u, carry):
        total_ref[pl.ds(pl.multiple_of(u * half, half), half), :] = jnp.zeros((half, 128), f32)
        seen_ref[u] = 0
        return carry

    def sweep(visit):
        def one_tile(s, carry):
            weights_ref[0:192, :] = main_ref[s, 0:192, :]
            weights_ref[192:256, :] = extra_rows(bias_ref[pl.ds(s, 1), :])

            def step(i, inner):
                for k in range(2):
                    unit = list_ref[s, 2 * i + k]
                    where = pl.ds(pl.multiple_of(unit * half, half), half)
                    visit(
                        unit,
                        where,
                        jnp.dot(
                            operand_ref[where, :], weights_ref[...], preferred_element_type=f32
                        ),
                    )
                return inner

            lax.fori_loop(0, (count_ref[s] + 1) // 2, step, 0)
            return carry

        lax.fori_loop(0, tiles, one_tile, 0)

    def add(unit, where, score):
        part = jnp.exp2(score)
        total_ref[where, :] += part[:, 0:128] + part[:, 128:256]
        seen_ref[unit] = 1

    lax.fori_loop(0, units + 1, clear, 0)
    sweep(add)
    ones = jnp.ones((8, 128), f32)
    lane = lax.broadcasted_iota(jnp.int32, (8, 128), 1)

    def lane_sums(block):
        return lax.dot_general(
            ones,
            block,
            (((1,), (1,)), ((), ())),
            precision=lax.Precision.HIGHEST,
            preferred_element_type=f32,
        )

    def finish(u, bad):
        where = pl.ds(pl.multiple_of(u * half, half), half)
        sums = lane_sums(total_ref[where, :])
        out_ref[pl.ds(u, 1), :] = jnp.where(
            sums > 0.0, jnp.log2(jnp.maximum(sums, 1e-37)), nothing
        )[0:1]
        needed = jnp.where(seen_ref[u] > 0, live_ref[u], 0)
        return jnp.maximum(bad, jnp.where((lane < needed) & (sums < 1e-25), 1.0, 0.0))

    bad = lax.fori_loop(0, units, finish, jnp.zeros((8, 128), f32))

    @pl.when(jnp.max(bad) > 0.0)
    def _():
        def clear_both(u, carry):
            where = pl.ds(pl.multiple_of(u * half, half), half)
            total_ref[where, :] = jnp.zeros((half, 128), f32)
            high_ref[where, :] = jnp.full((half, 128), floor, f32)
            return carry

        def add_safely(unit, where, score):
            one, two = score[:, 0:128], score[:, 128:256]
            old = high_ref[where, :]
            new = jnp.maximum(old, jnp.maximum(one, two))
            high_ref[where, :] = new
            total_ref[where, :] = (
                total_ref[where, :] * jnp.exp2(old - new)
                + jnp.exp2(one - new)
                + jnp.exp2(two - new)
            )

        def finish_safely(u, carry):
            where = pl.ds(pl.multiple_of(u * half, half), half)
            high = high_ref[where, :]
            top = jnp.max(high, axis=1, keepdims=True)
            sums = lane_sums(total_ref[where, :] * jnp.exp2(high - top))
            tops = lane_sums(jnp.where(lax.broadcasted_iota(jnp.int32, (half, 128), 1) == 0, top, 0.0))
            out_ref[pl.ds(u, 1), :] = jnp.where(
                sums > 0.0, tops + jnp.log2(jnp.maximum(sums, 1e-37)), nothing
            )[0:1]
            return carry

        lax.fori_loop(0, units + 1, clear_both, 0)
        sweep(add_safely)
        lax.fori_loop(0, units, finish_safely, 0)


def log_sum(parts):
    top = functools.reduce(jnp.maximum, parts)
    total = sum(jnp.exp2(p - top) for p in parts)
    return top + jnp.log2(total)


def shards(src_points, dst_points, dst_potential, partners, partner_count, src_count, dst_count):
    src_tiles = src_count.shape[0]
    dst_tiles = dst_count.shape[0]
    tile = src_points.shape[0] // src_tiles
    slots = partners.shape[1]
    rows = lax.axis_size("row")
    cols = lax.axis_size("col")
    row_here = lax.axis_index("row")
    col_here = lax.axis_index("col")
    share = dst_points.shape[0]
    units = 2 * dst_tiles
    smem = pl.BlockSpec(memory_space=pltpu.SMEM)
    vmem = pl.BlockSpec(memory_space=pltpu.VMEM)
    params = pltpu.CompilerParams(vmem_limit_bytes=48 * 1024 * 1024)

    spot = row_here * share + jnp.arange(share, dtype=jnp.int32)
    spot_tile = spot // tile
    spot_count = jnp.sum(
        jnp.where(
            spot_tile[:, None] == jnp.arange(dst_tiles, dtype=jnp.int32)[None, :],
            dst_count[None, :],
            0,
        ),
        axis=1,
    )
    mine_valid = spot - spot_tile * tile < spot_count
    level = scale * (dst_potential - 0.5 * jnp.sum(dst_points * dst_points, axis=1))
    level = jnp.where(mine_valid, level, nothing)
    mid = share // 2
    packed = scale * jnp.concatenate([dst_points[:mid], dst_points[mid:]], axis=1)
    tail = jnp.pad(level.reshape(2, mid), ((0, 0), (0, 256 - mid))).reshape(4, 128)
    wire = jnp.concatenate([packed, tail, jnp.zeros((4, 128), f32)], axis=0)
    gathered = lax.all_to_all(
        jnp.broadcast_to(wire[None], (rows,) + wire.shape), "row", 0, 0
    )

    main, bias = pl.pallas_call(
        prepare_sources,
        out_shape=(
            jax.ShapeDtypeStruct((src_tiles, 256, tile), bf16),
            jax.ShapeDtypeStruct((src_tiles, tile), f32),
        ),
        in_specs=[vmem],
        out_specs=(vmem, vmem),
        compiler_params=params,
    )(src_points.T)

    slot_on = jnp.arange(slots, dtype=jnp.int32)[None, :] < partner_count[:, None]
    local = jnp.where(slot_on, partners - col_here * dst_tiles, -1)
    unit_ids = jnp.arange(units, dtype=jnp.int32)
    live = jnp.clip(
        jnp.repeat(dst_count, 2) - (unit_ids % 2) * half, 0, half
    )
    active = jnp.any(local[:, :, None] == (unit_ids // 2)[None, None, :], axis=1) & (live > 0)[None, :]
    earlier = (unit_ids[:, None] < unit_ids[None, :]).astype(jnp.int32)
    rank = jnp.sum(jnp.where(active[:, :, None], earlier[None], 0), axis=1)
    counts = jnp.sum(active.astype(jnp.int32), axis=1)
    order = jnp.arange(units + 4, dtype=jnp.int32)
    listed = jnp.sum(
        jnp.where(
            active[:, :, None] & (rank[:, :, None] == order[None, None, :]),
            unit_ids[None, :, None],
            0,
        ),
        axis=1,
    )
    listed = jnp.where(order[None, :] < counts[:, None], listed, units)

    lse, operand = pl.pallas_call(
        row_pass,
        out_shape=(
            jax.ShapeDtypeStruct((src_tiles, tile), f32),
            jax.ShapeDtypeStruct((dst_tiles * tile + half, 256), bf16),
        ),
        in_specs=[smem, smem, vmem, vmem],
        out_specs=(vmem, vmem),
        compiler_params=params,
    )(counts, listed, gathered, main)

    reach = -(-slots // dst_tiles)
    steps = [d % cols for d in range(-reach, reach + 1)] + [cols // 2]
    idle = [d for d in range(cols) if d not in steps]
    mates = len(steps)

    def to(row, src, dst):
        return (row * cols + (row + src) % cols, row * cols + (row + dst) % cols)

    parts = [lse]
    for turn in range(1, mates):
        hops = [
            to(r, steps[a], steps[(a + turn) % mates]) for r in range(rows) for a in range(mates)
        ]
        parts.append(lax.ppermute(lse, ("row", "col"), hops))
    row_lse = log_sum(parts)
    counted = src_count.astype(f32)
    place = jnp.arange(tile, dtype=jnp.int32)
    src_live = place[None, :] < src_count[:, None]
    all_src = src_tiles * rows
    potential = jnp.where(
        src_live,
        entropy * (-jnp.log(counted)[:, None] - math.log(all_src) - ln2 * row_lse),
        0.0,
    )
    shared = potential.reshape(-1)
    member = functools.reduce(
        jnp.logical_or, [(col_here - row_here) % cols == d for d in steps]
    )
    src_potential = jnp.where(member, shared, 0.0)
    for begin in range(0, len(idle), mates):
        chunk = idle[begin : begin + mates]
        hops = [to(r, steps[a], d) for r in range(rows) for a, d in enumerate(chunk)]
        got = lax.ppermute(shared, ("row", "col"), hops)
        here = functools.reduce(
            jnp.logical_or, [(col_here - row_here) % cols == d for d in chunk]
        )
        src_potential = jnp.where(here, got, src_potential)

    mass_bias = jnp.where(
        src_live,
        bias - row_lse - jnp.log2(counted)[:, None] - math.log2(all_src),
        nothing,
    )
    col_part = pl.pallas_call(
        column_pass,
        out_shape=jax.ShapeDtypeStruct((units, half), f32),
        in_specs=[smem, smem, smem, vmem, vmem, vmem],
        out_specs=vmem,
        scratch_shapes=[
            pltpu.VMEM((256, tile), bf16),
            pltpu.VMEM((dst_tiles * tile + half, 128), f32),
            pltpu.VMEM((dst_tiles * tile + half, 128), f32),
            pltpu.SMEM((units + 1,), jnp.int32),
        ],
        compiler_params=params,
    )(counts, listed, live, main, operand, mass_bias)

    shared_out = lax.all_to_all(col_part.reshape(rows, share), "row", 0, 0)
    top = jnp.max(shared_out, axis=0)
    col_log = top + jnp.log2(jnp.sum(jnp.exp2(shared_out - top[None]), axis=0))
    dst_new = jnp.where(
        mine_valid & (top > 0.5 * nothing),
        entropy
        * (-jnp.log(spot_count.astype(f32)) - math.log(dst_tiles * cols) - ln2 * col_log)
        + dst_potential,
        0.0,
    )
    return src_potential, dst_new


def solution(mesh):
    in_specs = (
        P("row", None),
        P(("col", "row"), None),
        P(("col", "row")),
        P("row", None),
        P("row"),
        P("row"),
        P("col"),
    )
    out_specs = (P("row"), P(("col", "row")))
    return jax.shard_map(shards, mesh=mesh, in_specs=in_specs, out_specs=out_specs, check_vma=False)
```

```python
import functools
import math

import jax
import jax.numpy as jnp
from jax import lax
from jax.experimental import pallas as pl
from jax.experimental.pallas import tpu as pltpu
from jax.sharding import PartitionSpec as P

entropy = 0.1
scale = math.log2(math.e) / entropy
ln2 = math.log(2.0)
nothing = -1e30
floor = -1e25
unit_rows = 64
group = 12
f32 = jnp.float32
bf16 = jnp.bfloat16


def pieces(a):
    first = a.astype(bf16).astype(f32)
    rest = a - first
    second = rest.astype(bf16).astype(f32)
    return first, second, rest - second

def extra_rows(bias):
    place = lax.broadcasted_iota(jnp.int32, (64, bias.shape[1]), 0)
    block = jnp.where(place < 3, 1.0, 0.0)
    for k, piece in enumerate(pieces(bias)):
        block = jnp.where(place == 3 + k, piece, block)
    return block.astype(bf16)

def prepare_sources(points_ref, main_ref, bias_ref):
    tiles, depth, tile = main_ref.shape
    for s in range(tiles):
        x = points_ref[:, s * tile : (s + 1) * tile]
        high = x.astype(bf16)
        low = (x - high.astype(f32)).astype(bf16)
        bias = (-0.5 * scale) * jnp.sum(x * x, axis=0, keepdims=True)
        main_ref[s, 0:64, :] = high
        main_ref[s, 64:128, :] = high
        main_ref[s, 128:192, :] = low
        main_ref[s, 192:256, :] = extra_rows(bias)
        bias_ref[s : s + 1, :] = bias

def unpack_targets(wire_ref, operand_ref):
    lane = lax.broadcasted_iota(jnp.int32, (144, 128), 1)
    front = lane < 64
    sublane = lax.broadcasted_iota(jnp.int32, (16, 256), 0)
    r16 = lax.broadcasted_iota(jnp.int32, (16, 128), 0)
    l16 = lax.broadcasted_iota(jnp.int32, (16, 128), 1)
    pick = jnp.where((l16 == r16 + 64) & (r16 < 6), 1.0, 0.0).astype(bf16)

    def columns(row):
        stacked = jnp.where(sublane < 6, 1.0, 0.0)
        for k, piece in enumerate(pieces(row)):
            stacked = jnp.where(sublane == k, piece, stacked)
        return lax.dot_general(
            stacked.astype(bf16), pick, (((0,), (0,)), ((), ())), preferred_element_type=f32
        )[0:144]

    for m in range(wire_ref.shape[0]):
        both = wire_ref[m, 0:144, :]
        high = both.astype(bf16).astype(f32)
        low = both - high
        high_back = pltpu.roll(high, 64, 1)
        low_back = pltpu.roll(low, 64, 1)
        tail = wire_ref[m, 144:152, :]
        extra_a = columns(jnp.concatenate([tail[0:1], tail[1:2]], axis=1))
        extra_b = columns(jnp.concatenate([tail[2:3], tail[3:4]], axis=1))
        a = m * 288
        b = a + 144
        operand_ref[a : a + 144, 0:128] = jnp.where(front, high, low_back).astype(bf16)
        operand_ref[a : a + 144, 128:256] = jnp.where(front, high, extra_a).astype(bf16)
        operand_ref[b : b + 144, 0:128] = jnp.where(front, high_back, low).astype(bf16)
        operand_ref[b : b + 144, 128:256] = jnp.where(front, high_back, extra_b).astype(bf16)
    rows = wire_ref.shape[0] * 288
    dummy_lane = lax.broadcasted_iota(jnp.int32, (unit_rows, 256), 1)
    operand_ref[rows : rows + unit_rows, :] = jnp.where(dummy_lane == 192, nothing, 0.0).astype(bf16)

def pipeline(item_ref, list_ref, items, operand_ref, weights_ref, buffers, visit):
    per = list_ref.shape[1] // group

    def where(i):
        code = item_ref[i]
        s = code // per
        return s, (code - s * per) * group

    def units(i):
        s, first = where(i)
        return [list_ref[s, first + k] for k in range(group)]

    def multiply(i, buffer):
        s, first = where(i)
        rows = jnp.concatenate(
            [
                operand_ref[pl.ds(pl.multiple_of(u * unit_rows, unit_rows), unit_rows), :]
                for u in units(i)
            ],
            axis=0,
        )
        held = jnp.minimum(s, weights_ref.shape[0] - 1)
        buffer[...] = jnp.dot(rows, weights_ref[held], preferred_element_type=f32)

    one, two = buffers
    multiply(0, one)

    def step(j, carry):
        multiply(2 * j + 1, two)
        visit(jnp.minimum(where(2 * j)[0], weights_ref.shape[0] - 1), units(2 * j), one)
        multiply(2 * j + 2, one)
        visit(jnp.minimum(where(2 * j + 1)[0], weights_ref.shape[0] - 1), units(2 * j + 1), two)
        return carry

    lax.fori_loop(0, (items + 1) // 2, step, 0)

def row_pass(items_ref, item_ref, count_ref, list_ref, wire_ref, main_ref, need_ref, lse_ref, operand_ref, one, two, total_ref):
    tiles, depth, tile = main_ref.shape
    unpack_targets(wire_ref, operand_ref)
    total_ref[...] = jnp.zeros_like(total_ref)

    def visit(s, units, buffer):
        part = jnp.exp2(buffer[...]).reshape(4, unit_rows * group // 32, 8, tile)
        total_ref[s] += jnp.sum(jnp.sum(part, axis=1), axis=0)

    pipeline(item_ref, list_ref, items_ref[0], operand_ref, main_ref, (one, two), visit)
    total = jnp.sum(total_ref[...], axis=1)
    lse_ref[...] = jnp.where(total > 0.0, jnp.log2(jnp.maximum(total, 1e-37)), nothing)
    fine = (total > 1e-25) & (total < 1e30)
    bad = jnp.where(fine, 0.0, need_ref[...])

    @pl.when(jnp.max(bad) > 0.0)
    def _():
        def one_tile(s, carry):
            weights = main_ref[s]

            def step(i, state):
                high, total = state
                unit = list_ref[s, i]
                rows = operand_ref[pl.ds(pl.multiple_of(unit * unit_rows, unit_rows), unit_rows), :]
                score = jnp.dot(rows, weights, preferred_element_type=f32)
                score = score.reshape(unit_rows // 8, 8, tile)
                new = jnp.maximum(high, jnp.max(score, axis=0))
                total = total * jnp.exp2(high - new) + jnp.sum(jnp.exp2(score - new[None]), axis=0)
                return new, total

            start = (jnp.full((8, tile), floor, f32), jnp.zeros((8, tile), f32))
            high, total = lax.fori_loop(0, count_ref[s], step, start)
            top = jnp.max(high, axis=0, keepdims=True)
            total = jnp.sum(total * jnp.exp2(high - top), axis=0, keepdims=True)
            lse_ref[pl.ds(s, 1), :] = jnp.where(
                total > 0.0, top + jnp.log2(jnp.maximum(total, 1e-37)), nothing
            )
            return carry

        lax.fori_loop(0, tiles, one_tile, 0)

def column_pass(items_ref, item_ref, count_ref, list_ref, main_ref, operand_ref, bias_ref, need_ref, out_ref, one, two, weights_ref, total_ref, high_ref):
    tiles, depth, tile = main_ref.shape
    rows = total_ref.shape[0]
    weights_ref[:, 0:192, :] = main_ref[:, 0:192, :]
    for s in range(tiles):
        weights_ref[s, 192:256, :] = extra_rows(bias_ref[s : s + 1, :])
    total_ref[...] = jnp.zeros_like(total_ref)

    def visit(s, units, buffer):
        for k, u in enumerate(units):
            where = pl.ds(pl.multiple_of(u * unit_rows, unit_rows), unit_rows)
            part = jnp.exp2(buffer[k * unit_rows : (k + 1) * unit_rows, :])
            total_ref[where, :] += part[:, 0:128] + part[:, 128:256]

    pipeline(item_ref, list_ref, items_ref[0], operand_ref, weights_ref, (one, two), visit)
    eye = lax.broadcasted_iota(jnp.int32, (128, 128), 0) == lax.broadcasted_iota(jnp.int32, (128, 128), 1)

    def to_row(column):
        return jnp.sum(jnp.where(eye, column, 0.0), axis=0, keepdims=True)

    bad = jnp.zeros((1, 128), f32)
    for u in range(out_ref.shape[0]):
        sums = to_row(jnp.sum(total_ref[u * 128 : (u + 1) * 128, :], axis=1, keepdims=True))
        out_ref[u : u + 1, :] = jnp.where(sums > 0.0, jnp.log2(jnp.maximum(sums, 1e-37)), nothing)
        bad = jnp.maximum(bad, jnp.where(sums > 1e-25, 0.0, need_ref[u : u + 1, :]))

    @pl.when(jnp.max(bad) > 0.0)
    def _():
        total_ref[...] = jnp.zeros_like(total_ref)
        high_ref[...] = jnp.full_like(high_ref, floor)

        def one_tile(s, carry):
            def step(i, inner):
                unit = list_ref[s, i]
                where = pl.ds(pl.multiple_of(unit * unit_rows, unit_rows), unit_rows)
                score = jnp.dot(operand_ref[where, :], weights_ref[s], preferred_element_type=f32)
                a, b = score[:, 0:128], score[:, 128:256]
                old = high_ref[where, :]
                new = jnp.maximum(old, jnp.maximum(a, b))
                high_ref[where, :] = new
                total_ref[where, :] = (
                    total_ref[where, :] * jnp.exp2(old - new) + jnp.exp2(a - new) + jnp.exp2(b - new)
                )
                return inner

            lax.fori_loop(0, count_ref[s], step, 0)
            return carry

        lax.fori_loop(0, tiles, one_tile, 0)

        def finish(u, carry):
            where = pl.ds(pl.multiple_of(u * 128, 128), 128)
            high = high_ref[where, :]
            top = jnp.max(high, axis=1, keepdims=True)
            sums = to_row(jnp.sum(total_ref[where, :] * jnp.exp2(high - top), axis=1, keepdims=True))
            out_ref[pl.ds(u, 1), :] = jnp.where(
                sums > 0.0, to_row(top) + jnp.log2(jnp.maximum(sums, 1e-37)), nothing
            )
            return carry

        lax.fori_loop(0, out_ref.shape[0], finish, 0)


def log_sum(parts):
    top = functools.reduce(jnp.maximum, parts)
    total = sum(jnp.exp2(p - top) for p in parts)
    return top + jnp.log2(total)


def work_lists(partners, partner_count, dst_count, col_here):
    src_tiles, slots = partners.shape
    dst_tiles = dst_count.shape[0]
    per_tile = 256 // unit_rows
    units = dst_tiles * per_tile
    per = -(-units // group)
    slot_on = jnp.arange(slots, dtype=jnp.int32)[None, :] < partner_count[:, None]
    local = jnp.where(slot_on, partners - col_here * dst_tiles, -1)
    unit_ids = jnp.arange(units, dtype=jnp.int32)
    unit_tile = unit_ids // per_tile
    live = jnp.repeat(dst_count, per_tile) > (unit_ids % per_tile) * unit_rows
    active = jnp.any(local[:, :, None] == unit_tile[None, None, :], axis=1) & live[None, :]
    earlier = unit_ids[:, None] < unit_ids[None, :]
    rank = jnp.sum((active[:, :, None] & earlier[None]).astype(jnp.int32), axis=1)
    counts = jnp.sum(active.astype(jnp.int32), axis=1)
    order = jnp.arange(per * group, dtype=jnp.int32)
    listed = jnp.sum(
        jnp.where(
            active[:, :, None] & (rank[:, :, None] == order[None, None, :]),
            unit_ids[None, :, None] - units,
            0,
        ),
        axis=1,
    ) + units
    listed = jnp.concatenate([listed, jnp.full((1, per * group), units, jnp.int32)], axis=0)
    chunks = (counts + group - 1) // group
    tile_ids = jnp.arange(src_tiles, dtype=jnp.int32)
    first = jnp.sum(jnp.where(tile_ids[None, :] < tile_ids[:, None], chunks[None, :], 0), axis=1)
    within = jnp.arange(per, dtype=jnp.int32)
    spot = jnp.where(within[None, :] < chunks[:, None], first[:, None] + within[None, :], -1)
    code = tile_ids[:, None] * per + within[None, :] - src_tiles * per
    length = src_tiles * per + 2
    hit = spot.reshape(-1)[:, None] == jnp.arange(length, dtype=jnp.int32)[None, :]
    items = jnp.sum(jnp.where(hit, code.reshape(-1)[:, None], 0), axis=0) + src_tiles * per
    wanted = jnp.any(local[:, :, None] == jnp.arange(dst_tiles, dtype=jnp.int32), axis=1)
    return jnp.sum(chunks)[None], items, counts, listed, wanted


def shards(src_points, dst_points, dst_potential, partners, partner_count, src_count, dst_count):
    src_tiles = src_count.shape[0]
    dst_tiles = dst_count.shape[0]
    tile = src_points.shape[0] // src_tiles
    slots = partners.shape[1]
    rows = lax.axis_size("row")
    cols = lax.axis_size("col")
    row_here = lax.axis_index("row")
    col_here = lax.axis_index("col")
    share = dst_points.shape[0]
    points = dst_tiles * tile
    smem = pl.BlockSpec(memory_space=pltpu.SMEM)
    vmem = pl.BlockSpec(memory_space=pltpu.VMEM)
    params = pltpu.CompilerParams(vmem_limit_bytes=20 * 1024 * 1024)
    buffers = [pltpu.VMEM((unit_rows * group, tile), f32)] * 2

    spot = row_here * share + jnp.arange(share, dtype=jnp.int32)
    spot_tile = spot // tile
    spot_count = jnp.sum(
        jnp.where(
            spot_tile[:, None] == jnp.arange(dst_tiles, dtype=jnp.int32)[None, :],
            dst_count[None, :],
            0,
        ),
        axis=1,
    )
    mine_valid = spot - spot_tile * tile < spot_count
    level = scale * (dst_potential - 0.5 * jnp.sum(dst_points * dst_points, axis=1))
    level = jnp.where(mine_valid, level, nothing)
    mid = share // 2
    packed = scale * jnp.concatenate([dst_points[:mid], dst_points[mid:]], axis=1)
    tail = jnp.pad(level.reshape(2, mid), ((0, 0), (0, 256 - mid))).reshape(4, 128)
    wire = jnp.concatenate([packed, tail, jnp.zeros((4, 128), f32)], axis=0)
    gathered = lax.all_to_all(
        jnp.broadcast_to(wire[None], (rows,) + wire.shape), "row", 0, 0
    )

    main, bias = pl.pallas_call(
        prepare_sources,
        out_shape=(
            jax.ShapeDtypeStruct((src_tiles, 256, tile), bf16),
            jax.ShapeDtypeStruct((src_tiles, tile), f32),
        ),
        in_specs=[vmem],
        out_specs=(vmem, vmem),
        compiler_params=params,
    )(src_points.T)

    total_items, items, counts, listed, wanted = work_lists(
        partners, partner_count, dst_count, col_here
    )
    place = jnp.arange(tile, dtype=jnp.int32)
    src_live = place[None, :] < src_count[:, None]
    dst_live = place[None, :] < dst_count[:, None]
    src_need = jnp.where(src_live & (counts > 0)[:, None], 1.0, 0.0)
    dst_need = jnp.where(dst_live & jnp.any(wanted, axis=0)[:, None], 1.0, 0.0)
    dst_need = dst_need.reshape(points // 128, 128)

    lse, operand = pl.pallas_call(
        row_pass,
        out_shape=(
            jax.ShapeDtypeStruct((src_tiles, tile), f32),
            jax.ShapeDtypeStruct((points + unit_rows, 256), bf16),
        ),
        in_specs=[smem] * 4 + [vmem] * 3,
        out_specs=(vmem, vmem),
        scratch_shapes=buffers + [pltpu.VMEM((src_tiles, 8, tile), f32)],
        compiler_params=params,
    )(total_items, items, counts, listed, gathered, main, src_need)

    reach = -(-slots // dst_tiles)
    steps = [d % cols for d in range(-reach, reach + 1)] + [cols // 2]
    idle = [d for d in range(cols) if d not in steps]
    mates = len(steps)

    def to(row, src, dst):
        return (row * cols + (row + src) % cols, row * cols + (row + dst) % cols)

    parts = [lse]
    for turn in range(1, mates):
        hops = [
            to(r, steps[a], steps[(a + turn) % mates]) for r in range(rows) for a in range(mates)
        ]
        parts.append(lax.ppermute(lse, ("row", "col"), hops))
    row_lse = log_sum(parts)
    counted = src_count.astype(f32)
    all_src = src_tiles * rows
    potential = jnp.where(
        src_live,
        entropy * (-jnp.log(counted)[:, None] - math.log(all_src) - ln2 * row_lse),
        0.0,
    )
    shared = potential.reshape(-1)
    member = functools.reduce(
        jnp.logical_or, [(col_here - row_here) % cols == d for d in steps]
    )
    src_potential = jnp.where(member, shared, 0.0)
    for begin in range(0, len(idle), mates):
        chunk = idle[begin : begin + mates]
        hops = [to(r, steps[a], d) for r in range(rows) for a, d in enumerate(chunk)]
        got = lax.ppermute(shared, ("row", "col"), hops)
        here = functools.reduce(
            jnp.logical_or, [(col_here - row_here) % cols == d for d in chunk]
        )
        src_potential = jnp.where(here, got, src_potential)

    mass_bias = jnp.where(
        src_live,
        bias - row_lse - jnp.log2(counted)[:, None] - math.log2(all_src),
        nothing,
    )
    col_part = pl.pallas_call(
        column_pass,
        out_shape=jax.ShapeDtypeStruct((points // 128, 128), f32),
        in_specs=[smem] * 4 + [vmem] * 4,
        out_specs=vmem,
        scratch_shapes=buffers
        + [
            pltpu.VMEM((src_tiles, 256, tile), bf16),
            pltpu.VMEM((points + unit_rows, 128), f32),
            pltpu.VMEM((points + unit_rows, 128), f32),
        ],
        compiler_params=params,
    )(total_items, items, counts, listed, main, operand, mass_bias, dst_need)

    shared_out = lax.all_to_all(col_part.reshape(rows, share), "row", 0, 0)
    top = jnp.max(shared_out, axis=0)
    col_log = top + jnp.log2(jnp.sum(jnp.exp2(shared_out - top[None]), axis=0))
    dst_new = jnp.where(
        mine_valid & (top > 0.5 * nothing),
        entropy
        * (-jnp.log(spot_count.astype(f32)) - math.log(dst_tiles * cols) - ln2 * col_log)
        + dst_potential,
        0.0,
    )
    return src_potential, dst_new


def solution(mesh):
    in_specs = (
        P("row", None),
        P(("col", "row"), None),
        P(("col", "row")),
        P("row", None),
        P("row"),
        P("row"),
        P("col"),
    )
    out_specs = (P("row"), P(("col", "row")))
    return jax.shard_map(shards, mesh=mesh, in_specs=in_specs, out_specs=out_specs, check_vma=False)
```

```python
import functools
import math

import jax
import jax.numpy as jnp
from jax import lax
from jax.experimental import pallas as pl
from jax.experimental.pallas import tpu as pltpu
from jax.sharding import PartitionSpec as P

entropy = 0.1
scale = math.log2(math.e) / entropy
ln2 = math.log(2.0)
nothing = -1e30
floor = -1e25
unit_rows = 64
group = 12
ring = 4
f32 = jnp.float32
bf16 = jnp.bfloat16


def pieces(a):
    first = a.astype(bf16).astype(f32)
    rest = a - first
    second = rest.astype(bf16).astype(f32)
    return first, second, rest - second


def extra_rows(bias):
    place = lax.broadcasted_iota(jnp.int32, (64, bias.shape[1]), 0)
    block = jnp.where(place < 3, 1.0, 0.0)
    for k, piece in enumerate(pieces(bias)):
        block = jnp.where(place == 3 + k, piece, block)
    return block.astype(bf16)


def pack_targets(count_ref, points_ref, potential_ref, wire_ref, square_ref, line_ref):
    share = points_ref.shape[1]
    tile = 256
    mid = share // 2
    begin = lax.axis_index("row") * share
    first_tile = begin // tile
    offset = begin - first_tile * tile
    last_tile = jnp.minimum(first_tile + 1, count_ref.shape[0] - 1)
    points = points_ref[...]
    square_ref[...] = jnp.zeros_like(square_ref)
    square_ref[0:64, 0:share] = points
    turned = square_ref[...].T
    wire_ref[0:mid, :] = scale * (turned[0:mid] + pltpu.roll(turned[mid:share], 64, 1))
    level = scale * (potential_ref[...] - 0.5 * jnp.sum(points * points, axis=0, keepdims=True))
    spot = offset + lax.broadcasted_iota(jnp.int32, (1, share), 1)
    place = jnp.where(spot < tile, spot, spot - tile)
    bound = jnp.where(spot < tile, count_ref[first_tile], count_ref[last_tile])
    line_ref[...] = jnp.full_like(line_ref, nothing)
    line_ref[0:1, 0:share] = jnp.where(place < bound, level, nothing)
    wire_ref[mid : mid + 8, :] = jnp.zeros((8, 128), f32)
    for k in range(3):
        wire_ref[mid + k : mid + k + 1, :] = line_ref[0:1, 128 * k : 128 * (k + 1)]


def unpack_targets(held_ref, arrived, operand_ref):
    lane = lax.broadcasted_iota(jnp.int32, (144, 128), 1)
    front = lane < 64
    sublane = lax.broadcasted_iota(jnp.int32, (16, 384), 0)
    pick_row = lax.broadcasted_iota(jnp.int32, (16, 128), 0)
    pick_lane = lax.broadcasted_iota(jnp.int32, (16, 128), 1)
    pick = jnp.where((pick_lane == pick_row + 64) & (pick_row < 6), 1.0, 0.0).astype(bf16)
    row_here = lax.axis_index("row")
    x_here = row_here // ring
    y_here = row_here - x_here * ring
    for k in range(ring):
        arrived(k)
        x = lax.rem(x_here + ring - k, ring)
        for j in range(ring):
            y = lax.rem(y_here + ring - j, ring)
            a = pl.multiple_of((x * ring + y) * 288, 16)
            b = pl.multiple_of((x * ring + y) * 288 + 144, 16)
            both = held_ref[k, j, 0:144, :]
            high = both.astype(bf16).astype(f32)
            low = both - high
            high_back = pltpu.roll(high, 64, 1)
            low_back = pltpu.roll(low, 64, 1)
            tail = held_ref[k, j, 144:152, :]
            line = jnp.concatenate([tail[0:1], tail[1:2], tail[2:3]], axis=1)
            stacked = jnp.where(sublane < 6, 1.0, 0.0)
            for i, piece in enumerate(pieces(line)):
                stacked = jnp.where(sublane == i, piece, stacked)
            extra = lax.dot_general(
                stacked.astype(bf16), pick, (((0,), (0,)), ((), ())), preferred_element_type=f32
            )
            operand_ref[pl.ds(a, 144), 0:128] = jnp.where(front, high, low_back).astype(bf16)
            operand_ref[pl.ds(a, 144), 128:256] = jnp.where(front, high, extra[0:144]).astype(bf16)
            operand_ref[pl.ds(b, 144), 0:128] = jnp.where(front, high_back, low).astype(bf16)
            operand_ref[pl.ds(b, 144), 128:256] = jnp.where(
                front, high_back, extra[144:288]
            ).astype(bf16)
    rows = ring * ring * 288
    dummy_lane = lax.broadcasted_iota(jnp.int32, (unit_rows, 256), 1)
    operand_ref[rows : rows + unit_rows, :] = jnp.where(dummy_lane == 192, nothing, 0.0).astype(bf16)


def load_weights(points_ref, weights_ref, shift):
    tiles, depth, tile = weights_ref.shape
    for s in range(tiles):
        x = points_ref[:, s * tile : (s + 1) * tile]
        high = x.astype(bf16)
        low = (x - high.astype(f32)).astype(bf16)
        bias = (-0.5 * scale) * jnp.sum(x * x, axis=0, keepdims=True)
        weights_ref[s, 0:64, :] = high
        weights_ref[s, 64:128, :] = high
        weights_ref[s, 128:192, :] = low
        weights_ref[s, 192:256, :] = extra_rows(bias if shift is None else bias + shift[s : s + 1, :])


def load_all(points_ref, shift, wires, held_ref, sems, operand_ref, weights_ref):
    copies = [
        pltpu.make_async_copy(wire, held_ref.at[k], sems.at[k]) for k, wire in enumerate(wires)
    ]
    for copy in copies:
        copy.start()
    load_weights(points_ref, weights_ref, shift)
    unpack_targets(held_ref, lambda k: copies[k].wait(), operand_ref)


def pipeline(item_ref, list_ref, items, operand_ref, weights_ref, buffers, visit):
    per = list_ref.shape[1] // group
    last = weights_ref.shape[0] - 1

    def where(i):
        code = item_ref[i]
        s = code // per
        first = (code - s * per) * group
        return jnp.minimum(s, last), [list_ref[s, first + k] for k in range(group)]

    def multiply(i, buffer):
        s, units = where(i)
        rows = jnp.concatenate(
            [
                operand_ref[pl.ds(pl.multiple_of(u * unit_rows, unit_rows), unit_rows), :]
                for u in units
            ],
            axis=0,
        )
        buffer[...] = jnp.dot(rows, weights_ref[s], preferred_element_type=f32)

    one, two = buffers
    multiply(0, one)

    def step(j, carry):
        multiply(2 * j + 1, two)
        visit(*where(2 * j), one)
        multiply(2 * j + 2, one)
        visit(*where(2 * j + 1), two)
        return carry

    lax.fori_loop(0, (items + 1) // 2, step, 0)


def row_pass(
    items_ref, item_ref, count_ref, list_ref, points_ref, need_ref, w0, w1, w2, w3, lse_ref,
    held_ref, sems, operand_ref, weights_ref, one, two, total_ref,
):
    tiles, depth, tile = weights_ref.shape

    @pl.when(items_ref[0] == 0)
    def _():
        lse_ref[...] = jnp.full_like(lse_ref, nothing)

    @pl.when(items_ref[0] > 0)
    def _():
        load_all(points_ref, None, (w0, w1, w2, w3), held_ref, sems, operand_ref, weights_ref)
        total_ref[...] = jnp.zeros_like(total_ref)

        def visit(s, units, buffer):
            part = jnp.exp2(buffer[...]).reshape(4, unit_rows * group // 32, 8, tile)
            total_ref[s] += jnp.sum(jnp.sum(part, axis=1), axis=0)

        pipeline(item_ref, list_ref, items_ref[0], operand_ref, weights_ref, (one, two), visit)
        total = jnp.sum(total_ref[...], axis=1)
        lse_ref[...] = jnp.where(total > 0.0, jnp.log2(jnp.maximum(total, 1e-37)), nothing)
        fine = (total > 1e-25) & (total < 1e30)
        bad = jnp.where(fine, 0.0, need_ref[...])

        @pl.when(jnp.max(bad) > 0.0)
        def _():
            def one_tile(s, carry):
                weights = weights_ref[s]

                def step(i, state):
                    high, total = state
                    unit = list_ref[s, i]
                    rows = operand_ref[
                        pl.ds(pl.multiple_of(unit * unit_rows, unit_rows), unit_rows), :
                    ]
                    score = jnp.dot(rows, weights, preferred_element_type=f32)
                    score = score.reshape(unit_rows // 8, 8, tile)
                    new = jnp.maximum(high, jnp.max(score, axis=0))
                    total = total * jnp.exp2(high - new)
                    return new, total + jnp.sum(jnp.exp2(score - new[None]), axis=0)

                start = (jnp.full((8, tile), floor, f32), jnp.zeros((8, tile), f32))
                high, total = lax.fori_loop(0, count_ref[s], step, start)
                top = jnp.max(high, axis=0, keepdims=True)
                total = jnp.sum(total * jnp.exp2(high - top), axis=0, keepdims=True)
                lse_ref[pl.ds(s, 1), :] = jnp.where(
                    total > 0.0, top + jnp.log2(jnp.maximum(total, 1e-37)), nothing
                )
                return carry

            lax.fori_loop(0, tiles, one_tile, 0)


def column_pass(
    items_ref, item_ref, count_ref, list_ref, points_ref, need_ref, w0, w1, w2, w3, lse_ref,
    mass_ref, out_ref, held_ref, sems, operand_ref, weights_ref, one, two, total_ref, high_ref,
):
    tiles, depth, tile = weights_ref.shape

    @pl.when(items_ref[0] == 0)
    def _():
        out_ref[...] = jnp.full_like(out_ref, nothing)

    @pl.when(items_ref[0] > 0)
    def _():
        shift = mass_ref[...] - lse_ref[...]
        load_all(points_ref, shift, (w0, w1, w2, w3), held_ref, sems, operand_ref, weights_ref)
        total_ref[...] = jnp.zeros_like(total_ref)

        def visit(s, units, buffer):
            for k, u in enumerate(units):
                where = pl.ds(pl.multiple_of(u * unit_rows, unit_rows), unit_rows)
                part = jnp.exp2(buffer[k * unit_rows : (k + 1) * unit_rows, :])
                total_ref[where, :] += part[:, 0:128] + part[:, 128:256]

        pipeline(item_ref, list_ref, items_ref[0], operand_ref, weights_ref, (one, two), visit)
        eye = lax.broadcasted_iota(jnp.int32, (128, 128), 0) == lax.broadcasted_iota(
            jnp.int32, (128, 128), 1
        )

        def to_row(column):
            return jnp.sum(jnp.where(eye, column, 0.0), axis=0, keepdims=True)

        bad = jnp.zeros((1, 128), f32)
        for u in range(out_ref.shape[0]):
            sums = to_row(jnp.sum(total_ref[u * 128 : (u + 1) * 128, :], axis=1, keepdims=True))
            out_ref[u : u + 1, :] = jnp.where(
                sums > 0.0, jnp.log2(jnp.maximum(sums, 1e-37)), nothing
            )
            bad = jnp.maximum(bad, jnp.where(sums > 1e-25, 0.0, need_ref[u : u + 1, :]))

        @pl.when(jnp.max(bad) > 0.0)
        def _():
            total_ref[...] = jnp.zeros_like(total_ref)
            high_ref[...] = jnp.full_like(high_ref, floor)

            def one_tile(s, carry):
                def step(i, inner):
                    unit = list_ref[s, i]
                    where = pl.ds(pl.multiple_of(unit * unit_rows, unit_rows), unit_rows)
                    score = jnp.dot(
                        operand_ref[where, :], weights_ref[s], preferred_element_type=f32
                    )
                    a, b = score[:, 0:128], score[:, 128:256]
                    old = high_ref[where, :]
                    new = jnp.maximum(old, jnp.maximum(a, b))
                    high_ref[where, :] = new
                    total_ref[where, :] = (
                        total_ref[where, :] * jnp.exp2(old - new)
                        + jnp.exp2(a - new)
                        + jnp.exp2(b - new)
                    )
                    return inner

                lax.fori_loop(0, count_ref[s], step, 0)
                return carry

            lax.fori_loop(0, tiles, one_tile, 0)

            def finish(u, carry):
                where = pl.ds(pl.multiple_of(u * 128, 128), 128)
                high = high_ref[where, :]
                top = jnp.max(high, axis=1, keepdims=True)
                rest = total_ref[where, :] * jnp.exp2(high - top)
                sums = to_row(jnp.sum(rest, axis=1, keepdims=True))
                out_ref[pl.ds(u, 1), :] = jnp.where(
                    sums > 0.0, to_row(top) + jnp.log2(jnp.maximum(sums, 1e-37)), nothing
                )
                return carry

            lax.fori_loop(0, out_ref.shape[0], finish, 0)


def log_sum(parts):
    top = functools.reduce(jnp.maximum, parts)
    total = sum(jnp.exp2(p - top) for p in parts)
    return top + jnp.log2(total)


def work_lists(partners, partner_count, dst_count, col_here):
    src_tiles, slots = partners.shape
    dst_tiles = dst_count.shape[0]
    per_tile = 256 // unit_rows
    units = dst_tiles * per_tile
    per = -(-units // group)
    slot_on = jnp.arange(slots, dtype=jnp.int32)[None, :] < partner_count[:, None]
    local = jnp.where(slot_on, partners - col_here * dst_tiles, -1)
    unit_ids = jnp.arange(units, dtype=jnp.int32)
    unit_tile = unit_ids // per_tile
    live = jnp.repeat(dst_count, per_tile) > (unit_ids % per_tile) * unit_rows
    active = jnp.any(local[:, :, None] == unit_tile[None, None, :], axis=1) & live[None, :]
    earlier = unit_ids[:, None] < unit_ids[None, :]
    rank = jnp.sum((active[:, :, None] & earlier[None]).astype(jnp.int32), axis=1)
    counts = jnp.sum(active.astype(jnp.int32), axis=1)
    order = jnp.arange(per * group, dtype=jnp.int32)
    listed = jnp.sum(
        jnp.where(
            active[:, :, None] & (rank[:, :, None] == order[None, None, :]),
            unit_ids[None, :, None] - units,
            0,
        ),
        axis=1,
    ) + units
    listed = jnp.concatenate([listed, jnp.full((1, per * group), units, jnp.int32)], axis=0)
    chunks = (counts + group - 1) // group
    tile_ids = jnp.arange(src_tiles, dtype=jnp.int32)
    first = jnp.sum(jnp.where(tile_ids[None, :] < tile_ids[:, None], chunks[None, :], 0), axis=1)
    within = jnp.arange(per, dtype=jnp.int32)
    spot = jnp.where(within[None, :] < chunks[:, None], first[:, None] + within[None, :], -1)
    code = tile_ids[:, None] * per + within[None, :] - src_tiles * per
    length = src_tiles * per + 2
    hit = spot.reshape(-1)[:, None] == jnp.arange(length, dtype=jnp.int32)[None, :]
    items = jnp.sum(jnp.where(hit, code.reshape(-1)[:, None], 0), axis=0) + src_tiles * per
    wanted = jnp.any(local[:, :, None] == jnp.arange(dst_tiles, dtype=jnp.int32), axis=1)
    return jnp.sum(chunks), items, counts, listed, wanted


def roles(parity, cols):
    four = [d % cols for d in ((-2, -1, 0, 1), (-1, 0, 1, 2))[parity]]
    lead = [0, (1, -1)[parity] % cols]
    near = lead + [d for d in four if d not in lead]
    out = [(2, -2)[parity] % cols, cols // 2]
    return near, out + [d for d in range(cols) if d not in near and d not in out]


def shards(src_points, dst_points, dst_potential, partners, partner_count, src_count, dst_count):
    src_tiles = src_count.shape[0]
    dst_tiles = dst_count.shape[0]
    tile = src_points.shape[0] // src_tiles
    rows = lax.axis_size("row")
    cols = lax.axis_size("col")
    row_here = lax.axis_index("row")
    col_here = lax.axis_index("col")
    share = dst_points.shape[0]
    points = dst_tiles * tile
    smem = pl.BlockSpec(memory_space=pltpu.SMEM)
    vmem = pl.BlockSpec(memory_space=pltpu.VMEM)
    anywhere = pl.BlockSpec(memory_space=pl.ANY)
    params = pltpu.CompilerParams(vmem_limit_bytes=24 * 1024 * 1024)
    places = [roles(r % 2, cols) for r in range(rows)]
    near = [[(r + d) % cols for d in places[r][0]] for r in range(rows)]
    far = [[(r + d) % cols for d in places[r][1]] for r in range(rows)]
    turn = [
        0 if d in places[p][0] else 1 + places[p][1].index(d) // 4
        for p in range(2)
        for d in range(cols)
    ]
    at = row_here % 2 * cols + (col_here - row_here) % cols
    role = jnp.sum(
        jnp.where(jnp.arange(2 * cols) == at, jnp.array(turn, jnp.int32), 0), dtype=jnp.int32
    )
    in_near = role == 0

    def send(a, hops):
        return lax.ppermute(a, ("row", "col"), [(s[0] * cols + s[1], d[0] * cols + d[1]) for s, d in hops])

    every = [(r, c) for r in range(rows) for c in range(cols)]

    wire = pl.pallas_call(
        pack_targets,
        out_shape=jax.ShapeDtypeStruct((share // 2 + 8, 128), f32),
        in_specs=[smem, vmem, vmem],
        out_specs=vmem,
        scratch_shapes=[pltpu.VMEM((128, 384), f32), pltpu.VMEM((8, 384), f32)],
        compiler_params=params,
    )(dst_count, dst_points.T, dst_potential[None, :])

    def around(r, dx, dy):
        return (r // ring + dx) % ring * ring + (r + dy) % ring

    bundle = jnp.stack(
        [wire] + [send(wire, [((r, c), (around(r, 0, k), c)) for r, c in every]) for k in (1, 2, 3)]
    )
    busy = [set(near[r] + far[r][:2]) for r in range(rows)]
    wires = [bundle] + [
        send(
            bundle,
            [((r, c), (around(r, k, 0), c)) for r, c in every if c in busy[around(r, k, 0)]],
        )
        for k in (1, 2, 3)
    ]

    total_items, items, counts, listed, wanted = work_lists(
        partners, partner_count, dst_count, col_here
    )
    near_items = jnp.where(in_near, total_items, 0)[None]
    far_items = jnp.where(in_near, 0, total_items)[None]
    place = jnp.arange(tile, dtype=jnp.int32)
    src_live = place[None, :] < src_count[:, None]
    dst_live = place[None, :] < dst_count[:, None]
    src_need = jnp.where(src_live & (counts > 0)[:, None], 1.0, 0.0)
    dst_need = jnp.where(dst_live & jnp.any(wanted, axis=0)[:, None], 1.0, 0.0)
    dst_need = dst_need.reshape(points // 128, 128)
    counted = src_count.astype(f32)
    all_src = src_tiles * rows
    mass = jnp.where(src_live, -jnp.log2(counted)[:, None] - math.log2(all_src), nothing)

    scratch = [
        pltpu.VMEM((ring, ring) + wire.shape, f32),
        pltpu.SemaphoreType.DMA((ring,)),
        pltpu.VMEM((points + unit_rows, 256), bf16),
        pltpu.VMEM((src_tiles, 256, tile), bf16),
        pltpu.VMEM((unit_rows * group, tile), f32),
        pltpu.VMEM((unit_rows * group, tile), f32),
    ]
    heavy = pl.CostEstimate(flops=8_000_000_000, bytes_accessed=4_000_000, transcendentals=8_000_000)
    light = pl.CostEstimate(flops=100_000_000, bytes_accessed=100_000, transcendentals=100_000)
    turned = src_points.T

    def sum_rows(amount, cost):
        return pl.pallas_call(
            row_pass,
            out_shape=jax.ShapeDtypeStruct((src_tiles, tile), f32),
            in_specs=[smem] * 4 + [vmem] * 2 + [anywhere] * ring,
            out_specs=vmem,
            scratch_shapes=scratch + [pltpu.VMEM((src_tiles, 8, tile), f32)],
            compiler_params=params,
            cost_estimate=cost,
        )(amount, items, counts, listed, turned, src_need, *wires)

    def sum_columns(amount, lse, cost):
        return pl.pallas_call(
            column_pass,
            out_shape=jax.ShapeDtypeStruct((points // 128, 128), f32),
            in_specs=[smem] * 4 + [vmem] * 2 + [anywhere] * ring + [vmem] * 2,
            out_specs=vmem,
            scratch_shapes=scratch + [pltpu.VMEM((points + unit_rows, 128), f32)] * 2,
            compiler_params=params,
            cost_estimate=cost,
        )(amount, items, counts, listed, turned, dst_need, *wires, lse, mass)

    far_lse = sum_rows(far_items, light)
    early = send(far_lse, [((r, far[r][k]), (r, near[r][k])) for r in range(rows) for k in (0, 1)])
    near_lse = sum_rows(near_items, heavy)
    got_early = (col_here == row_here) | (col_here == row_here + 1 - 2 * (row_here % 2))
    lse = log_sum([near_lse, jnp.where(got_early, early, nothing)])
    lse = log_sum([lse, send(lse, [((r, c), (r, c ^ 1)) for r, c in every])])
    lse = log_sum(
        [
            lse,
            send(
                lse,
                [
                    ((r, c), (r, d))
                    for r in range(rows)
                    for c in near[r]
                    for d in near[r]
                    if (c - d) % cols in (2, cols - 2)
                ],
            ),
        ]
    )
    finals = [
        send(lse, [((r, near[r][k]), (r, far[r][4 * j + k])) for r in range(rows) for k in range(4)])
        for j in range(3)
    ]
    near_part = sum_columns(near_items, lse, heavy)
    far_part = sum_columns(far_items, finals[0], light)
    col_part = jnp.where(in_near, near_part, far_part)
    shared_out = lax.all_to_all(col_part.reshape(rows, share), "row", 0, 0)

    row_lse = lse
    for j in range(3):
        row_lse = jnp.where(role == j + 1, finals[j], row_lse)
    src_potential = jnp.where(
        src_live,
        entropy * (-jnp.log(counted)[:, None] - math.log(all_src) - ln2 * row_lse),
        0.0,
    ).reshape(-1)

    spot = row_here * share + jnp.arange(share, dtype=jnp.int32)
    spot_tile = spot // tile
    spot_count = jnp.sum(
        jnp.where(
            spot_tile[:, None] == jnp.arange(dst_tiles, dtype=jnp.int32)[None, :],
            dst_count[None, :],
            0,
        ),
        axis=1,
    )
    top = jnp.max(shared_out, axis=0)
    col_log = top + jnp.log2(jnp.sum(jnp.exp2(shared_out - top[None]), axis=0))
    dst_new = jnp.where(
        (spot - spot_tile * tile < spot_count) & (top > 0.5 * nothing),
        entropy
        * (-jnp.log(spot_count.astype(f32)) - math.log(dst_tiles * cols) - ln2 * col_log)
        + dst_potential,
        0.0,
    )
    return src_potential, dst_new


def solution(mesh):
    in_specs = (
        P("row", None),
        P(("col", "row"), None),
        P(("col", "row")),
        P("row", None),
        P("row"),
        P("row"),
        P("col"),
    )
    out_specs = (P("row"), P(("col", "row")))
    return jax.shard_map(shards, mesh=mesh, in_specs=in_specs, out_specs=out_specs, check_vma=False)
```

```python
import functools
import math

import jax
import jax.numpy as jnp
from jax import lax
from jax.experimental import pallas as pl
from jax.experimental.pallas import tpu as pltpu
from jax.sharding import PartitionSpec as P

entropy = 0.1
scale = math.log2(math.e) / entropy
ln2 = math.log(2.0)
nothing = -1e30
floor = -1e25
unit_rows = 64
group = 12
ring = 4
f32 = jnp.float32
bf16 = jnp.bfloat16


def pieces(a):
    first = a.astype(bf16).astype(f32)
    rest = a - first
    second = rest.astype(bf16).astype(f32)
    return first, second, rest - second


def extra_rows(bias):
    place = lax.broadcasted_iota(jnp.int32, (64, bias.shape[1]), 0)
    block = jnp.where(place < 3, 1.0, 0.0)
    for k, piece in enumerate(pieces(bias)):
        block = jnp.where(place == 3 + k, piece, block)
    return block.astype(bf16)


def pack_targets(count_ref, points_ref, potential_ref, wire_ref, square_ref, line_ref):
    share = points_ref.shape[1]
    tile = 256
    mid = share // 2
    begin = lax.axis_index("row") * share
    first_tile = begin // tile
    offset = begin - first_tile * tile
    last_tile = jnp.minimum(first_tile + 1, count_ref.shape[0] - 1)
    points = points_ref[...]
    square_ref[...] = jnp.zeros_like(square_ref)
    square_ref[0:64, 0:share] = points
    turned = square_ref[...].T
    wire_ref[0:mid, :] = scale * (turned[0:mid] + pltpu.roll(turned[mid:share], 64, 1))
    level = scale * (potential_ref[...] - 0.5 * jnp.sum(points * points, axis=0, keepdims=True))
    spot = offset + lax.broadcasted_iota(jnp.int32, (1, share), 1)
    place = jnp.where(spot < tile, spot, spot - tile)
    bound = jnp.where(spot < tile, count_ref[first_tile], count_ref[last_tile])
    line_ref[...] = jnp.full_like(line_ref, nothing)
    line_ref[0:1, 0:share] = jnp.where(place < bound, level, nothing)
    wire_ref[mid : mid + 8, :] = jnp.zeros((8, 128), f32)
    for k in range(3):
        wire_ref[mid + k : mid + k + 1, :] = line_ref[0:1, 128 * k : 128 * (k + 1)]


def unpack_targets(held_ref, arrived, operand_ref):
    lane = lax.broadcasted_iota(jnp.int32, (144, 128), 1)
    front = lane < 64
    sublane = lax.broadcasted_iota(jnp.int32, (16, 384), 0)
    pick_row = lax.broadcasted_iota(jnp.int32, (16, 128), 0)
    pick_lane = lax.broadcasted_iota(jnp.int32, (16, 128), 1)
    pick = jnp.where((pick_lane == pick_row + 64) & (pick_row < 6), 1.0, 0.0).astype(bf16)
    row_here = lax.axis_index("row")
    x_here = row_here // ring
    y_here = row_here - x_here * ring
    even = lax.rem(lax.axis_index("col"), 2) == 0
    for k in range(ring):
        arrived(k)
        for j in range(ring):
            x = lax.rem(x_here + ring - jnp.where(even, k, j), ring)
            y = lax.rem(y_here + ring - jnp.where(even, j, k), ring)
            a = pl.multiple_of((x * ring + y) * 288, 16)
            b = pl.multiple_of((x * ring + y) * 288 + 144, 16)
            both = held_ref[k, j, 0:144, :]
            high = both.astype(bf16).astype(f32)
            low = both - high
            high_back = pltpu.roll(high, 64, 1)
            low_back = pltpu.roll(low, 64, 1)
            tail = held_ref[k, j, 144:152, :]
            line = jnp.concatenate([tail[0:1], tail[1:2], tail[2:3]], axis=1)
            stacked = jnp.where(sublane < 6, 1.0, 0.0)
            for i, piece in enumerate(pieces(line)):
                stacked = jnp.where(sublane == i, piece, stacked)
            extra = lax.dot_general(
                stacked.astype(bf16), pick, (((0,), (0,)), ((), ())), preferred_element_type=f32
            )
            operand_ref[pl.ds(a, 144), 0:128] = jnp.where(front, high, low_back).astype(bf16)
            operand_ref[pl.ds(a, 144), 128:256] = jnp.where(front, high, extra[0:144]).astype(bf16)
            operand_ref[pl.ds(b, 144), 0:128] = jnp.where(front, high_back, low).astype(bf16)
            operand_ref[pl.ds(b, 144), 128:256] = jnp.where(
                front, high_back, extra[144:288]
            ).astype(bf16)
    rows = ring * ring * 288
    dummy_lane = lax.broadcasted_iota(jnp.int32, (unit_rows, 256), 1)
    operand_ref[rows : rows + unit_rows, :] = jnp.where(dummy_lane == 192, nothing, 0.0).astype(bf16)


def load_weights(points_ref, weights_ref, shift):
    tiles, depth, tile = weights_ref.shape
    for s in range(tiles):
        x = points_ref[:, s * tile : (s + 1) * tile]
        high = x.astype(bf16)
        low = (x - high.astype(f32)).astype(bf16)
        bias = (-0.5 * scale) * jnp.sum(x * x, axis=0, keepdims=True)
        weights_ref[s, 0:64, :] = high
        weights_ref[s, 64:128, :] = high
        weights_ref[s, 128:192, :] = low
        weights_ref[s, 192:256, :] = extra_rows(bias if shift is None else bias + shift[s : s + 1, :])


def load_all(points_ref, shift, wires, held_ref, sems, operand_ref, weights_ref):
    copies = [
        pltpu.make_async_copy(wire, held_ref.at[k], sems.at[k]) for k, wire in enumerate(wires)
    ]
    for copy in copies:
        copy.start()
    load_weights(points_ref, weights_ref, shift)
    unpack_targets(held_ref, lambda k: copies[k].wait(), operand_ref)


def pipeline(item_ref, list_ref, items, operand_ref, weights_ref, buffers, visit):
    per = list_ref.shape[1] // group
    last = weights_ref.shape[0] - 1

    def where(i):
        code = item_ref[i]
        s = code // per
        first = (code - s * per) * group
        return jnp.minimum(s, last), [list_ref[s, first + k] for k in range(group)]

    def multiply(i, buffer):
        s, units = where(i)
        rows = jnp.concatenate(
            [
                operand_ref[pl.ds(pl.multiple_of(u * unit_rows, unit_rows), unit_rows), :]
                for u in units
            ],
            axis=0,
        )
        buffer[...] = jnp.dot(rows, weights_ref[s], preferred_element_type=f32)

    one, two = buffers
    multiply(0, one)

    def step(j, carry):
        multiply(2 * j + 1, two)
        visit(*where(2 * j), one)
        multiply(2 * j + 2, one)
        visit(*where(2 * j + 1), two)
        return carry

    lax.fori_loop(0, (items + 1) // 2, step, 0)


def row_pass(
    items_ref, item_ref, count_ref, list_ref, points_ref, need_ref, w0, w1, w2, w3, lse_ref,
    held_ref, sems, operand_ref, weights_ref, one, two, total_ref,
):
    tiles, depth, tile = weights_ref.shape

    @pl.when(items_ref[0] == 0)
    def _():
        lse_ref[...] = jnp.full_like(lse_ref, nothing)

    @pl.when(items_ref[0] > 0)
    def _():
        load_all(points_ref, None, (w0, w1, w2, w3), held_ref, sems, operand_ref, weights_ref)
        total_ref[...] = jnp.zeros_like(total_ref)

        def visit(s, units, buffer):
            part = jnp.exp2(buffer[...]).reshape(4, unit_rows * group // 32, 8, tile)
            total_ref[s] += jnp.sum(jnp.sum(part, axis=1), axis=0)

        pipeline(item_ref, list_ref, items_ref[0], operand_ref, weights_ref, (one, two), visit)
        total = jnp.sum(total_ref[...], axis=1)
        lse_ref[...] = jnp.where(total > 0.0, jnp.log2(jnp.maximum(total, 1e-37)), nothing)
        fine = (total > 1e-25) & (total < 1e30)
        bad = jnp.where(fine, 0.0, need_ref[...])

        @pl.when(jnp.max(bad) > 0.0)
        def _():
            def one_tile(s, carry):
                weights = weights_ref[s]

                def step(i, state):
                    high, total = state
                    unit = list_ref[s, i]
                    rows = operand_ref[
                        pl.ds(pl.multiple_of(unit * unit_rows, unit_rows), unit_rows), :
                    ]
                    score = jnp.dot(rows, weights, preferred_element_type=f32)
                    score = score.reshape(unit_rows // 8, 8, tile)
                    new = jnp.maximum(high, jnp.max(score, axis=0))
                    total = total * jnp.exp2(high - new)
                    return new, total + jnp.sum(jnp.exp2(score - new[None]), axis=0)

                start = (jnp.full((8, tile), floor, f32), jnp.zeros((8, tile), f32))
                high, total = lax.fori_loop(0, count_ref[s], step, start)
                top = jnp.max(high, axis=0, keepdims=True)
                total = jnp.sum(total * jnp.exp2(high - top), axis=0, keepdims=True)
                lse_ref[pl.ds(s, 1), :] = jnp.where(
                    total > 0.0, top + jnp.log2(jnp.maximum(total, 1e-37)), nothing
                )
                return carry

            lax.fori_loop(0, tiles, one_tile, 0)


def column_pass(
    items_ref, item_ref, count_ref, list_ref, points_ref, need_ref, w0, w1, w2, w3, lse_ref,
    mass_ref, other_ref, out_ref, held_ref, sems, operand_ref, weights_ref, one, two, total_ref, high_ref,
):
    tiles, depth, tile = weights_ref.shape

    @pl.when(items_ref[0] == 0)
    def _():
        out_ref[...] = other_ref[...]

    @pl.when(items_ref[0] > 0)
    def _():
        shift = mass_ref[...] - lse_ref[...]
        load_all(points_ref, shift, (w0, w1, w2, w3), held_ref, sems, operand_ref, weights_ref)
        total_ref[...] = jnp.zeros_like(total_ref)

        def visit(s, units, buffer):
            for k, u in enumerate(units):
                where = pl.ds(pl.multiple_of(u * unit_rows, unit_rows), unit_rows)
                part = jnp.exp2(buffer[k * unit_rows : (k + 1) * unit_rows, :])
                total_ref[where, :] += part[:, 0:128] + part[:, 128:256]

        pipeline(item_ref, list_ref, items_ref[0], operand_ref, weights_ref, (one, two), visit)
        eye = lax.broadcasted_iota(jnp.int32, (128, 128), 0) == lax.broadcasted_iota(
            jnp.int32, (128, 128), 1
        )

        def to_row(column):
            return jnp.sum(jnp.where(eye, column, 0.0), axis=0, keepdims=True)

        bad = jnp.zeros((1, 128), f32)
        for u in range(out_ref.shape[0]):
            sums = to_row(jnp.sum(total_ref[u * 128 : (u + 1) * 128, :], axis=1, keepdims=True))
            out_ref[u : u + 1, :] = jnp.where(
                sums > 0.0, jnp.log2(jnp.maximum(sums, 1e-37)), nothing
            )
            bad = jnp.maximum(bad, jnp.where(sums > 1e-25, 0.0, need_ref[u : u + 1, :]))

        @pl.when(jnp.max(bad) > 0.0)
        def _():
            total_ref[...] = jnp.zeros_like(total_ref)
            high_ref[...] = jnp.full_like(high_ref, floor)

            def one_tile(s, carry):
                def step(i, inner):
                    unit = list_ref[s, i]
                    where = pl.ds(pl.multiple_of(unit * unit_rows, unit_rows), unit_rows)
                    score = jnp.dot(
                        operand_ref[where, :], weights_ref[s], preferred_element_type=f32
                    )
                    a, b = score[:, 0:128], score[:, 128:256]
                    old = high_ref[where, :]
                    new = jnp.maximum(old, jnp.maximum(a, b))
                    high_ref[where, :] = new
                    total_ref[where, :] = (
                        total_ref[where, :] * jnp.exp2(old - new)
                        + jnp.exp2(a - new)
                        + jnp.exp2(b - new)
                    )
                    return inner

                lax.fori_loop(0, count_ref[s], step, 0)
                return carry

            lax.fori_loop(0, tiles, one_tile, 0)

            def finish(u, carry):
                where = pl.ds(pl.multiple_of(u * 128, 128), 128)
                high = high_ref[where, :]
                top = jnp.max(high, axis=1, keepdims=True)
                rest = total_ref[where, :] * jnp.exp2(high - top)
                sums = to_row(jnp.sum(rest, axis=1, keepdims=True))
                out_ref[pl.ds(u, 1), :] = jnp.where(
                    sums > 0.0, to_row(top) + jnp.log2(jnp.maximum(sums, 1e-37)), nothing
                )
                return carry

            lax.fori_loop(0, out_ref.shape[0], finish, 0)


def log_sum(parts):
    top = functools.reduce(jnp.maximum, parts)
    total = sum(jnp.exp2(p - top) for p in parts)
    return top + jnp.log2(total)


def work_lists(partners, partner_count, dst_count, col_here):
    src_tiles, slots = partners.shape
    dst_tiles = dst_count.shape[0]
    per_tile = 256 // unit_rows
    units = dst_tiles * per_tile
    per = -(-units // group)
    slot_on = jnp.arange(slots, dtype=jnp.int32)[None, :] < partner_count[:, None]
    local = jnp.where(slot_on, partners - col_here * dst_tiles, -1)
    unit_ids = jnp.arange(units, dtype=jnp.int32)
    unit_tile = unit_ids // per_tile
    live = jnp.repeat(dst_count, per_tile) > (unit_ids % per_tile) * unit_rows
    active = jnp.any(local[:, :, None] == unit_tile[None, None, :], axis=1) & live[None, :]
    earlier = unit_ids[:, None] < unit_ids[None, :]
    rank = jnp.sum((active[:, :, None] & earlier[None]).astype(jnp.int32), axis=1)
    counts = jnp.sum(active.astype(jnp.int32), axis=1)
    order = jnp.arange(per * group, dtype=jnp.int32)
    listed = jnp.sum(
        jnp.where(
            active[:, :, None] & (rank[:, :, None] == order[None, None, :]),
            unit_ids[None, :, None] - units,
            0,
        ),
        axis=1,
    ) + units
    listed = jnp.concatenate([listed, jnp.full((1, per * group), units, jnp.int32)], axis=0)
    chunks = (counts + group - 1) // group
    tile_ids = jnp.arange(src_tiles, dtype=jnp.int32)
    first = jnp.sum(jnp.where(tile_ids[None, :] < tile_ids[:, None], chunks[None, :], 0), axis=1)
    within = jnp.arange(per, dtype=jnp.int32)
    spot = jnp.where(within[None, :] < chunks[:, None], first[:, None] + within[None, :], -1)
    code = tile_ids[:, None] * per + within[None, :] - src_tiles * per
    length = src_tiles * per + 2
    hit = spot.reshape(-1)[:, None] == jnp.arange(length, dtype=jnp.int32)[None, :]
    items = jnp.sum(jnp.where(hit, code.reshape(-1)[:, None], 0), axis=0) + src_tiles * per
    wanted = jnp.any(local[:, :, None] == jnp.arange(dst_tiles, dtype=jnp.int32), axis=1)
    return jnp.sum(chunks), items, counts, listed, wanted


def roles(parity, cols):
    four = [d % cols for d in ((-2, -1, 0, 1), (-1, 0, 1, 2))[parity]]
    lead = [0, (1, -1)[parity] % cols]
    near = lead + [d for d in four if d not in lead]
    out = [(2, -2)[parity] % cols, cols // 2]
    return near, out + [d for d in range(cols) if d not in near and d not in out]


def shards(src_points, dst_points, dst_potential, partners, partner_count, src_count, dst_count):
    src_tiles = src_count.shape[0]
    dst_tiles = dst_count.shape[0]
    tile = src_points.shape[0] // src_tiles
    rows = lax.axis_size("row")
    cols = lax.axis_size("col")
    row_here = lax.axis_index("row")
    col_here = lax.axis_index("col")
    share = dst_points.shape[0]
    points = dst_tiles * tile
    smem = pl.BlockSpec(memory_space=pltpu.SMEM)
    vmem = pl.BlockSpec(memory_space=pltpu.VMEM)
    anywhere = pl.BlockSpec(memory_space=pl.ANY)
    params = pltpu.CompilerParams(vmem_limit_bytes=24 * 1024 * 1024)
    places = [roles(r % 2, cols) for r in range(rows)]
    near = [[(r + d) % cols for d in places[r][0]] for r in range(rows)]
    far = [[(r + d) % cols for d in places[r][1]] for r in range(rows)]
    turn = [
        0 if d in places[p][0] else 1 + places[p][1].index(d) // 4
        for p in range(2)
        for d in range(cols)
    ]
    at = row_here % 2 * cols + (col_here - row_here) % cols
    role = jnp.sum(
        jnp.where(jnp.arange(2 * cols) == at, jnp.array(turn, jnp.int32), 0), dtype=jnp.int32
    )
    in_near = role == 0

    def send(a, hops):
        return lax.ppermute(a, ("row", "col"), [(s[0] * cols + s[1], d[0] * cols + d[1]) for s, d in hops])

    every = [(r, c) for r in range(rows) for c in range(cols)]

    wire = pl.pallas_call(
        pack_targets,
        out_shape=jax.ShapeDtypeStruct((share // 2 + 8, 128), f32),
        in_specs=[smem, vmem, vmem],
        out_specs=vmem,
        scratch_shapes=[pltpu.VMEM((128, 384), f32), pltpu.VMEM((8, 384), f32)],
        compiler_params=params,
    )(dst_count, dst_points.T, dst_potential[None, :])

    def around(r, dx, dy):
        return (r // ring + dx) % ring * ring + (r + dy) % ring

    def first_hop(r, c, k):
        return around(r, 0, k) if c % 2 == 0 else around(r, k, 0)

    def second_hop(r, c, k):
        return around(r, k, 0) if c % 2 == 0 else around(r, 0, k)

    bundle = jnp.stack(
        [wire]
        + [send(wire, [((r, c), (first_hop(r, c, k), c)) for r, c in every]) for k in (1, 2, 3)]
    )
    bundle, partners, partner_count, dst_count, src_count = lax.optimization_barrier(
        (bundle, partners, partner_count, dst_count, src_count)
    )
    busy = [set(near[r] + far[r][:2]) for r in range(rows)]
    wires = [bundle] + [
        send(
            bundle,
            [
                ((r, c), (second_hop(r, c, k), c))
                for r, c in every
                if c in busy[second_hop(r, c, k)]
            ],
        )
        for k in (1, 2, 3)
    ]

    total_items, items, counts, listed, wanted = work_lists(
        partners, partner_count, dst_count, col_here
    )
    near_items = jnp.where(in_near, total_items, 0)[None]
    far_items = jnp.where(in_near, 0, total_items)[None]
    place = jnp.arange(tile, dtype=jnp.int32)
    src_live = place[None, :] < src_count[:, None]
    dst_live = place[None, :] < dst_count[:, None]
    src_need = jnp.where(src_live & (counts > 0)[:, None], 1.0, 0.0)
    dst_need = jnp.where(dst_live & jnp.any(wanted, axis=0)[:, None], 1.0, 0.0)
    dst_need = dst_need.reshape(points // 128, 128)
    counted = src_count.astype(f32)
    all_src = src_tiles * rows
    mass = jnp.where(src_live, -jnp.log2(counted)[:, None] - math.log2(all_src), nothing)

    scratch = [
        pltpu.VMEM((ring, ring) + wire.shape, f32),
        pltpu.SemaphoreType.DMA((ring,)),
        pltpu.VMEM((points + unit_rows, 256), bf16),
        pltpu.VMEM((src_tiles, 256, tile), bf16),
        pltpu.VMEM((unit_rows * group, tile), f32),
        pltpu.VMEM((unit_rows * group, tile), f32),
    ]
    heavy = pl.CostEstimate(flops=8_000_000_000, bytes_accessed=4_000_000, transcendentals=8_000_000)
    light = pl.CostEstimate(flops=100_000_000, bytes_accessed=100_000, transcendentals=100_000)
    turned = src_points.T

    def sum_rows(amount, cost):
        return pl.pallas_call(
            row_pass,
            out_shape=jax.ShapeDtypeStruct((src_tiles, tile), f32),
            in_specs=[smem] * 4 + [vmem] * 2 + [anywhere] * ring,
            out_specs=vmem,
            scratch_shapes=scratch + [pltpu.VMEM((src_tiles, 8, tile), f32)],
            compiler_params=params,
            cost_estimate=cost,
        )(amount, items, counts, listed, turned, src_need, *wires)

    def sum_columns(amount, lse, other, cost):
        return pl.pallas_call(
            column_pass,
            out_shape=jax.ShapeDtypeStruct((points // 128, 128), f32),
            in_specs=[smem] * 4 + [vmem] * 2 + [anywhere] * ring + [vmem] * 3,
            out_specs=vmem,
            scratch_shapes=scratch + [pltpu.VMEM((points + unit_rows, 128), f32)] * 2,
            compiler_params=params,
            cost_estimate=cost,
        )(amount, items, counts, listed, turned, dst_need, *wires, lse, mass, other)

    far_lse = sum_rows(far_items, light)
    early = send(far_lse, [((r, far[r][k]), (r, near[r][k])) for r in range(rows) for k in (0, 1)])
    near_lse = sum_rows(near_items, heavy)
    got_early = (col_here == row_here) | (col_here == row_here + 1 - 2 * (row_here % 2))
    lse = log_sum([near_lse, jnp.where(got_early, early, nothing)])
    lse = log_sum([lse, send(lse, [((r, c), (r, c ^ 1)) for r, c in every])])
    lse = log_sum(
        [
            lse,
            send(
                lse,
                [
                    ((r, c), (r, d))
                    for r in range(rows)
                    for c in near[r]
                    for d in near[r]
                    if (c - d) % cols in (2, cols - 2)
                ],
            ),
        ]
    )
    def final(a, j):
        return send(
            a, [((r, near[r][k]), (r, far[r][4 * j + k])) for r in range(rows) for k in range(4)]
        )

    blank = jnp.full((points // 128, 128), nothing, f32)
    finals = [final(lse, 0)]
    near_part = sum_columns(near_items, lse, blank, heavy)
    late, near_part = lax.optimization_barrier((lse, near_part))
    finals += [final(late, 1), final(late, 2)]
    col_part = sum_columns(far_items, finals[0], near_part, light)
    shared_out = lax.all_to_all(col_part.reshape(rows, share), "row", 0, 0)

    row_lse = lse
    for j in range(3):
        row_lse = jnp.where(role == j + 1, finals[j], row_lse)
    src_potential = jnp.where(
        src_live,
        entropy * (-jnp.log(counted)[:, None] - math.log(all_src) - ln2 * row_lse),
        0.0,
    ).reshape(-1)

    spot = row_here * share + jnp.arange(share, dtype=jnp.int32)
    spot_tile = spot // tile
    spot_count = jnp.sum(
        jnp.where(
            spot_tile[:, None] == jnp.arange(dst_tiles, dtype=jnp.int32)[None, :],
            dst_count[None, :],
            0,
        ),
        axis=1,
    )
    top = jnp.max(shared_out, axis=0)
    col_log = top + jnp.log2(jnp.sum(jnp.exp2(shared_out - top[None]), axis=0))
    dst_new = jnp.where(
        (spot - spot_tile * tile < spot_count) & (top > 0.5 * nothing),
        entropy
        * (-jnp.log(spot_count.astype(f32)) - math.log(dst_tiles * cols) - ln2 * col_log)
        + dst_potential,
        0.0,
    )
    return src_potential, dst_new


def solution(mesh):
    in_specs = (
        P("row", None),
        P(("col", "row"), None),
        P(("col", "row")),
        P("row", None),
        P("row"),
        P("row"),
        P("col"),
    )
    out_specs = (P("row"), P(("col", "row")))
    return jax.shard_map(shards, mesh=mesh, in_specs=in_specs, out_specs=out_specs, check_vma=False)
```

```python
import functools
import math

import jax
import jax.numpy as jnp
from jax import lax
from jax.experimental import pallas as pl
from jax.experimental.pallas import tpu as pltpu
from jax.sharding import PartitionSpec as P

entropy = 0.1
scale = math.log2(math.e) / entropy
ln2 = math.log(2.0)
nothing = -1e30
floor = -1e25
unit_rows = 64
group = 12
span = 8
ring = 4
f32 = jnp.float32
bf16 = jnp.bfloat16


def pieces(a):
    first = a.astype(bf16).astype(f32)
    rest = a - first
    second = rest.astype(bf16).astype(f32)
    return first, second, rest - second


def extra_rows(bias):
    place = lax.broadcasted_iota(jnp.int32, (64, bias.shape[1]), 0)
    block = jnp.where(place < 3, 1.0, 0.0)
    for k, piece in enumerate(pieces(bias)):
        block = jnp.where(place == 3 + k, piece, block)
    return block.astype(bf16)


def pack_targets(count_ref, points_ref, potential_ref, wire_ref, square_ref, line_ref):
    share = points_ref.shape[1]
    tile = 256
    mid = share // 2
    begin = lax.axis_index("row") * share
    first_tile = begin // tile
    offset = begin - first_tile * tile
    last_tile = jnp.minimum(first_tile + 1, count_ref.shape[0] - 1)
    points = points_ref[...]
    square_ref[...] = jnp.zeros_like(square_ref)
    square_ref[0:64, 0:share] = points
    turned = square_ref[...].T
    wire_ref[0:mid, :] = scale * (turned[0:mid] + pltpu.roll(turned[mid:share], 64, 1))
    level = scale * (potential_ref[...].reshape(1, share) - 0.5 * jnp.sum(points * points, axis=0, keepdims=True))
    spot = offset + lax.broadcasted_iota(jnp.int32, (1, share), 1)
    place = jnp.where(spot < tile, spot, spot - tile)
    bound = jnp.where(spot < tile, count_ref[first_tile], count_ref[last_tile])
    line_ref[...] = jnp.full_like(line_ref, nothing)
    line_ref[0:1, 0:share] = jnp.where(place < bound, level, nothing)
    wire_ref[mid : mid + 8, :] = jnp.zeros((8, 128), f32)
    for k in range(3):
        wire_ref[mid + k : mid + k + 1, :] = line_ref[0:1, 128 * k : 128 * (k + 1)]


def unpack_targets(held_ref, arrived, operand_ref):
    lane = lax.broadcasted_iota(jnp.int32, (144, 128), 1)
    front = lane < 64
    sublane = lax.broadcasted_iota(jnp.int32, (16, 384), 0)
    pick_row = lax.broadcasted_iota(jnp.int32, (16, 128), 0)
    pick_lane = lax.broadcasted_iota(jnp.int32, (16, 128), 1)
    pick = jnp.where((pick_lane == pick_row + 64) & (pick_row < 6), 1.0, 0.0).astype(bf16)
    row_here = lax.axis_index("row")
    x_here = row_here // ring
    y_here = row_here - x_here * ring
    even = lax.rem(lax.axis_index("col"), 2) == 0
    for k in range(ring):
        arrived(k)
        for j in range(ring):
            x = lax.rem(x_here + ring - jnp.where(even, k, j), ring)
            y = lax.rem(y_here + ring - jnp.where(even, j, k), ring)
            a = pl.multiple_of((x * ring + y) * 288, 16)
            b = pl.multiple_of((x * ring + y) * 288 + 144, 16)
            both = held_ref[k, j, 0:144, :]
            high = both.astype(bf16).astype(f32)
            low = both - high
            high_back = pltpu.roll(high, 64, 1)
            low_back = pltpu.roll(low, 64, 1)
            tail = held_ref[k, j, 144:152, :]
            line = jnp.concatenate([tail[0:1], tail[1:2], tail[2:3]], axis=1)
            stacked = jnp.where(sublane < 6, 1.0, 0.0)
            for i, piece in enumerate(pieces(line)):
                stacked = jnp.where(sublane == i, piece, stacked)
            extra = lax.dot_general(
                stacked.astype(bf16), pick, (((0,), (0,)), ((), ())), preferred_element_type=f32
            )
            operand_ref[pl.ds(a, 144), 0:128] = jnp.where(front, high, low_back).astype(bf16)
            operand_ref[pl.ds(a, 144), 128:256] = jnp.where(front, high, extra[0:144]).astype(bf16)
            operand_ref[pl.ds(b, 144), 0:128] = jnp.where(front, high_back, low).astype(bf16)
            operand_ref[pl.ds(b, 144), 128:256] = jnp.where(
                front, high_back, extra[144:288]
            ).astype(bf16)
    rows = ring * ring * 288
    dummy_lane = lax.broadcasted_iota(jnp.int32, (unit_rows, 256), 1)
    operand_ref[rows : rows + unit_rows, :] = jnp.where(dummy_lane == 192, nothing, 0.0).astype(bf16)


def load_weights(points_ref, weights_ref, shift):
    tiles, depth, tile = weights_ref.shape
    for s in range(tiles):
        x = points_ref[:, s * tile : (s + 1) * tile]
        high = x.astype(bf16)
        low = (x - high.astype(f32)).astype(bf16)
        bias = (-0.5 * scale) * jnp.sum(x * x, axis=0, keepdims=True)
        weights_ref[s, 0:64, :] = high
        weights_ref[s, 64:128, :] = high
        weights_ref[s, 128:192, :] = low
        weights_ref[s, 192:256, :] = extra_rows(bias if shift is None else bias + shift[s : s + 1, :])


def load_all(points_ref, shift, wires, held_ref, sems, operand_ref, weights_ref):
    copies = [
        pltpu.make_async_copy(wire, held_ref.at[k], sems.at[k]) for k, wire in enumerate(wires)
    ]
    for copy in copies:
        copy.start()
    load_weights(points_ref, weights_ref, shift)
    unpack_targets(held_ref, lambda k: copies[k].wait(), operand_ref)


def plan_work(count_ref, local_ref, plan_ref):
    src_tiles = local_ref.shape[0] - 6
    per_tile = 256 // unit_rows
    units = count_ref.shape[0] * per_tile
    per = units // group
    unit = lax.broadcasted_iota(jnp.int32, (24, 128), 1)
    tile_of = unit // per_tile
    bound = jnp.zeros((24, 128), jnp.int32)
    for t in range(count_ref.shape[0]):
        bound = jnp.where(tile_of == t, count_ref[t], bound)
    live = bound > (unit - tile_of * per_tile) * unit_rows
    hits = jnp.zeros((24, 128), f32)
    for k in range(local_ref.shape[1]):
        hits = jnp.where(local_ref[:, k : k + 1] == tile_of, 1.0, hits)
    active = jnp.where(live, hits, 0.0)
    down = lax.broadcasted_iota(jnp.int32, (128, 128), 0)
    across = lax.broadcasted_iota(jnp.int32, (128, 128), 1)
    upto = jnp.where(down <= across, 1.0, 0.0).astype(bf16)
    rank = jnp.dot(active.astype(bf16), upto, preferred_element_type=f32)
    counts = jnp.broadcast_to(rank[:, 127:128], (24, 128))
    place = jnp.where(active > 0.0, rank - 1.0, -1.0)
    place = jnp.concatenate([place, jnp.full((104, 128), -1.0, f32)], axis=0).T
    position = across.astype(f32)
    value = (down - units).astype(f32)
    plan_ref[...] = jnp.full_like(plan_ref, units)
    last = lax.broadcasted_iota(jnp.int32, (1, 128), 1)
    chunks = jnp.floor((counts + (group - 0.5)) / group).astype(jnp.int32)
    begin = jnp.zeros((1, 128), jnp.int32)
    items = jnp.full((1, 128), src_tiles * per, jnp.int32)
    for s in range(src_tiles):
        listed = jnp.sum(
            jnp.where(place[:, s : s + 1] == position, value, 0.0), axis=0, keepdims=True
        )
        plan_ref[s : s + 1, :] = jnp.where(
            last == 127, counts[s : s + 1], listed + units
        ).astype(jnp.int32)
        along = last - begin
        inside = (along >= 0) & (along < chunks[s : s + 1])
        items = jnp.where(inside, s * per + along, items)
        begin = begin + chunks[s : s + 1]
    plan_ref[src_tiles + 1 : src_tiles + 2, :] = items
    row = lax.axis_index("row")
    apart = lax.axis_index("col") - row + 2 - lax.rem(row, 2) + 16
    near = jnp.where(lax.rem(apart, 16) < 4, 1, 0)
    plan_ref[src_tiles + 2 : src_tiles + 3, :] = begin * jnp.where(last == 0, near, 1 - near)


def pipeline(plan_ref, items, operand_ref, weights_ref, buffers, visit):
    tiles, depth, tile = weights_ref.shape
    per = (operand_ref.shape[0] // unit_rows - 1) // group

    def where(i):
        code = plan_ref[tiles + 1, i]
        s = code // per
        first = (code - s * per) * group
        return jnp.minimum(s, tiles - 1), [plan_ref[s, first + k] for k in range(group)]

    def step(j, carry):
        for k in range(span):
            s, units = where(span * j + k)
            rows = jnp.concatenate(
                [
                    operand_ref[pl.ds(pl.multiple_of(u * unit_rows, unit_rows), unit_rows), :]
                    for u in units
                ],
                axis=0,
            )
            buffers[k][...] = jnp.dot(rows, weights_ref[s], preferred_element_type=f32)
        for k in range(span):
            visit(*where(span * j + k), buffers[k])
        return carry

    lax.fori_loop(0, (items + span - 1) // span, step, 0)


def row_pass(
    which, plan_ref, points_ref, need_ref, w0, w1, w2, w3, lse_ref,
    held_ref, sems, operand_ref, weights_ref, total_ref, *buffers,
):
    tiles, depth, tile = weights_ref.shape
    items = plan_ref[tiles + 2, which]

    @pl.when(items == 0)
    def _():
        lse_ref[...] = jnp.full_like(lse_ref, nothing)

    @pl.when(items > 0)
    def _():
        load_all(points_ref, None, (w0, w1, w2, w3), held_ref, sems, operand_ref, weights_ref)
        total_ref[...] = jnp.zeros_like(total_ref)

        def visit(s, units, buffer):
            part = jnp.exp2(buffer[...]).reshape(4, unit_rows * group // 32, 8, tile)
            total_ref[s] += jnp.sum(jnp.sum(part, axis=1), axis=0)

        pipeline(plan_ref, items, operand_ref, weights_ref, buffers, visit)
        total = jnp.sum(total_ref[...], axis=1)
        lse_ref[...] = jnp.where(total > 0.0, jnp.log2(jnp.maximum(total, 1e-37)), nothing)
        fine = (total > 1e-25) & (total < 1e30)
        bad = jnp.where(fine, 0.0, need_ref[...])

        @pl.when(jnp.max(bad) > 0.0)
        def _():
            def one_tile(s, carry):
                weights = weights_ref[s]

                def step(i, state):
                    high, total = state
                    unit = plan_ref[s, i]
                    rows = operand_ref[
                        pl.ds(pl.multiple_of(unit * unit_rows, unit_rows), unit_rows), :
                    ]
                    score = jnp.dot(rows, weights, preferred_element_type=f32)
                    score = score.reshape(unit_rows // 8, 8, tile)
                    new = jnp.maximum(high, jnp.max(score, axis=0))
                    total = total * jnp.exp2(high - new)
                    return new, total + jnp.sum(jnp.exp2(score - new[None]), axis=0)

                start = (jnp.full((8, tile), floor, f32), jnp.zeros((8, tile), f32))
                high, total = lax.fori_loop(0, plan_ref[s, 127], step, start)
                top = jnp.max(high, axis=0, keepdims=True)
                total = jnp.sum(total * jnp.exp2(high - top), axis=0, keepdims=True)
                lse_ref[pl.ds(s, 1), :] = jnp.where(
                    total > 0.0, top + jnp.log2(jnp.maximum(total, 1e-37)), nothing
                )
                return carry

            lax.fori_loop(0, tiles, one_tile, 0)


def column_pass(
    which, plan_ref, points_ref, need_ref, w0, w1, w2, w3, lse_ref, mass_ref, other_ref, out_ref,
    held_ref, sems, operand_ref, weights_ref, total_ref, high_ref, *buffers,
):
    tiles, depth, tile = weights_ref.shape
    items = plan_ref[tiles + 2, which]

    @pl.when(items == 0)
    def _():
        out_ref[...] = other_ref[...]

    @pl.when(items > 0)
    def _():
        shift = mass_ref[...] - lse_ref[...]
        load_all(points_ref, shift, (w0, w1, w2, w3), held_ref, sems, operand_ref, weights_ref)
        total_ref[...] = jnp.zeros_like(total_ref)

        def visit(s, units, buffer):
            for k, u in enumerate(units):
                where = pl.ds(pl.multiple_of(u * unit_rows, unit_rows), unit_rows)
                part = jnp.exp2(buffer[k * unit_rows : (k + 1) * unit_rows, :])
                total_ref[where, :] += part[:, 0:128] + part[:, 128:256]

        pipeline(plan_ref, items, operand_ref, weights_ref, buffers, visit)
        eye = lax.broadcasted_iota(jnp.int32, (128, 128), 0) == lax.broadcasted_iota(
            jnp.int32, (128, 128), 1
        )

        def to_row(column):
            return jnp.sum(jnp.where(eye, column, 0.0), axis=0, keepdims=True)

        bad = jnp.zeros((1, 128), f32)
        for u in range(out_ref.shape[0]):
            sums = to_row(jnp.sum(total_ref[u * 128 : (u + 1) * 128, :], axis=1, keepdims=True))
            out_ref[u : u + 1, :] = jnp.where(
                sums > 0.0, jnp.log2(jnp.maximum(sums, 1e-37)), nothing
            )
            bad = jnp.maximum(bad, jnp.where(sums > 1e-25, 0.0, need_ref[u : u + 1, :]))

        @pl.when(jnp.max(bad) > 0.0)
        def _():
            total_ref[...] = jnp.zeros_like(total_ref)
            high_ref[...] = jnp.full_like(high_ref, floor)

            def one_tile(s, carry):
                def step(i, inner):
                    unit = plan_ref[s, i]
                    where = pl.ds(pl.multiple_of(unit * unit_rows, unit_rows), unit_rows)
                    score = jnp.dot(
                        operand_ref[where, :], weights_ref[s], preferred_element_type=f32
                    )
                    a, b = score[:, 0:128], score[:, 128:256]
                    old = high_ref[where, :]
                    new = jnp.maximum(old, jnp.maximum(a, b))
                    high_ref[where, :] = new
                    total_ref[where, :] = (
                        total_ref[where, :] * jnp.exp2(old - new)
                        + jnp.exp2(a - new)
                        + jnp.exp2(b - new)
                    )
                    return inner

                lax.fori_loop(0, plan_ref[s, 127], step, 0)
                return carry

            lax.fori_loop(0, tiles, one_tile, 0)

            def finish(u, carry):
                where = pl.ds(pl.multiple_of(u * 128, 128), 128)
                high = high_ref[where, :]
                top = jnp.max(high, axis=1, keepdims=True)
                rest = total_ref[where, :] * jnp.exp2(high - top)
                sums = to_row(jnp.sum(rest, axis=1, keepdims=True))
                out_ref[pl.ds(u, 1), :] = jnp.where(
                    sums > 0.0, to_row(top) + jnp.log2(jnp.maximum(sums, 1e-37)), nothing
                )
                return carry

            lax.fori_loop(0, out_ref.shape[0], finish, 0)


def log_sum(parts):
    top = functools.reduce(jnp.maximum, parts)
    total = sum(jnp.exp2(p - top) for p in parts)
    return top + jnp.log2(total)


def roles(parity, cols):
    four = [d % cols for d in ((-2, -1, 0, 1), (-1, 0, 1, 2))[parity]]
    lead = [0, (1, -1)[parity] % cols]
    near = lead + [d for d in four if d not in lead]
    out = [(2, -2)[parity] % cols, cols // 2]
    begin = four[0]
    out += [(begin + 5) % cols, (begin + 6) % cols]
    return near, out + [d for d in range(cols) if d not in near and d not in out]


def shards(src_points, dst_points, dst_potential, partners, partner_count, src_count, dst_count):
    src_tiles = src_count.shape[0]
    dst_tiles = dst_count.shape[0]
    tile = src_points.shape[0] // src_tiles
    slots = partners.shape[1]
    rows = lax.axis_size("row")
    cols = lax.axis_size("col")
    row_here = lax.axis_index("row")
    col_here = lax.axis_index("col")
    share = dst_points.shape[0]
    points = dst_tiles * tile
    smem = pl.BlockSpec(memory_space=pltpu.SMEM)
    vmem = pl.BlockSpec(memory_space=pltpu.VMEM)
    anywhere = pl.BlockSpec(memory_space=pl.ANY)
    params = pltpu.CompilerParams(vmem_limit_bytes=24 * 1024 * 1024)
    places = [roles(r % 2, cols) for r in range(rows)]
    near = [[(r + d) % cols for d in places[r][0]] for r in range(rows)]
    far = [[(r + d) % cols for d in places[r][1]] for r in range(rows)]
    parity = lax.rem(row_here, 2)
    apart = lax.rem(col_here - row_here + 2 - parity + cols, cols)
    in_near = apart < 4
    in_far = (
        (apart == 5)
        | (apart == 6)
        | (apart == jnp.where(parity == 0, 4, cols - 1))
        | (apart == jnp.where(parity == 0, 10, 9))
    )

    def send(a, hops):
        return lax.ppermute(a, ("row", "col"), [(s[0] * cols + s[1], d[0] * cols + d[1]) for s, d in hops])

    every = [(r, c) for r in range(rows) for c in range(cols)]

    wire = pl.pallas_call(
        pack_targets,
        out_shape=jax.ShapeDtypeStruct((share // 2 + 8, 128), f32),
        in_specs=[smem, vmem, vmem],
        out_specs=vmem,
        scratch_shapes=[pltpu.VMEM((128, 384), f32), pltpu.VMEM((8, 384), f32)],
        compiler_params=params,
    )(dst_count, dst_points.T, dst_potential)

    def around(r, dx, dy):
        return (r // ring + dx) % ring * ring + (r + dy) % ring

    def first_hop(r, c, k):
        return around(r, 0, k) if c % 2 == 0 else around(r, k, 0)

    def second_hop(r, c, k):
        return around(r, k, 0) if c % 2 == 0 else around(r, 0, k)

    bundle = jnp.stack(
        [wire]
        + [send(wire, [((r, c), (first_hop(r, c, k), c)) for r, c in every]) for k in (1, 2, 3)]
    )
    busy = [set(near[r] + far[r][:2]) for r in range(rows)]
    slot_on = jnp.arange(slots, dtype=jnp.int32)[None, :] < partner_count[:, None]
    local = jnp.where(slot_on, partners - col_here * dst_tiles, -1)
    plan = pl.pallas_call(
        plan_work,
        out_shape=jax.ShapeDtypeStruct((24, 128), jnp.int32),
        in_specs=[smem, vmem],
        out_specs=vmem,
        compiler_params=params,
    )(dst_count, jnp.pad(local, ((0, 24 - src_tiles), (0, 0)), constant_values=-1))
    plan, local, dst_count, src_count, bundle = lax.optimization_barrier(
        (plan, local, dst_count, src_count, bundle)
    )
    wires = [bundle] + [
        send(
            bundle,
            [
                ((r, c), (second_hop(r, c, k), c))
                for r, c in every
                if c in busy[second_hop(r, c, k)]
            ],
        )
        for k in (1, 2, 3)
    ]
    place = jnp.arange(tile, dtype=jnp.int32)
    src_live = place[None, :] < src_count[:, None]
    dst_live = place[None, :] < dst_count[:, None]
    wanted = jnp.any(local[:, :, None] == jnp.arange(dst_tiles, dtype=jnp.int32), axis=1)
    src_need = jnp.where(src_live & jnp.any(wanted, axis=1)[:, None], 1.0, 0.0)
    dst_need = jnp.where(dst_live & jnp.any(wanted, axis=0)[:, None], 1.0, 0.0)
    dst_need = dst_need.reshape(points // 128, 128)
    counted = src_count.astype(f32)
    all_src = src_tiles * rows
    mass = jnp.where(src_live, -jnp.log2(counted)[:, None] - math.log2(all_src), nothing)

    scratch = [
        pltpu.VMEM((ring, ring) + wire.shape, f32),
        pltpu.SemaphoreType.DMA((ring,)),
        pltpu.VMEM((points + unit_rows, 256), bf16),
        pltpu.VMEM((src_tiles, 256, tile), bf16),
    ]
    buffers = [pltpu.VMEM((unit_rows * group, tile), f32)] * span
    heavy = pl.CostEstimate(flops=8_000_000_000, bytes_accessed=4_000_000, transcendentals=8_000_000)
    light = pl.CostEstimate(flops=100_000_000, bytes_accessed=100_000, transcendentals=100_000)
    turned = src_points.T

    def sum_rows(which, cost):
        return pl.pallas_call(
            functools.partial(row_pass, which),
            out_shape=jax.ShapeDtypeStruct((src_tiles, tile), f32),
            in_specs=[smem] + [vmem] * 2 + [anywhere] * ring,
            out_specs=vmem,
            scratch_shapes=scratch + [pltpu.VMEM((src_tiles, 8, tile), f32)] + buffers,
            compiler_params=params,
            cost_estimate=cost,
        )(plan, turned, src_need, *wires)

    def sum_columns(which, lse, other, cost):
        return pl.pallas_call(
            functools.partial(column_pass, which),
            out_shape=jax.ShapeDtypeStruct((points // 128, 128), f32),
            in_specs=[smem] + [vmem] * 2 + [anywhere] * ring + [vmem] * 3,
            out_specs=vmem,
            scratch_shapes=scratch + [pltpu.VMEM((points + unit_rows, 128), f32)] * 2 + buffers,
            compiler_params=params,
            cost_estimate=cost,
        )(plan, turned, dst_need, *wires, lse, mass, other)

    far_lse = sum_rows(1, light)
    early = send(far_lse, [((r, far[r][k]), (r, near[r][k])) for r in range(rows) for k in (0, 1)])
    near_lse = sum_rows(0, heavy)
    got_early = (col_here == row_here) | (col_here == row_here + 1 - 2 * parity)
    lse = log_sum([near_lse, jnp.where(got_early, early, nothing)])

    def pairs(test):
        return [((r, c), (r, d)) for r in range(rows) for c in near[r] for d in near[r] if test(c, d)]

    lse = log_sum(
        [
            lse,
            send(lse, [((r, c), (r, c ^ 1)) for r, c in every]),
            send(lse, pairs(lambda c, d: (c - d) % cols in (2, cols - 2))),
            send(lse, pairs(lambda c, d: (c - (d ^ 1)) % cols in (2, cols - 2))),
        ]
    )
    spread = send(lse, [((r, near[r][k]), (r, far[r][k])) for r in range(rows) for k in range(4)])
    blank = jnp.full((points // 128, 128), nothing, f32)
    near_part = sum_columns(0, lse, blank, heavy)
    col_part = sum_columns(1, spread, near_part, light)
    known = jnp.where(in_far, spread, lse)
    known, near_part = lax.optimization_barrier((known, near_part))
    rest = send(
        known,
        [((r, (near[r] + far[r])[k]), (r, far[r][4 + k])) for r in range(rows) for k in range(8)],
    )
    shared_out = lax.all_to_all(col_part.reshape(rows, share), "row", 0, 0)

    row_lse = jnp.where(in_near | in_far, known, rest)
    src_potential = jnp.where(
        src_live,
        entropy * (-jnp.log(counted)[:, None] - math.log(all_src) - ln2 * row_lse),
        0.0,
    ).reshape(-1)

    spot = row_here * share + jnp.arange(share, dtype=jnp.int32)
    spot_tile = spot // tile
    spot_count = jnp.sum(
        jnp.where(
            spot_tile[:, None] == jnp.arange(dst_tiles, dtype=jnp.int32)[None, :],
            dst_count[None, :],
            0,
        ),
        axis=1,
    )
    top = jnp.max(shared_out, axis=0)
    col_log = top + jnp.log2(jnp.sum(jnp.exp2(shared_out - top[None]), axis=0))
    dst_new = jnp.where(
        (spot - spot_tile * tile < spot_count) & (top > 0.5 * nothing),
        entropy
        * (-jnp.log(spot_count.astype(f32)) - math.log(dst_tiles * cols) - ln2 * col_log)
        + dst_potential,
        0.0,
    )
    return src_potential, dst_new


def solution(mesh):
    in_specs = (
        P("row", None),
        P(("col", "row"), None),
        P(("col", "row")),
        P("row", None),
        P("row"),
        P("row"),
        P("col"),
    )
    out_specs = (P("row"), P(("col", "row")))
    return jax.shard_map(shards, mesh=mesh, in_specs=in_specs, out_specs=out_specs, check_vma=False)
```

```python
import functools
import math

import jax
import jax.numpy as jnp
from jax import lax
from jax.experimental import pallas as pl
from jax.experimental.pallas import tpu as pltpu
from jax.sharding import PartitionSpec as P

entropy = 0.1
scale = math.log2(math.e) / entropy
ln2 = math.log(2.0)
nothing = -1e30
floor = -1e25
unit_rows = 64
group = 12
span = 8
ring = 4
f32 = jnp.float32
bf16 = jnp.bfloat16


def pieces(a):
    first = a.astype(bf16).astype(f32)
    rest = a - first
    second = rest.astype(bf16).astype(f32)
    return first, second, rest - second


def extra_rows(bias):
    place = lax.broadcasted_iota(jnp.int32, (64, bias.shape[1]), 0)
    block = jnp.where(place < 3, 1.0, 0.0)
    for k, piece in enumerate(pieces(bias)):
        block = jnp.where(place == 3 + k, piece, block)
    return block.astype(bf16)


def pack_targets(count_ref, points_ref, potential_ref, wire_ref, square_ref, line_ref):
    share = points_ref.shape[1]
    tile = 256
    mid = share // 2
    begin = lax.axis_index("row") * share
    first_tile = begin // tile
    offset = begin - first_tile * tile
    last_tile = jnp.minimum(first_tile + 1, count_ref.shape[0] - 1)
    points = points_ref[...]
    square_ref[...] = jnp.zeros_like(square_ref)
    square_ref[0:64, 0:share] = points
    turned = square_ref[...].T
    wire_ref[0:mid, :] = scale * (turned[0:mid] + pltpu.roll(turned[mid:share], 64, 1))
    level = scale * (potential_ref[...].reshape(1, share) - 0.5 * jnp.sum(points * points, axis=0, keepdims=True))
    spot = offset + lax.broadcasted_iota(jnp.int32, (1, share), 1)
    place = jnp.where(spot < tile, spot, spot - tile)
    bound = jnp.where(spot < tile, count_ref[first_tile], count_ref[last_tile])
    line_ref[...] = jnp.full_like(line_ref, nothing)
    line_ref[0:1, 0:share] = jnp.where(place < bound, level, nothing)
    wire_ref[mid : mid + 8, :] = jnp.zeros((8, 128), f32)
    for k in range(3):
        wire_ref[mid + k : mid + k + 1, :] = line_ref[0:1, 128 * k : 128 * (k + 1)]


def unpack_targets(held_ref, arrived, operand_ref):
    lane = lax.broadcasted_iota(jnp.int32, (144, 128), 1)
    front = lane < 64
    sublane = lax.broadcasted_iota(jnp.int32, (16, 384), 0)
    pick_row = lax.broadcasted_iota(jnp.int32, (16, 128), 0)
    pick_lane = lax.broadcasted_iota(jnp.int32, (16, 128), 1)
    pick = jnp.where((pick_lane == pick_row + 64) & (pick_row < 6), 1.0, 0.0).astype(bf16)
    row_here = lax.axis_index("row")
    x_here = row_here // ring
    y_here = row_here - x_here * ring
    even = lax.rem(lax.axis_index("col"), 2) == 0
    for k in range(ring):
        arrived(k)
        for j in range(ring):
            x = lax.rem(x_here + ring - jnp.where(even, k, j), ring)
            y = lax.rem(y_here + ring - jnp.where(even, j, k), ring)
            a = pl.multiple_of((x * ring + y) * 288, 16)
            b = pl.multiple_of((x * ring + y) * 288 + 144, 16)
            both = held_ref[k, j, 0:144, :]
            high = both.astype(bf16).astype(f32)
            low = both - high
            high_back = pltpu.roll(high, 64, 1)
            low_back = pltpu.roll(low, 64, 1)
            tail = held_ref[k, j, 144:152, :]
            line = jnp.concatenate([tail[0:1], tail[1:2], tail[2:3]], axis=1)
            stacked = jnp.where(sublane < 6, 1.0, 0.0)
            for i, piece in enumerate(pieces(line)):
                stacked = jnp.where(sublane == i, piece, stacked)
            extra = lax.dot_general(
                stacked.astype(bf16), pick, (((0,), (0,)), ((), ())), preferred_element_type=f32
            )
            operand_ref[pl.ds(a, 144), 0:128] = jnp.where(front, high, low_back).astype(bf16)
            operand_ref[pl.ds(a, 144), 128:256] = jnp.where(front, high, extra[0:144]).astype(bf16)
            operand_ref[pl.ds(b, 144), 0:128] = jnp.where(front, high_back, low).astype(bf16)
            operand_ref[pl.ds(b, 144), 128:256] = jnp.where(
                front, high_back, extra[144:288]
            ).astype(bf16)
    rows = ring * ring * 288
    dummy_lane = lax.broadcasted_iota(jnp.int32, (unit_rows, 256), 1)
    operand_ref[rows : rows + unit_rows, :] = jnp.where(dummy_lane == 192, nothing, 0.0).astype(bf16)


def load_weights(points_ref, weights_ref, shift):
    tiles, depth, tile = weights_ref.shape
    for s in range(tiles):
        x = points_ref[:, s * tile : (s + 1) * tile]
        high = x.astype(bf16)
        low = (x - high.astype(f32)).astype(bf16)
        bias = (-0.5 * scale) * jnp.sum(x * x, axis=0, keepdims=True)
        weights_ref[s, 0:64, :] = high
        weights_ref[s, 64:128, :] = high
        weights_ref[s, 128:192, :] = low
        weights_ref[s, 192:256, :] = extra_rows(bias if shift is None else bias + shift[s : s + 1, :])


def load_all(points_ref, shift, wires, held_ref, sems, operand_ref, weights_ref):
    copies = [
        pltpu.make_async_copy(wire, held_ref.at[k], sems.at[k]) for k, wire in enumerate(wires)
    ]
    for copy in copies:
        copy.start()
    load_weights(points_ref, weights_ref, shift)
    unpack_targets(held_ref, lambda k: copies[k].wait(), operand_ref)


def plan_work(count_ref, local_ref, plan_ref):
    src_tiles = local_ref.shape[0] - 6
    per_tile = 256 // unit_rows
    units = count_ref.shape[0] * per_tile
    per = units // group
    unit = lax.broadcasted_iota(jnp.int32, (24, 128), 1)
    tile_of = unit // per_tile
    bound = jnp.zeros((24, 128), jnp.int32)
    for t in range(count_ref.shape[0]):
        bound = jnp.where(tile_of == t, count_ref[t], bound)
    live = bound > (unit - tile_of * per_tile) * unit_rows
    hits = jnp.zeros((24, 128), f32)
    for k in range(local_ref.shape[1]):
        hits = jnp.where(local_ref[:, k : k + 1] == tile_of, 1.0, hits)
    active = jnp.where(live, hits, 0.0)
    down = lax.broadcasted_iota(jnp.int32, (128, 128), 0)
    across = lax.broadcasted_iota(jnp.int32, (128, 128), 1)
    upto = jnp.where(down <= across, 1.0, 0.0).astype(bf16)
    rank = jnp.dot(active.astype(bf16), upto, preferred_element_type=f32)
    counts = jnp.broadcast_to(rank[:, 127:128], (24, 128))
    place = jnp.where(active > 0.0, rank - 1.0, -1.0)
    place = jnp.concatenate([place, jnp.full((104, 128), -1.0, f32)], axis=0).T
    position = across.astype(f32)
    value = (down - units).astype(f32)
    plan_ref[...] = jnp.full_like(plan_ref, units)
    last = lax.broadcasted_iota(jnp.int32, (1, 128), 1)
    chunks = jnp.floor((counts + (group - 0.5)) / group).astype(jnp.int32)
    begin = jnp.zeros((1, 128), jnp.int32)
    items = jnp.full((1, 128), src_tiles * per, jnp.int32)
    for s in range(src_tiles):
        listed = jnp.sum(
            jnp.where(place[:, s : s + 1] == position, value, 0.0), axis=0, keepdims=True
        )
        plan_ref[s : s + 1, :] = jnp.where(
            last == 127, counts[s : s + 1], listed + units
        ).astype(jnp.int32)
        along = last - begin
        inside = (along >= 0) & (along < chunks[s : s + 1])
        items = jnp.where(inside, s * per + along, items)
        begin = begin + chunks[s : s + 1]
    plan_ref[src_tiles + 1 : src_tiles + 2, :] = items
    row = lax.axis_index("row")
    apart = lax.axis_index("col") - row + 2 - lax.rem(row, 2) + 16
    near = jnp.where(lax.rem(apart, 16) < 4, 1, 0)
    plan_ref[src_tiles + 2 : src_tiles + 3, :] = begin * jnp.where(last == 0, near, 1 - near)


def pipeline(plan_ref, items, operand_ref, weights_ref, buffers, visit):
    tiles, depth, tile = weights_ref.shape
    per = (operand_ref.shape[0] // unit_rows - 1) // group

    def where(i):
        code = plan_ref[tiles + 1, i]
        s = code // per
        first = (code - s * per) * group
        return jnp.minimum(s, tiles - 1), [plan_ref[s, first + k] for k in range(group)]

    def step(j, carry):
        for k in range(span):
            s, units = where(span * j + k)
            rows = jnp.concatenate(
                [
                    operand_ref[pl.ds(pl.multiple_of(u * unit_rows, unit_rows), unit_rows), :]
                    for u in units
                ],
                axis=0,
            )
            buffers[k][...] = jnp.dot(rows, weights_ref[s], preferred_element_type=f32)
        for k in range(span):
            visit(*where(span * j + k), buffers[k])
        return carry

    lax.fori_loop(0, (items + span - 1) // span, step, 0)


def row_pass(
    which, plan_ref, points_ref, need_ref, w0, w1, w2, w3, lse_ref,
    held_ref, sems, operand_ref, weights_ref, total_ref, *buffers,
):
    tiles, depth, tile = weights_ref.shape
    items = plan_ref[tiles + 2, which]

    @pl.when(items == 0)
    def _():
        lse_ref[...] = jnp.full_like(lse_ref, nothing)

    @pl.when(items > 0)
    def _():
        load_all(points_ref, None, (w0, w1, w2, w3), held_ref, sems, operand_ref, weights_ref)
        total_ref[...] = jnp.zeros_like(total_ref)

        def visit(s, units, buffer):
            part = jnp.exp2(buffer[...]).reshape(4, unit_rows * group // 32, 8, tile)
            total_ref[s] += jnp.sum(jnp.sum(part, axis=1), axis=0)

        pipeline(plan_ref, items, operand_ref, weights_ref, buffers, visit)
        total = jnp.sum(total_ref[...], axis=1)
        lse_ref[...] = jnp.where(total > 0.0, jnp.log2(jnp.maximum(total, 1e-37)), nothing)
        fine = (total > 1e-25) & (total < 1e30)
        bad = jnp.where(fine, 0.0, need_ref[...])

        @pl.when(jnp.max(bad) > 0.0)
        def _():
            def one_tile(s, carry):
                weights = weights_ref[s]

                def step(i, state):
                    high, total = state
                    unit = plan_ref[s, i]
                    rows = operand_ref[
                        pl.ds(pl.multiple_of(unit * unit_rows, unit_rows), unit_rows), :
                    ]
                    score = jnp.dot(rows, weights, preferred_element_type=f32)
                    score = score.reshape(unit_rows // 8, 8, tile)
                    new = jnp.maximum(high, jnp.max(score, axis=0))
                    total = total * jnp.exp2(high - new)
                    return new, total + jnp.sum(jnp.exp2(score - new[None]), axis=0)

                start = (jnp.full((8, tile), floor, f32), jnp.zeros((8, tile), f32))
                high, total = lax.fori_loop(0, plan_ref[s, 127], step, start)
                top = jnp.max(high, axis=0, keepdims=True)
                total = jnp.sum(total * jnp.exp2(high - top), axis=0, keepdims=True)
                lse_ref[pl.ds(s, 1), :] = jnp.where(
                    total > 0.0, top + jnp.log2(jnp.maximum(total, 1e-37)), nothing
                )
                return carry

            lax.fori_loop(0, tiles, one_tile, 0)


def column_pass(
    which, plan_ref, points_ref, need_ref, w0, w1, w2, w3, lse_ref, mass_ref, other_ref, out_ref,
    held_ref, sems, operand_ref, weights_ref, total_ref, high_ref, *buffers,
):
    tiles, depth, tile = weights_ref.shape
    items = plan_ref[tiles + 2, which]

    @pl.when(items == 0)
    def _():
        out_ref[...] = other_ref[...]

    @pl.when(items > 0)
    def _():
        shift = mass_ref[...] - lse_ref[...]
        load_all(points_ref, shift, (w0, w1, w2, w3), held_ref, sems, operand_ref, weights_ref)
        total_ref[...] = jnp.zeros_like(total_ref)

        def visit(s, units, buffer):
            for k, u in enumerate(units):
                where = pl.ds(pl.multiple_of(u * unit_rows, unit_rows), unit_rows)
                part = jnp.exp2(buffer[k * unit_rows : (k + 1) * unit_rows, :])
                total_ref[where, :] += part[:, 0:128] + part[:, 128:256]

        pipeline(plan_ref, items, operand_ref, weights_ref, buffers, visit)
        eye = lax.broadcasted_iota(jnp.int32, (128, 128), 0) == lax.broadcasted_iota(
            jnp.int32, (128, 128), 1
        )

        def to_row(column):
            return jnp.sum(jnp.where(eye, column, 0.0), axis=0, keepdims=True)

        bad = jnp.zeros((1, 128), f32)
        for u in range(out_ref.shape[0]):
            sums = to_row(jnp.sum(total_ref[u * 128 : (u + 1) * 128, :], axis=1, keepdims=True))
            out_ref[u : u + 1, :] = jnp.where(
                sums > 0.0, jnp.log2(jnp.maximum(sums, 1e-37)), nothing
            )
            bad = jnp.maximum(bad, jnp.where(sums > 1e-25, 0.0, need_ref[u : u + 1, :]))

        @pl.when(jnp.max(bad) > 0.0)
        def _():
            total_ref[...] = jnp.zeros_like(total_ref)
            high_ref[...] = jnp.full_like(high_ref, floor)

            def one_tile(s, carry):
                def step(i, inner):
                    unit = plan_ref[s, i]
                    where = pl.ds(pl.multiple_of(unit * unit_rows, unit_rows), unit_rows)
                    score = jnp.dot(
                        operand_ref[where, :], weights_ref[s], preferred_element_type=f32
                    )
                    a, b = score[:, 0:128], score[:, 128:256]
                    old = high_ref[where, :]
                    new = jnp.maximum(old, jnp.maximum(a, b))
                    high_ref[where, :] = new
                    total_ref[where, :] = (
                        total_ref[where, :] * jnp.exp2(old - new)
                        + jnp.exp2(a - new)
                        + jnp.exp2(b - new)
                    )
                    return inner

                lax.fori_loop(0, plan_ref[s, 127], step, 0)
                return carry

            lax.fori_loop(0, tiles, one_tile, 0)

            def finish(u, carry):
                where = pl.ds(pl.multiple_of(u * 128, 128), 128)
                high = high_ref[where, :]
                top = jnp.max(high, axis=1, keepdims=True)
                rest = total_ref[where, :] * jnp.exp2(high - top)
                sums = to_row(jnp.sum(rest, axis=1, keepdims=True))
                out_ref[pl.ds(u, 1), :] = jnp.where(
                    sums > 0.0, to_row(top) + jnp.log2(jnp.maximum(sums, 1e-37)), nothing
                )
                return carry

            lax.fori_loop(0, out_ref.shape[0], finish, 0)


def log_sum(parts):
    top = functools.reduce(jnp.maximum, parts)
    total = sum(jnp.exp2(p - top) for p in parts)
    return top + jnp.log2(total)


def roles(parity, cols):
    four = [d % cols for d in ((-2, -1, 0, 1), (-1, 0, 1, 2))[parity]]
    lead = [0, (1, -1)[parity] % cols]
    near = lead + [d for d in four if d not in lead]
    out = [(2, -2)[parity] % cols, cols // 2]
    begin = four[0]
    out += [(begin + 5) % cols, (begin + 6) % cols]
    return near, out + [d for d in range(cols) if d not in near and d not in out]


def filled(hops, count, cols):
    found = dict(hops)
    back = {d: s for s, d in hops}
    for rank in range(4):
        free = [d for d in range(count) if d not in back]
        for s in [s for s in range(count) if s not in found]:
            if rank == 0:
                picks = [back[s]] if s in back and back[s] in free else []
            elif rank == 1:
                picks = [s ^ 1] if s ^ 1 in free else []
            else:
                picks = [d for d in free if d != s and (d // cols == s // cols or rank == 3)]
                picks.sort(key=lambda d: min((d - s) % cols, (s - d) % cols))
            if picks:
                found[s] = picks[0]
                back[picks[0]] = s
                free.remove(picks[0])
    return sorted(found.items())


def shards(src_points, dst_points, dst_potential, partners, partner_count, src_count, dst_count):
    src_tiles = src_count.shape[0]
    dst_tiles = dst_count.shape[0]
    tile = src_points.shape[0] // src_tiles
    slots = partners.shape[1]
    rows = lax.axis_size("row")
    cols = lax.axis_size("col")
    row_here = lax.axis_index("row")
    col_here = lax.axis_index("col")
    share = dst_points.shape[0]
    points = dst_tiles * tile
    smem = pl.BlockSpec(memory_space=pltpu.SMEM)
    vmem = pl.BlockSpec(memory_space=pltpu.VMEM)
    anywhere = pl.BlockSpec(memory_space=pl.ANY)
    params = pltpu.CompilerParams(vmem_limit_bytes=24 * 1024 * 1024)
    places = [roles(r % 2, cols) for r in range(rows)]
    near = [[(r + d) % cols for d in places[r][0]] for r in range(rows)]
    far = [[(r + d) % cols for d in places[r][1]] for r in range(rows)]
    parity = lax.rem(row_here, 2)
    apart = lax.rem(col_here - row_here + 2 - parity + cols, cols)
    in_near = apart < 4
    in_far = (
        (apart == 5)
        | (apart == 6)
        | (apart == jnp.where(parity == 0, 4, cols - 1))
        | (apart == jnp.where(parity == 0, 10, 9))
    )

    def send(a, hops, full=True):
        hops = [(s[0] * cols + s[1], d[0] * cols + d[1]) for s, d in hops]
        return lax.ppermute(a, ("row", "col"), filled(hops, rows * cols, cols) if full else hops)

    every = [(r, c) for r in range(rows) for c in range(cols)]

    wire = pl.pallas_call(
        pack_targets,
        out_shape=jax.ShapeDtypeStruct((share // 2 + 8, 128), f32),
        in_specs=[smem, vmem, vmem],
        out_specs=vmem,
        scratch_shapes=[pltpu.VMEM((128, 384), f32), pltpu.VMEM((8, 384), f32)],
        compiler_params=params,
    )(dst_count, dst_points.T, dst_potential)

    def around(r, dx, dy):
        return (r // ring + dx) % ring * ring + (r + dy) % ring

    def first_hop(r, c, k):
        return around(r, 0, k) if c % 2 == 0 else around(r, k, 0)

    def second_hop(r, c, k):
        return around(r, k, 0) if c % 2 == 0 else around(r, 0, k)

    bundle = jnp.stack(
        [wire]
        + [send(wire, [((r, c), (first_hop(r, c, k), c)) for r, c in every]) for k in (1, 2, 3)]
    )
    busy = [set(near[r] + far[r][:2]) for r in range(rows)]
    slot_on = jnp.arange(slots, dtype=jnp.int32)[None, :] < partner_count[:, None]
    local = jnp.where(slot_on, partners - col_here * dst_tiles, -1)
    plan = pl.pallas_call(
        plan_work,
        out_shape=jax.ShapeDtypeStruct((24, 128), jnp.int32),
        in_specs=[smem, vmem],
        out_specs=vmem,
        compiler_params=params,
    )(dst_count, jnp.pad(local, ((0, 24 - src_tiles), (0, 0)), constant_values=-1))
    plan, local, dst_count, src_count, bundle = lax.optimization_barrier(
        (plan, local, dst_count, src_count, bundle)
    )
    wires = [bundle] + [
        send(
            bundle,
            [
                ((r, c), (second_hop(r, c, k), c))
                for r, c in every
                if c in busy[second_hop(r, c, k)]
            ],
            full=False,
        )
        for k in (1, 2, 3)
    ]
    place = jnp.arange(tile, dtype=jnp.int32)
    src_live = place[None, :] < src_count[:, None]
    dst_live = place[None, :] < dst_count[:, None]
    wanted = jnp.any(local[:, :, None] == jnp.arange(dst_tiles, dtype=jnp.int32), axis=1)
    src_need = jnp.where(src_live & jnp.any(wanted, axis=1)[:, None], 1.0, 0.0)
    dst_need = jnp.where(dst_live & jnp.any(wanted, axis=0)[:, None], 1.0, 0.0)
    dst_need = dst_need.reshape(points // 128, 128)
    counted = src_count.astype(f32)
    all_src = src_tiles * rows
    mass = jnp.where(src_live, -jnp.log2(counted)[:, None] - math.log2(all_src), nothing)

    scratch = [
        pltpu.VMEM((ring, ring) + wire.shape, f32),
        pltpu.SemaphoreType.DMA((ring,)),
        pltpu.VMEM((points + unit_rows, 256), bf16),
        pltpu.VMEM((src_tiles, 256, tile), bf16),
    ]
    buffers = [pltpu.VMEM((unit_rows * group, tile), f32)] * span
    heavy = pl.CostEstimate(flops=8_000_000_000, bytes_accessed=4_000_000, transcendentals=8_000_000)
    light = pl.CostEstimate(flops=100_000_000, bytes_accessed=100_000, transcendentals=100_000)
    turned = src_points.T

    def sum_rows(which, cost):
        return pl.pallas_call(
            functools.partial(row_pass, which),
            out_shape=jax.ShapeDtypeStruct((src_tiles, tile), f32),
            in_specs=[smem] + [vmem] * 2 + [anywhere] * ring,
            out_specs=vmem,
            scratch_shapes=scratch + [pltpu.VMEM((src_tiles, 8, tile), f32)] + buffers,
            compiler_params=params,
            cost_estimate=cost,
        )(plan, turned, src_need, *wires)

    def sum_columns(which, lse, other, cost):
        return pl.pallas_call(
            functools.partial(column_pass, which),
            out_shape=jax.ShapeDtypeStruct((points // 128, 128), f32),
            in_specs=[smem] + [vmem] * 2 + [anywhere] * ring + [vmem] * 3,
            out_specs=vmem,
            scratch_shapes=scratch + [pltpu.VMEM((points + unit_rows, 128), f32)] * 2 + buffers,
            compiler_params=params,
            cost_estimate=cost,
        )(plan, turned, dst_need, *wires, lse, mass, other)

    far_lse = sum_rows(1, light)
    early = send(far_lse, [((r, far[r][k]), (r, near[r][k])) for r in range(rows) for k in (0, 1)])
    near_lse = sum_rows(0, heavy)
    got_early = (col_here == row_here) | (col_here == row_here + 1 - 2 * parity)
    lse = log_sum([near_lse, jnp.where(got_early, early, nothing)])

    def pairs(test):
        return [((r, c), (r, d)) for r in range(rows) for c in near[r] for d in near[r] if test(c, d)]

    lse = log_sum(
        [
            lse,
            send(lse, [((r, c), (r, c ^ 1)) for r, c in every]),
            send(lse, pairs(lambda c, d: (c - d) % cols in (2, cols - 2))),
            send(lse, pairs(lambda c, d: (c - (d ^ 1)) % cols in (2, cols - 2))),
        ]
    )
    spread = send(lse, [((r, near[r][k]), (r, far[r][k])) for r in range(rows) for k in range(4)])
    blank = jnp.full((points // 128, 128), nothing, f32)
    near_part = sum_columns(0, lse, blank, heavy)
    col_part = sum_columns(1, spread, near_part, light)
    known = jnp.where(in_far, spread, lse)
    known, near_part = lax.optimization_barrier((known, near_part))
    rest = send(
        known,
        [((r, (near[r] + far[r])[k]), (r, far[r][4 + k])) for r in range(rows) for k in range(8)],
    )
    shared_out = lax.all_to_all(col_part.reshape(rows, share), "row", 0, 0)

    row_lse = jnp.where(in_near | in_far, known, rest)
    src_potential = jnp.where(
        src_live,
        entropy * (-jnp.log(counted)[:, None] - math.log(all_src) - ln2 * row_lse),
        0.0,
    ).reshape(-1)

    spot = row_here * share + jnp.arange(share, dtype=jnp.int32)
    spot_tile = spot // tile
    spot_count = jnp.sum(
        jnp.where(
            spot_tile[:, None] == jnp.arange(dst_tiles, dtype=jnp.int32)[None, :],
            dst_count[None, :],
            0,
        ),
        axis=1,
    )
    top = jnp.max(shared_out, axis=0)
    col_log = top + jnp.log2(jnp.sum(jnp.exp2(shared_out - top[None]), axis=0))
    dst_new = jnp.where(
        (spot - spot_tile * tile < spot_count) & (top > 0.5 * nothing),
        entropy
        * (-jnp.log(spot_count.astype(f32)) - math.log(dst_tiles * cols) - ln2 * col_log)
        + dst_potential,
        0.0,
    )
    return src_potential, dst_new


def solution(mesh):
    in_specs = (
        P("row", None),
        P(("col", "row"), None),
        P(("col", "row")),
        P("row", None),
        P("row"),
        P("row"),
        P("col"),
    )
    out_specs = (P("row"), P(("col", "row")))
    return jax.shard_map(shards, mesh=mesh, in_specs=in_specs, out_specs=out_specs, check_vma=False)
```

```python
import functools
import math

import jax
import jax.numpy as jnp
from jax import lax
from jax.experimental import pallas as pl
from jax.experimental.pallas import tpu as pltpu
from jax.sharding import PartitionSpec as P

entropy = 0.1
scale = math.log2(math.e) / entropy
ln2 = math.log(2.0)
nothing = -1e30
floor = -1e25
unit_rows = 64
group = 12
span = 8
ring = 4
f32 = jnp.float32
bf16 = jnp.bfloat16


def pieces(a):
    first = a.astype(bf16).astype(f32)
    rest = a - first
    second = rest.astype(bf16).astype(f32)
    return first, second, rest - second


def extra_rows(bias):
    place = lax.broadcasted_iota(jnp.int32, (64, bias.shape[1]), 0)
    block = jnp.where(place < 3, 1.0, 0.0)
    for k, piece in enumerate(pieces(bias)):
        block = jnp.where(place == 3 + k, piece, block)
    return block.astype(bf16)


def pack_targets(
    count_ref, points_ref, potential_ref, wire_ref, square_ref, line_ref, tally_ref, held_ref, level_ref, sems,
):
    copies = [
        pltpu.make_async_copy(source, target, sems.at[k])
        for k, (source, target) in enumerate(
            ((points_ref, held_ref), (potential_ref, level_ref), (count_ref, tally_ref))
        )
    ]
    for copy in copies:
        copy.start()
    share = held_ref.shape[1]
    tile = 256
    mid = share // 2
    begin = lax.axis_index("row") * share
    first_tile = begin // tile
    offset = begin - first_tile * tile
    last_tile = jnp.minimum(first_tile + 1, tally_ref.shape[0] - 1)
    square_ref[...] = jnp.zeros_like(square_ref)
    line_ref[...] = jnp.full_like(line_ref, nothing)
    wire_ref[mid : mid + 8, :] = jnp.zeros((8, 128), f32)
    for copy in copies:
        copy.wait()
    points = held_ref[...]
    square_ref[0:64, 0:share] = points
    turned = square_ref[...].T
    wire_ref[0:mid, :] = scale * (turned[0:mid] + pltpu.roll(turned[mid:share], 64, 1))
    level = level_ref[...].reshape(1, share)
    level = scale * (level - 0.5 * jnp.sum(points * points, axis=0, keepdims=True))
    spot = offset + lax.broadcasted_iota(jnp.int32, (1, share), 1)
    place = jnp.where(spot < tile, spot, spot - tile)
    bound = jnp.where(spot < tile, tally_ref[first_tile], tally_ref[last_tile])
    line_ref[0:1, 0:share] = jnp.where(place < bound, level, nothing)
    for k in range(3):
        wire_ref[mid + k : mid + k + 1, :] = line_ref[0:1, 128 * k : 128 * (k + 1)]


def unpack_targets(held_ref, arrived, operand_ref):
    lane = lax.broadcasted_iota(jnp.int32, (144, 128), 1)
    front = lane < 64
    sublane = lax.broadcasted_iota(jnp.int32, (16, 384), 0)
    pick_row = lax.broadcasted_iota(jnp.int32, (16, 128), 0)
    pick_lane = lax.broadcasted_iota(jnp.int32, (16, 128), 1)
    pick = jnp.where((pick_lane == pick_row + 64) & (pick_row < 6), 1.0, 0.0).astype(bf16)
    row_here = lax.axis_index("row")
    x_here = row_here // ring
    y_here = row_here - x_here * ring
    even = lax.rem(lax.axis_index("col"), 2) == 0
    for k in range(ring):
        arrived(k)
        for j in range(ring):
            x = lax.rem(x_here + ring - jnp.where(even, k, j), ring)
            y = lax.rem(y_here + ring - jnp.where(even, j, k), ring)
            a = pl.multiple_of((x * ring + y) * 288, 16)
            b = pl.multiple_of((x * ring + y) * 288 + 144, 16)
            both = held_ref[k, j, 0:144, :]
            high = both.astype(bf16).astype(f32)
            low = both - high
            high_back = pltpu.roll(high, 64, 1)
            low_back = pltpu.roll(low, 64, 1)
            tail = held_ref[k, j, 144:152, :]
            line = jnp.concatenate([tail[0:1], tail[1:2], tail[2:3]], axis=1)
            stacked = jnp.where(sublane < 6, 1.0, 0.0)
            for i, piece in enumerate(pieces(line)):
                stacked = jnp.where(sublane == i, piece, stacked)
            extra = lax.dot_general(
                stacked.astype(bf16), pick, (((0,), (0,)), ((), ())), preferred_element_type=f32
            )
            operand_ref[pl.ds(a, 144), 0:128] = jnp.where(front, high, low_back).astype(bf16)
            operand_ref[pl.ds(a, 144), 128:256] = jnp.where(front, high, extra[0:144]).astype(bf16)
            operand_ref[pl.ds(b, 144), 0:128] = jnp.where(front, high_back, low).astype(bf16)
            operand_ref[pl.ds(b, 144), 128:256] = jnp.where(
                front, high_back, extra[144:288]
            ).astype(bf16)
    rows = ring * ring * 288
    dummy_lane = lax.broadcasted_iota(jnp.int32, (unit_rows, 256), 1)
    operand_ref[rows : rows + unit_rows, :] = jnp.where(dummy_lane == 192, nothing, 0.0).astype(bf16)


def load_weights(points_ref, weights_ref, shift):
    tiles, depth, tile = weights_ref.shape
    for s in range(tiles):
        x = points_ref[:, s * tile : (s + 1) * tile]
        high = x.astype(bf16)
        low = (x - high.astype(f32)).astype(bf16)
        bias = (-0.5 * scale) * jnp.sum(x * x, axis=0, keepdims=True)
        weights_ref[s, 0:64, :] = high
        weights_ref[s, 64:128, :] = high
        weights_ref[s, 128:192, :] = low
        weights_ref[s, 192:256, :] = extra_rows(bias if shift is None else bias + shift[s : s + 1, :])


def load_all(points_ref, shift, wires, held_ref, sems, operand_ref, weights_ref):
    copies = [
        pltpu.make_async_copy(wire, held_ref.at[k], sems.at[k]) for k, wire in enumerate(wires)
    ]
    for copy in copies:
        copy.start()
    load_weights(points_ref, weights_ref, shift)
    unpack_targets(held_ref, lambda k: copies[k].wait(), operand_ref)


def plan_work(count_ref, local_ref, plan_ref):
    src_tiles = local_ref.shape[0] - 6
    per_tile = 256 // unit_rows
    units = count_ref.shape[0] * per_tile
    per = units // group
    unit = lax.broadcasted_iota(jnp.int32, (24, 128), 1)
    tile_of = unit // per_tile
    bound = jnp.zeros((24, 128), jnp.int32)
    for t in range(count_ref.shape[0]):
        bound = jnp.where(tile_of == t, count_ref[t], bound)
    live = bound > (unit - tile_of * per_tile) * unit_rows
    hits = jnp.zeros((24, 128), f32)
    for k in range(local_ref.shape[1]):
        hits = jnp.where(local_ref[:, k : k + 1] == tile_of, 1.0, hits)
    active = jnp.where(live, hits, 0.0)
    down = lax.broadcasted_iota(jnp.int32, (128, 128), 0)
    across = lax.broadcasted_iota(jnp.int32, (128, 128), 1)
    upto = jnp.where(down <= across, 1.0, 0.0).astype(bf16)
    rank = jnp.dot(active.astype(bf16), upto, preferred_element_type=f32)
    counts = jnp.broadcast_to(rank[:, 127:128], (24, 128))
    place = jnp.where(active > 0.0, rank - 1.0, -1.0)
    place = jnp.concatenate([place, jnp.full((104, 128), -1.0, f32)], axis=0).T
    position = across.astype(f32)
    value = (down - units).astype(f32)
    plan_ref[...] = jnp.full_like(plan_ref, units)
    last = lax.broadcasted_iota(jnp.int32, (1, 128), 1)
    chunks = jnp.floor((counts + (group - 0.5)) / group).astype(jnp.int32)
    begin = jnp.zeros((1, 128), jnp.int32)
    items = jnp.full((1, 128), src_tiles * per, jnp.int32)
    for s in range(src_tiles):
        listed = jnp.sum(
            jnp.where(place[:, s : s + 1] == position, value, 0.0), axis=0, keepdims=True
        )
        plan_ref[s : s + 1, :] = jnp.where(
            last == 127, counts[s : s + 1], listed + units
        ).astype(jnp.int32)
        along = last - begin
        inside = (along >= 0) & (along < chunks[s : s + 1])
        items = jnp.where(inside, s * per + along, items)
        begin = begin + chunks[s : s + 1]
    plan_ref[src_tiles + 1 : src_tiles + 2, :] = items
    row = lax.axis_index("row")
    apart = lax.axis_index("col") - row + 2 - lax.rem(row, 2) + 16
    near = jnp.where(lax.rem(apart, 16) < 4, 1, 0)
    plan_ref[src_tiles + 2 : src_tiles + 3, :] = begin * jnp.where(last == 0, near, 1 - near)


def pipeline(plan_ref, items, operand_ref, weights_ref, buffers, visit):
    tiles, depth, tile = weights_ref.shape
    per = (operand_ref.shape[0] // unit_rows - 1) // group

    def where(i):
        code = plan_ref[tiles + 1, i]
        s = code // per
        first = (code - s * per) * group
        return jnp.minimum(s, tiles - 1), [plan_ref[s, first + k] for k in range(group)]

    def step(j, carry):
        for k in range(span):
            s, units = where(span * j + k)
            rows = jnp.concatenate(
                [
                    operand_ref[pl.ds(pl.multiple_of(u * unit_rows, unit_rows), unit_rows), :]
                    for u in units
                ],
                axis=0,
            )
            buffers[k][...] = jnp.dot(rows, weights_ref[s], preferred_element_type=f32)
        for k in range(span):
            visit(*where(span * j + k), buffers[k])
        return carry

    lax.fori_loop(0, (items + span - 1) // span, step, 0)


def row_pass(
    which, plan_ref, points_ref, need_ref, w0, w1, w2, w3, lse_ref,
    held_ref, sems, operand_ref, weights_ref, total_ref, *buffers,
):
    tiles, depth, tile = weights_ref.shape
    items = plan_ref[tiles + 2, which]

    @pl.when(items == 0)
    def _():
        lse_ref[...] = jnp.full_like(lse_ref, nothing)

    @pl.when(items > 0)
    def _():
        load_all(points_ref, None, (w0, w1, w2, w3), held_ref, sems, operand_ref, weights_ref)
        total_ref[...] = jnp.zeros_like(total_ref)

        def visit(s, units, buffer):
            part = jnp.exp2(buffer[...]).reshape(4, unit_rows * group // 32, 8, tile)
            total_ref[s] += jnp.sum(jnp.sum(part, axis=1), axis=0)

        pipeline(plan_ref, items, operand_ref, weights_ref, buffers, visit)
        total = jnp.sum(total_ref[...], axis=1)
        lse_ref[...] = jnp.where(total > 0.0, jnp.log2(jnp.maximum(total, 1e-37)), nothing)
        fine = (total > 1e-25) & (total < 1e30)
        bad = jnp.where(fine, 0.0, need_ref[...])

        @pl.when(jnp.max(bad) > 0.0)
        def _():
            def one_tile(s, carry):
                weights = weights_ref[s]

                def step(i, state):
                    high, total = state
                    unit = plan_ref[s, i]
                    rows = operand_ref[
                        pl.ds(pl.multiple_of(unit * unit_rows, unit_rows), unit_rows), :
                    ]
                    score = jnp.dot(rows, weights, preferred_element_type=f32)
                    score = score.reshape(unit_rows // 8, 8, tile)
                    new = jnp.maximum(high, jnp.max(score, axis=0))
                    total = total * jnp.exp2(high - new)
                    return new, total + jnp.sum(jnp.exp2(score - new[None]), axis=0)

                start = (jnp.full((8, tile), floor, f32), jnp.zeros((8, tile), f32))
                high, total = lax.fori_loop(0, plan_ref[s, 127], step, start)
                top = jnp.max(high, axis=0, keepdims=True)
                total = jnp.sum(total * jnp.exp2(high - top), axis=0, keepdims=True)
                lse_ref[pl.ds(s, 1), :] = jnp.where(
                    total > 0.0, top + jnp.log2(jnp.maximum(total, 1e-37)), nothing
                )
                return carry

            lax.fori_loop(0, tiles, one_tile, 0)


def column_pass(
    which, plan_ref, points_ref, need_ref, w0, w1, w2, w3, lse_ref, mass_ref, a0, a1, a2, a3,
    o0, o1, o2, o3, held_ref, sems, operand_ref, weights_ref, total_ref, high_ref, *buffers,
):
    tiles, depth, tile = weights_ref.shape
    items = plan_ref[tiles + 2, which]
    outs = (o0, o1, o2, o3)

    @pl.when(items == 0)
    def _():
        for out, other in zip(outs, (a0, a1, a2, a3)):
            out[...] = other[...]

    @pl.when(items > 0)
    def _():
        shift = mass_ref[...] - lse_ref[...]
        load_all(points_ref, shift, (w0, w1, w2, w3), held_ref, sems, operand_ref, weights_ref)
        total_ref[...] = jnp.zeros_like(total_ref)

        def visit(s, units, buffer):
            for k, u in enumerate(units):
                where = pl.ds(pl.multiple_of(u * unit_rows, unit_rows), unit_rows)
                part = jnp.exp2(buffer[k * unit_rows : (k + 1) * unit_rows, :])
                total_ref[where, :] += part[:, 0:128] + part[:, 128:256]

        pipeline(plan_ref, items, operand_ref, weights_ref, buffers, visit)
        eye = lax.broadcasted_iota(jnp.int32, (128, 128), 0) == lax.broadcasted_iota(
            jnp.int32, (128, 128), 1
        )
        x_here = lax.axis_index("row") // ring

        def to_row(column):
            return jnp.sum(
                jnp.where(eye[0 : column.shape[0]], column, 0.0), axis=0, keepdims=True
            )

        def blocks():
            for k in range(ring):
                for j in range(ring):
                    shard = lax.rem(x_here + k, ring) * ring + j
                    for i, size in enumerate((128, 128, 32)):
                        start = pl.multiple_of(shard * 288 + 128 * i, 32)
                        yield outs[k], 8 * j + i, pl.ds(start, size), shard * 8 + i

        for out in outs:
            out[...] = jnp.full_like(out, nothing)
        bad = jnp.zeros((1, 128), f32)
        for out, row, where, spot in blocks():
            sums = to_row(jnp.sum(total_ref[where, :], axis=1, keepdims=True))
            out[row : row + 1, :] = jnp.where(
                sums > 0.0, jnp.log2(jnp.maximum(sums, 1e-37)), nothing
            )
            bad = jnp.maximum(bad, jnp.where(sums > 1e-25, 0.0, need_ref[pl.ds(spot, 1), :]))

        @pl.when(jnp.max(bad) > 0.0)
        def _():
            total_ref[...] = jnp.zeros_like(total_ref)
            high_ref[...] = jnp.full_like(high_ref, floor)

            def one_tile(s, carry):
                def step(i, inner):
                    unit = plan_ref[s, i]
                    where = pl.ds(pl.multiple_of(unit * unit_rows, unit_rows), unit_rows)
                    score = jnp.dot(
                        operand_ref[where, :], weights_ref[s], preferred_element_type=f32
                    )
                    a, b = score[:, 0:128], score[:, 128:256]
                    old = high_ref[where, :]
                    new = jnp.maximum(old, jnp.maximum(a, b))
                    high_ref[where, :] = new
                    total_ref[where, :] = (
                        total_ref[where, :] * jnp.exp2(old - new)
                        + jnp.exp2(a - new)
                        + jnp.exp2(b - new)
                    )
                    return inner

                lax.fori_loop(0, plan_ref[s, 127], step, 0)
                return carry

            lax.fori_loop(0, tiles, one_tile, 0)
            for out, row, where, spot in blocks():
                high = high_ref[where, :]
                top = jnp.max(high, axis=1, keepdims=True)
                rest = total_ref[where, :] * jnp.exp2(high - top)
                sums = to_row(jnp.sum(rest, axis=1, keepdims=True))
                out[row : row + 1, :] = jnp.where(
                    sums > 0.0, to_row(top) + jnp.log2(jnp.maximum(sums, 1e-37)), nothing
                )


def merged(refs):
    parts = [ref[...] for ref in refs]
    top = functools.reduce(jnp.maximum, parts)
    return top + jnp.log2(sum(jnp.exp2(p - top) for p in parts))


def merge_columns(a0, a1, a2, a3, o0, o1, o2, o3, held_ref):
    held_ref[...] = merged((a0, a1, a2, a3))
    row = lax.axis_index("row")
    y_here = row - row // ring * ring
    for k, out in enumerate((o0, o1, o2, o3)):
        out[...] = held_ref[pl.ds(pl.multiple_of(lax.rem(y_here + k, ring) * 8, 8), 8), :]


def log_sum(parts):
    top = functools.reduce(jnp.maximum, parts)
    total = sum(jnp.exp2(p - top) for p in parts)
    return top + jnp.log2(total)


def roles(parity, cols):
    four = [d % cols for d in ((-2, -1, 0, 1), (-1, 0, 1, 2))[parity]]
    lead = [0, (1, -1)[parity] % cols]
    near = lead + [d for d in four if d not in lead]
    out = [(2, -2)[parity] % cols, cols // 2]
    begin = four[0]
    out += [(begin + 5) % cols, (begin + 6) % cols]
    return near, out + [d for d in range(cols) if d not in near and d not in out]


def filled(hops, count, cols):
    found = dict(hops)
    back = {d: s for s, d in hops}
    for rank in range(4):
        free = [d for d in range(count) if d not in back]
        for s in [s for s in range(count) if s not in found]:
            if rank == 0:
                picks = [back[s]] if s in back and back[s] in free else []
            elif rank == 1:
                picks = [s ^ 1] if s ^ 1 in free else []
            else:
                picks = [d for d in free if d != s and (d // cols == s // cols or rank == 3)]
                picks.sort(key=lambda d: min((d - s) % cols, (s - d) % cols))
            if picks:
                found[s] = picks[0]
                back[picks[0]] = s
                free.remove(picks[0])
    return sorted(found.items())


def shards(src_points, dst_points, dst_potential, partners, partner_count, src_count, dst_count):
    src_tiles = src_count.shape[0]
    dst_tiles = dst_count.shape[0]
    tile = src_points.shape[0] // src_tiles
    slots = partners.shape[1]
    rows = lax.axis_size("row")
    cols = lax.axis_size("col")
    row_here = lax.axis_index("row")
    col_here = lax.axis_index("col")
    share = dst_points.shape[0]
    points = dst_tiles * tile
    smem = pl.BlockSpec(memory_space=pltpu.SMEM)
    vmem = pl.BlockSpec(memory_space=pltpu.VMEM)
    anywhere = pl.BlockSpec(memory_space=pl.ANY)
    params = pltpu.CompilerParams(vmem_limit_bytes=24 * 1024 * 1024)
    places = [roles(r % 2, cols) for r in range(rows)]
    near = [[(r + d) % cols for d in places[r][0]] for r in range(rows)]
    far = [[(r + d) % cols for d in places[r][1]] for r in range(rows)]
    parity = lax.rem(row_here, 2)
    apart = lax.rem(col_here - row_here + 2 - parity + cols, cols)
    in_near = apart < 4
    in_far = (
        (apart == 5)
        | (apart == 6)
        | (apart == jnp.where(parity == 0, 4, cols - 1))
        | (apart == jnp.where(parity == 0, 10, 9))
    )

    def send(a, hops, full=True):
        hops = [(s[0] * cols + s[1], d[0] * cols + d[1]) for s, d in hops]
        return lax.ppermute(a, ("row", "col"), filled(hops, rows * cols, cols) if full else hops)

    every = [(r, c) for r in range(rows) for c in range(cols)]

    wire = pl.pallas_call(
        pack_targets,
        out_shape=jax.ShapeDtypeStruct((share // 2 + 8, 128), f32),
        in_specs=[anywhere] * 3,
        out_specs=vmem,
        scratch_shapes=[
            pltpu.VMEM((128, 384), f32),
            pltpu.VMEM((8, 384), f32),
            pltpu.SMEM((dst_tiles,), jnp.int32),
            pltpu.VMEM((64, share), f32),
            pltpu.VMEM((share,), f32),
            pltpu.SemaphoreType.DMA((3,)),
        ],
        compiler_params=params,
    )(dst_count, dst_points.T, dst_potential)

    def around(r, dx, dy):
        return (r // ring + dx) % ring * ring + (r + dy) % ring

    def first_hop(r, c, k):
        return around(r, 0, k) if c % 2 == 0 else around(r, k, 0)

    def second_hop(r, c, k):
        return around(r, k, 0) if c % 2 == 0 else around(r, 0, k)

    bundle = jnp.stack(
        [wire]
        + [send(wire, [((r, c), (first_hop(r, c, k), c)) for r, c in every]) for k in (1, 2, 3)]
    )
    busy = [set(near[r] + far[r][:2]) for r in range(rows)]
    slot_on = jnp.arange(slots, dtype=jnp.int32)[None, :] < partner_count[:, None]
    local = jnp.where(slot_on, partners - col_here * dst_tiles, -1)
    plan = pl.pallas_call(
        plan_work,
        out_shape=jax.ShapeDtypeStruct((24, 128), jnp.int32),
        in_specs=[smem, vmem],
        out_specs=vmem,
        compiler_params=params,
    )(dst_count, jnp.pad(local, ((0, 24 - src_tiles), (0, 0)), constant_values=-1))
    plan, local, dst_count, src_count, bundle = lax.optimization_barrier(
        (plan, local, dst_count, src_count, bundle)
    )
    wires = [bundle] + [
        send(
            bundle,
            [
                ((r, c), (second_hop(r, c, k), c))
                for r, c in every
                if c in busy[second_hop(r, c, k)]
            ],
            full=False,
        )
        for k in (1, 2, 3)
    ]
    place = jnp.arange(tile, dtype=jnp.int32)
    src_live = place[None, :] < src_count[:, None]
    dst_live = place[None, :] < dst_count[:, None]
    wanted = jnp.any(local[:, :, None] == jnp.arange(dst_tiles, dtype=jnp.int32), axis=1)
    src_need = jnp.where(src_live & jnp.any(wanted, axis=1)[:, None], 1.0, 0.0)
    dst_need = jnp.where(dst_live & jnp.any(wanted, axis=0)[:, None], 1.0, 0.0)
    dst_need = jnp.pad(dst_need.reshape(rows, share), ((0, 0), (0, 1024 - share)))
    dst_need = dst_need.reshape(rows * 8, 128)
    counted = src_count.astype(f32)
    all_src = src_tiles * rows
    mass = jnp.where(src_live, -jnp.log2(counted)[:, None] - math.log2(all_src), nothing)

    scratch = [
        pltpu.VMEM((ring, ring) + wire.shape, f32),
        pltpu.SemaphoreType.DMA((ring,)),
        pltpu.VMEM((points + unit_rows, 256), bf16),
        pltpu.VMEM((src_tiles, 256, tile), bf16),
    ]
    buffers = [pltpu.VMEM((unit_rows * group, tile), f32)] * span
    heavy = pl.CostEstimate(flops=8_000_000_000, bytes_accessed=4_000_000, transcendentals=8_000_000)
    light = pl.CostEstimate(flops=100_000_000, bytes_accessed=100_000, transcendentals=100_000)
    turned = src_points.T

    def sum_rows(which, cost):
        return pl.pallas_call(
            functools.partial(row_pass, which),
            out_shape=jax.ShapeDtypeStruct((src_tiles, tile), f32),
            in_specs=[smem] + [vmem] * 2 + [anywhere] * ring,
            out_specs=vmem,
            scratch_shapes=scratch + [pltpu.VMEM((src_tiles, 8, tile), f32)] + buffers,
            compiler_params=params,
            cost_estimate=cost,
        )(plan, turned, src_need, *wires)

    def sum_columns(which, lse, others, cost):
        return pl.pallas_call(
            functools.partial(column_pass, which),
            out_shape=[jax.ShapeDtypeStruct((8 * ring, 128), f32)] * ring,
            in_specs=[smem] + [vmem] * 2 + [anywhere] * ring + [vmem] * (2 + ring),
            out_specs=[vmem] * ring,
            scratch_shapes=scratch + [pltpu.VMEM((points + unit_rows, 128), f32)] * 2 + buffers,
            compiler_params=params,
            cost_estimate=cost,
        )(plan, turned, dst_need, *wires, lse, mass, *others)

    far_lse = sum_rows(1, light)
    hops = []
    for r in range(rows):
        for k in (0, 1):
            loop = [far[r][k], near[r][k], near[r][2 + k], far[r][k] ^ 1]
            hops += [((r, loop[i]), (r, loop[(i + 1) % 4])) for i in range(4)]
    early = send(far_lse, hops)
    near_lse = sum_rows(0, heavy)
    got_early = (col_here == row_here) | (col_here == row_here + 1 - 2 * parity)
    lse = log_sum([near_lse, jnp.where(got_early, early, nothing)])

    def pairs(test):
        return [((r, c), (r, d)) for r in range(rows) for c in near[r] for d in near[r] if test(c, d)]

    lse = log_sum(
        [
            lse,
            send(lse, [((r, c), (r, c ^ 1)) for r, c in every]),
            send(lse, pairs(lambda c, d: (c - d) % cols in (2, cols - 2))),
            send(lse, pairs(lambda c, d: (c - (d ^ 1)) % cols in (2, cols - 2))),
        ]
    )
    spread = send(lse, [((r, near[r][k]), (r, far[r][k])) for r in range(rows) for k in range(4)])
    blank = [jnp.full((8 * ring, 128), nothing, f32)] * ring
    near_part = sum_columns(0, lse, blank, heavy)
    col_part = sum_columns(1, spread, near_part, light)
    known = jnp.where(in_far, spread, lse)
    known, last = lax.optimization_barrier((known, col_part[0]))
    rest = send(
        known,
        [((r, (near[r] + far[r])[k]), (r, far[r][4 + k])) for r in range(rows) for k in range(8)],
    )
    col_part = [last] + [
        send(col_part[k], [((r, c), (around(r, k, 0), c)) for r, c in every]) for k in (1, 2, 3)
    ]
    col_part = pl.pallas_call(
        merge_columns,
        out_shape=[jax.ShapeDtypeStruct((8, 128), f32)] * ring,
        in_specs=[vmem] * ring,
        out_specs=[vmem] * ring,
        scratch_shapes=[pltpu.VMEM((8 * ring, 128), f32)],
        compiler_params=params,
    )(*col_part)
    col_part = [col_part[0]] + [
        send(col_part[k], [((r, c), (around(r, 0, k), c)) for r, c in every]) for k in (1, 2, 3)
    ]
    col_log = log_sum(col_part).reshape(-1)[:share]

    row_lse = jnp.where(in_near | in_far, known, rest)
    src_potential = jnp.where(
        src_live,
        entropy * (-jnp.log(counted)[:, None] - math.log(all_src) - ln2 * row_lse),
        0.0,
    ).reshape(-1)

    spot = row_here * share + jnp.arange(share, dtype=jnp.int32)
    spot_tile = spot // tile
    spot_count = jnp.sum(
        jnp.where(
            spot_tile[:, None] == jnp.arange(dst_tiles, dtype=jnp.int32)[None, :],
            dst_count[None, :],
            0,
        ),
        axis=1,
    )
    dst_new = jnp.where(
        (spot - spot_tile * tile < spot_count) & (col_log > 0.5 * nothing),
        entropy
        * (-jnp.log(spot_count.astype(f32)) - math.log(dst_tiles * cols) - ln2 * col_log)
        + dst_potential,
        0.0,
    )
    return src_potential, dst_new


def solution(mesh):
    in_specs = (
        P("row", None),
        P(("col", "row"), None),
        P(("col", "row")),
        P("row", None),
        P("row"),
        P("row"),
        P("col"),
    )
    out_specs = (P("row"), P(("col", "row")))
    return jax.shard_map(shards, mesh=mesh, in_specs=in_specs, out_specs=out_specs, check_vma=False)
```

```python
import functools
import math

import jax
import jax.numpy as jnp
from jax import lax
from jax.experimental import pallas as pl
from jax.experimental.pallas import tpu as pltpu
from jax.sharding import PartitionSpec as P

entropy = 0.1
scale = math.log2(math.e) / entropy
ln2 = math.log(2.0)
nothing = -1e30
floor = -1e25
unit_rows = 64
group = 12
span = 8
ring = 4
f32 = jnp.float32
bf16 = jnp.bfloat16


def pieces(a):
    first = a.astype(bf16).astype(f32)
    rest = a - first
    second = rest.astype(bf16).astype(f32)
    return first, second, rest - second


def extra_rows(bias):
    place = lax.broadcasted_iota(jnp.int32, (64, bias.shape[1]), 0)
    block = jnp.where(place < 3, 1.0, 0.0)
    for k, piece in enumerate(pieces(bias)):
        block = jnp.where(place == 3 + k, piece, block)
    return block.astype(bf16)


def pack_targets(
    count_ref, points_ref, potential_ref, wire_ref, square_ref, line_ref, tally_ref, held_ref, level_ref, sems,
):
    copies = [
        pltpu.make_async_copy(source, target, sems.at[k])
        for k, (source, target) in enumerate(
            ((points_ref, held_ref), (potential_ref, level_ref), (count_ref, tally_ref))
        )
    ]
    for copy in copies:
        copy.start()
    share = held_ref.shape[1]
    tile = 256
    mid = share // 2
    begin = lax.axis_index("row") * share
    first_tile = begin // tile
    offset = begin - first_tile * tile
    last_tile = jnp.minimum(first_tile + 1, tally_ref.shape[0] - 1)
    square_ref[...] = jnp.zeros_like(square_ref)
    line_ref[...] = jnp.full_like(line_ref, nothing)
    wire_ref[mid : mid + 8, :] = jnp.zeros((8, 128), f32)
    for copy in copies:
        copy.wait()
    points = held_ref[...]
    square_ref[0:64, 0:share] = points
    turned = square_ref[...].T
    wire_ref[0:mid, :] = scale * (turned[0:mid] + pltpu.roll(turned[mid:share], 64, 1))
    level = level_ref[...].reshape(1, share)
    level = scale * (level - 0.5 * jnp.sum(points * points, axis=0, keepdims=True))
    spot = offset + lax.broadcasted_iota(jnp.int32, (1, share), 1)
    place = jnp.where(spot < tile, spot, spot - tile)
    bound = jnp.where(spot < tile, tally_ref[first_tile], tally_ref[last_tile])
    line_ref[0:1, 0:share] = jnp.where(place < bound, level, nothing)
    for k in range(3):
        wire_ref[mid + k : mid + k + 1, :] = line_ref[0:1, 128 * k : 128 * (k + 1)]


def unpack_targets(held_ref, arrived, operand_ref):
    lane = lax.broadcasted_iota(jnp.int32, (144, 128), 1)
    front = lane < 64
    sublane = lax.broadcasted_iota(jnp.int32, (16, 384), 0)
    pick_row = lax.broadcasted_iota(jnp.int32, (16, 128), 0)
    pick_lane = lax.broadcasted_iota(jnp.int32, (16, 128), 1)
    pick = jnp.where((pick_lane == pick_row + 64) & (pick_row < 6), 1.0, 0.0).astype(bf16)
    row_here = lax.axis_index("row")
    x_here = row_here // ring
    y_here = row_here - x_here * ring
    even = lax.rem(lax.axis_index("col"), 2) == 0
    for k in range(ring):
        arrived(k)
        for j in range(ring):
            x = lax.rem(x_here + ring - jnp.where(even, k, j), ring)
            y = lax.rem(y_here + ring - jnp.where(even, j, k), ring)
            a = pl.multiple_of((x * ring + y) * 288, 16)
            b = pl.multiple_of((x * ring + y) * 288 + 144, 16)
            both = held_ref[k, j, 0:144, :]
            high = both.astype(bf16).astype(f32)
            low = both - high
            high_back = pltpu.roll(high, 64, 1)
            low_back = pltpu.roll(low, 64, 1)
            tail = held_ref[k, j, 144:152, :]
            line = jnp.concatenate([tail[0:1], tail[1:2], tail[2:3]], axis=1)
            stacked = jnp.where(sublane < 6, 1.0, 0.0)
            for i, piece in enumerate(pieces(line)):
                stacked = jnp.where(sublane == i, piece, stacked)
            extra = lax.dot_general(
                stacked.astype(bf16), pick, (((0,), (0,)), ((), ())), preferred_element_type=f32
            )
            operand_ref[pl.ds(a, 144), 0:128] = jnp.where(front, high, low_back).astype(bf16)
            operand_ref[pl.ds(a, 144), 128:256] = jnp.where(front, high, extra[0:144]).astype(bf16)
            operand_ref[pl.ds(b, 144), 0:128] = jnp.where(front, high_back, low).astype(bf16)
            operand_ref[pl.ds(b, 144), 128:256] = jnp.where(
                front, high_back, extra[144:288]
            ).astype(bf16)
    rows = ring * ring * 288
    dummy_lane = lax.broadcasted_iota(jnp.int32, (unit_rows, 256), 1)
    operand_ref[rows : rows + unit_rows, :] = jnp.where(dummy_lane == 192, nothing, 0.0).astype(bf16)


def load_weights(points_ref, weights_ref, shift):
    tiles, depth, tile = weights_ref.shape
    for s in range(tiles):
        x = points_ref[:, s * tile : (s + 1) * tile]
        high = x.astype(bf16)
        low = (x - high.astype(f32)).astype(bf16)
        bias = (-0.5 * scale) * jnp.sum(x * x, axis=0, keepdims=True)
        weights_ref[s, 0:64, :] = high
        weights_ref[s, 64:128, :] = high
        weights_ref[s, 128:192, :] = low
        weights_ref[s, 192:256, :] = extra_rows(bias if shift is None else bias + shift[s : s + 1, :])


def load_all(points_ref, shift, wires, rows_ref, held_ref, sems, operand_ref, weights_ref):
    points = pltpu.make_async_copy(points_ref, rows_ref, sems.at[ring])
    copies = [
        pltpu.make_async_copy(wire, held_ref.at[k], sems.at[k]) for k, wire in enumerate(wires)
    ]
    points.start()
    for copy in copies:
        copy.start()
    points.wait()
    load_weights(rows_ref, weights_ref, shift)
    unpack_targets(held_ref, lambda k: copies[k].wait(), operand_ref)


def plan_work(count_ref, local_ref, plan_ref):
    src_tiles = local_ref.shape[0] - 6
    per_tile = 256 // unit_rows
    units = count_ref.shape[0] * per_tile
    per = units // group
    unit = lax.broadcasted_iota(jnp.int32, (24, 128), 1)
    tile_of = unit // per_tile
    bound = jnp.zeros((24, 128), jnp.int32)
    for t in range(count_ref.shape[0]):
        bound = jnp.where(tile_of == t, count_ref[t], bound)
    live = bound > (unit - tile_of * per_tile) * unit_rows
    hits = jnp.zeros((24, 128), f32)
    for k in range(local_ref.shape[1]):
        hits = jnp.where(local_ref[:, k : k + 1] == tile_of, 1.0, hits)
    active = jnp.where(live, hits, 0.0)
    down = lax.broadcasted_iota(jnp.int32, (128, 128), 0)
    across = lax.broadcasted_iota(jnp.int32, (128, 128), 1)
    upto = jnp.where(down <= across, 1.0, 0.0).astype(bf16)
    rank = jnp.dot(active.astype(bf16), upto, preferred_element_type=f32)
    counts = jnp.broadcast_to(rank[:, 127:128], (24, 128))
    place = jnp.where(active > 0.0, rank - 1.0, -1.0)
    place = jnp.concatenate([place, jnp.full((104, 128), -1.0, f32)], axis=0).T
    position = across.astype(f32)
    value = (down - units).astype(f32)
    plan_ref[...] = jnp.full_like(plan_ref, units)
    last = lax.broadcasted_iota(jnp.int32, (1, 128), 1)
    chunks = jnp.floor((counts + (group - 0.5)) / group).astype(jnp.int32)
    begin = jnp.zeros((1, 128), jnp.int32)
    items = jnp.full((1, 128), src_tiles * per, jnp.int32)
    for s in range(src_tiles):
        listed = jnp.sum(
            jnp.where(place[:, s : s + 1] == position, value, 0.0), axis=0, keepdims=True
        )
        plan_ref[s : s + 1, :] = jnp.where(
            last == 127, counts[s : s + 1], listed + units
        ).astype(jnp.int32)
        along = last - begin
        inside = (along >= 0) & (along < chunks[s : s + 1])
        items = jnp.where(inside, s * per + along, items)
        begin = begin + chunks[s : s + 1]
    plan_ref[src_tiles + 1 : src_tiles + 2, :] = items
    row = lax.axis_index("row")
    apart = lax.axis_index("col") - row + 2 - lax.rem(row, 2) + 16
    near = jnp.where(lax.rem(apart, 16) < 4, 1, 0)
    plan_ref[src_tiles + 2 : src_tiles + 3, :] = begin * jnp.where(last == 0, near, 1 - near)


def pipeline(plan_ref, items, operand_ref, weights_ref, buffers, visit):
    tiles, depth, tile = weights_ref.shape
    per = (operand_ref.shape[0] // unit_rows - 1) // group

    def where(i):
        code = plan_ref[tiles + 1, i]
        s = code // per
        first = (code - s * per) * group
        return jnp.minimum(s, tiles - 1), [plan_ref[s, first + k] for k in range(group)]

    def step(j, carry):
        for k in range(span):
            s, units = where(span * j + k)
            rows = jnp.concatenate(
                [
                    operand_ref[pl.ds(pl.multiple_of(u * unit_rows, unit_rows), unit_rows), :]
                    for u in units
                ],
                axis=0,
            )
            buffers[k][...] = jnp.dot(rows, weights_ref[s], preferred_element_type=f32)
        for k in range(span):
            visit(*where(span * j + k), buffers[k])
        return carry

    lax.fori_loop(0, (items + span - 1) // span, step, 0)


def row_pass(
    which, plan_ref, points_ref, need_ref, w0, w1, w2, w3, lse_ref,
    rows_ref, held_ref, sems, operand_ref, weights_ref, total_ref, *buffers,
):
    tiles, depth, tile = weights_ref.shape
    items = plan_ref[tiles + 2, which]

    @pl.when(items == 0)
    def _():
        lse_ref[...] = jnp.full_like(lse_ref, nothing)

    @pl.when(items > 0)
    def _():
        load_all(points_ref, None, (w0, w1, w2, w3), rows_ref, held_ref, sems, operand_ref, weights_ref)
        total_ref[...] = jnp.zeros_like(total_ref)

        def visit(s, units, buffer):
            part = jnp.exp2(buffer[...]).reshape(4, unit_rows * group // 32, 8, tile)
            total_ref[s] += jnp.sum(jnp.sum(part, axis=1), axis=0)

        pipeline(plan_ref, items, operand_ref, weights_ref, buffers, visit)
        total = jnp.sum(total_ref[...], axis=1)
        lse_ref[...] = jnp.where(total > 0.0, jnp.log2(jnp.maximum(total, 1e-37)), nothing)
        fine = (total > 1e-25) & (total < 1e30)
        bad = jnp.where(fine, 0.0, need_ref[...])

        @pl.when(jnp.max(bad) > 0.0)
        def _():
            def one_tile(s, carry):
                weights = weights_ref[s]

                def step(i, state):
                    high, total = state
                    unit = plan_ref[s, i]
                    rows = operand_ref[
                        pl.ds(pl.multiple_of(unit * unit_rows, unit_rows), unit_rows), :
                    ]
                    score = jnp.dot(rows, weights, preferred_element_type=f32)
                    score = score.reshape(unit_rows // 8, 8, tile)
                    new = jnp.maximum(high, jnp.max(score, axis=0))
                    total = total * jnp.exp2(high - new)
                    return new, total + jnp.sum(jnp.exp2(score - new[None]), axis=0)

                start = (jnp.full((8, tile), floor, f32), jnp.zeros((8, tile), f32))
                high, total = lax.fori_loop(0, plan_ref[s, 127], step, start)
                top = jnp.max(high, axis=0, keepdims=True)
                total = jnp.sum(total * jnp.exp2(high - top), axis=0, keepdims=True)
                lse_ref[pl.ds(s, 1), :] = jnp.where(
                    total > 0.0, top + jnp.log2(jnp.maximum(total, 1e-37)), nothing
                )
                return carry

            lax.fori_loop(0, tiles, one_tile, 0)


def column_pass(
    which, plan_ref, points_ref, need_ref, w0, w1, w2, w3, lse_ref, mass_ref, other_ref, out_ref,
    rows_ref, held_ref, sems, operand_ref, weights_ref, total_ref, high_ref, *buffers,
):
    tiles, depth, tile = weights_ref.shape
    items = plan_ref[tiles + 2, which]

    @pl.when(items == 0)
    def _():
        out_ref[...] = other_ref[...]

    @pl.when(items > 0)
    def _():
        shift = mass_ref[...] - lse_ref[...]
        load_all(points_ref, shift, (w0, w1, w2, w3), rows_ref, held_ref, sems, operand_ref, weights_ref)
        total_ref[...] = jnp.zeros_like(total_ref)

        def visit(s, units, buffer):
            for k, u in enumerate(units):
                where = pl.ds(pl.multiple_of(u * unit_rows, unit_rows), unit_rows)
                part = jnp.exp2(buffer[k * unit_rows : (k + 1) * unit_rows, :])
                total_ref[where, :] += part[:, 0:128] + part[:, 128:256]

        pipeline(plan_ref, items, operand_ref, weights_ref, buffers, visit)
        eye = lax.broadcasted_iota(jnp.int32, (128, 128), 0) == lax.broadcasted_iota(
            jnp.int32, (128, 128), 1
        )

        def to_row(column):
            return jnp.sum(
                jnp.where(eye[0 : column.shape[0]], column, 0.0), axis=0, keepdims=True
            )

        blocks = [
            (8 * shard + i, slice(shard * 288 + 128 * i, shard * 288 + 128 * i + size))
            for shard in range(ring * ring)
            for i, size in enumerate((128, 128, 32))
        ]
        out_ref[...] = jnp.full_like(out_ref, nothing)
        bad = jnp.zeros((1, 128), f32)
        for row, where in blocks:
            sums = to_row(jnp.sum(total_ref[where, :], axis=1, keepdims=True))
            out_ref[row : row + 1, :] = jnp.where(
                sums > 0.0, jnp.log2(jnp.maximum(sums, 1e-37)), nothing
            )
            bad = jnp.maximum(bad, jnp.where(sums > 1e-25, 0.0, need_ref[row : row + 1, :]))

        @pl.when(jnp.max(bad) > 0.0)
        def _():
            total_ref[...] = jnp.zeros_like(total_ref)
            high_ref[...] = jnp.full_like(high_ref, floor)

            def one_tile(s, carry):
                def step(i, inner):
                    unit = plan_ref[s, i]
                    where = pl.ds(pl.multiple_of(unit * unit_rows, unit_rows), unit_rows)
                    score = jnp.dot(
                        operand_ref[where, :], weights_ref[s], preferred_element_type=f32
                    )
                    a, b = score[:, 0:128], score[:, 128:256]
                    old = high_ref[where, :]
                    new = jnp.maximum(old, jnp.maximum(a, b))
                    high_ref[where, :] = new
                    total_ref[where, :] = (
                        total_ref[where, :] * jnp.exp2(old - new)
                        + jnp.exp2(a - new)
                        + jnp.exp2(b - new)
                    )
                    return inner

                lax.fori_loop(0, plan_ref[s, 127], step, 0)
                return carry

            lax.fori_loop(0, tiles, one_tile, 0)
            for row, where in blocks:
                high = high_ref[where, :]
                top = jnp.max(high, axis=1, keepdims=True)
                rest = total_ref[where, :] * jnp.exp2(high - top)
                sums = to_row(jnp.sum(rest, axis=1, keepdims=True))
                out_ref[row : row + 1, :] = jnp.where(
                    sums > 0.0, to_row(top) + jnp.log2(jnp.maximum(sums, 1e-37)), nothing
                )


def log_sum(parts):
    top = functools.reduce(jnp.maximum, parts)
    total = sum(jnp.exp2(p - top) for p in parts)
    return top + jnp.log2(total)


def roles(parity, cols):
    four = [d % cols for d in ((-2, -1, 0, 1), (-1, 0, 1, 2))[parity]]
    lead = [0, (1, -1)[parity] % cols]
    near = lead + [d for d in four if d not in lead]
    out = [(2, -2)[parity] % cols, cols // 2]
    begin = four[0]
    out += [(begin + 5) % cols, (begin + 6) % cols]
    return near, out + [d for d in range(cols) if d not in near and d not in out]


def filled(hops, count, cols):
    found = dict(hops)
    back = {d: s for s, d in hops}
    for rank in range(4):
        free = [d for d in range(count) if d not in back]
        for s in [s for s in range(count) if s not in found]:
            if rank == 0:
                picks = [back[s]] if s in back and back[s] in free else []
            elif rank == 1:
                picks = [s ^ 1] if s ^ 1 in free else []
            else:
                picks = [d for d in free if d != s and (d // cols == s // cols or rank == 3)]
                picks.sort(key=lambda d: min((d - s) % cols, (s - d) % cols))
            if picks:
                found[s] = picks[0]
                back[picks[0]] = s
                free.remove(picks[0])
    return sorted(found.items())


def shards(src_points, dst_points, dst_potential, partners, partner_count, src_count, dst_count):
    src_tiles = src_count.shape[0]
    dst_tiles = dst_count.shape[0]
    tile = src_points.shape[0] // src_tiles
    slots = partners.shape[1]
    rows = lax.axis_size("row")
    cols = lax.axis_size("col")
    row_here = lax.axis_index("row")
    col_here = lax.axis_index("col")
    share = dst_points.shape[0]
    points = dst_tiles * tile
    smem = pl.BlockSpec(memory_space=pltpu.SMEM)
    vmem = pl.BlockSpec(memory_space=pltpu.VMEM)
    anywhere = pl.BlockSpec(memory_space=pl.ANY)
    far_memory = pl.BlockSpec(memory_space=pltpu.HBM)
    params = pltpu.CompilerParams(vmem_limit_bytes=24 * 1024 * 1024)
    places = [roles(r % 2, cols) for r in range(rows)]
    near = [[(r + d) % cols for d in places[r][0]] for r in range(rows)]
    far = [[(r + d) % cols for d in places[r][1]] for r in range(rows)]
    parity = lax.rem(row_here, 2)
    apart = lax.rem(col_here - row_here + 2 - parity + cols, cols)
    in_near = apart < 4
    in_far = (
        (apart == 5)
        | (apart == 6)
        | (apart == jnp.where(parity == 0, 4, cols - 1))
        | (apart == jnp.where(parity == 0, 10, 9))
    )

    def send(a, hops, full=True):
        hops = [(s[0] * cols + s[1], d[0] * cols + d[1]) for s, d in hops]
        return lax.ppermute(a, ("row", "col"), filled(hops, rows * cols, cols) if full else hops)

    every = [(r, c) for r in range(rows) for c in range(cols)]

    wire = pl.pallas_call(
        pack_targets,
        out_shape=jax.ShapeDtypeStruct((share // 2 + 8, 128), f32),
        in_specs=[far_memory] * 3,
        out_specs=vmem,
        scratch_shapes=[
            pltpu.VMEM((128, 384), f32),
            pltpu.VMEM((8, 384), f32),
            pltpu.SMEM((dst_tiles,), jnp.int32),
            pltpu.VMEM((64, share), f32),
            pltpu.VMEM((share,), f32),
            pltpu.SemaphoreType.DMA((3,)),
        ],
        compiler_params=params,
    )(dst_count, dst_points.T, dst_potential)

    def around(r, dx, dy):
        return (r // ring + dx) % ring * ring + (r + dy) % ring

    def first_hop(r, c, k):
        return around(r, 0, k) if c % 2 == 0 else around(r, k, 0)

    def second_hop(r, c, k):
        return around(r, k, 0) if c % 2 == 0 else around(r, 0, k)

    bundle = jnp.stack(
        [wire]
        + [send(wire, [((r, c), (first_hop(r, c, k), c)) for r, c in every]) for k in (1, 2, 3)]
    )
    busy = [set(near[r] + far[r][:2]) for r in range(rows)]
    slot_on = jnp.arange(slots, dtype=jnp.int32)[None, :] < partner_count[:, None]
    local = jnp.where(slot_on, partners - col_here * dst_tiles, -1)
    plan = pl.pallas_call(
        plan_work,
        out_shape=jax.ShapeDtypeStruct((24, 128), jnp.int32),
        in_specs=[smem, vmem],
        out_specs=vmem,
        compiler_params=params,
    )(dst_count, jnp.pad(local, ((0, 24 - src_tiles), (0, 0)), constant_values=-1))
    plan, local, dst_count, src_count, bundle = lax.optimization_barrier(
        (plan, local, dst_count, src_count, bundle)
    )
    wires = [bundle] + [
        send(
            bundle,
            [
                ((r, c), (second_hop(r, c, k), c))
                for r, c in every
                if c in busy[second_hop(r, c, k)]
            ],
            full=False,
        )
        for k in (1, 2, 3)
    ]
    place = jnp.arange(tile, dtype=jnp.int32)
    src_live = place[None, :] < src_count[:, None]
    dst_live = place[None, :] < dst_count[:, None]
    wanted = jnp.any(local[:, :, None] == jnp.arange(dst_tiles, dtype=jnp.int32), axis=1)
    src_need = jnp.where(src_live & jnp.any(wanted, axis=1)[:, None], 1.0, 0.0)
    dst_need = jnp.where(dst_live & jnp.any(wanted, axis=0)[:, None], 1.0, 0.0)
    dst_need = jnp.pad(dst_need.reshape(rows, share), ((0, 0), (0, 1024 - share)))
    dst_need = dst_need.reshape(rows * 8, 128)
    counted = src_count.astype(f32)
    all_src = src_tiles * rows
    mass = jnp.where(src_live, -jnp.log2(counted)[:, None] - math.log2(all_src), nothing)

    scratch = [
        pltpu.VMEM((64, src_tiles * tile), f32),
        pltpu.VMEM((ring, ring) + wire.shape, f32),
        pltpu.SemaphoreType.DMA((ring + 1,)),
        pltpu.VMEM((points + unit_rows, 256), bf16),
        pltpu.VMEM((src_tiles, 256, tile), bf16),
    ]
    buffers = [pltpu.VMEM((unit_rows * group, tile), f32)] * span
    heavy = pl.CostEstimate(flops=8_000_000_000, bytes_accessed=4_000_000, transcendentals=8_000_000)
    light = pl.CostEstimate(flops=100_000_000, bytes_accessed=100_000, transcendentals=100_000)
    turned = src_points.T

    def sum_rows(which, cost):
        return pl.pallas_call(
            functools.partial(row_pass, which),
            out_shape=jax.ShapeDtypeStruct((src_tiles, tile), f32),
            in_specs=[smem, far_memory, vmem] + [anywhere] * ring,
            out_specs=vmem,
            scratch_shapes=scratch + [pltpu.VMEM((src_tiles, 8, tile), f32)] + buffers,
            compiler_params=params,
            cost_estimate=cost,
        )(plan, turned, src_need, *wires)

    def sum_columns(which, lse, other, cost):
        return pl.pallas_call(
            functools.partial(column_pass, which),
            out_shape=jax.ShapeDtypeStruct((8 * rows, 128), f32),
            in_specs=[smem, far_memory, vmem] + [anywhere] * ring + [vmem] * 3,
            out_specs=vmem,
            scratch_shapes=scratch + [pltpu.VMEM((points + unit_rows, 128), f32)] * 2 + buffers,
            compiler_params=params,
            cost_estimate=cost,
        )(plan, turned, dst_need, *wires, lse, mass, other)

    far_lse = sum_rows(1, light)
    early = send(
        far_lse,
        [((r, far[r][k]), (r, near[r][k])) for r in range(rows) for k in (0, 1)],
        full=False,
    )
    near_lse = sum_rows(0, heavy)
    got_early = (col_here == row_here) | (col_here == row_here + 1 - 2 * parity)
    lse = log_sum([near_lse, jnp.where(got_early, early, nothing)])

    def pairs(test):
        return [((r, c), (r, d)) for r in range(rows) for c in near[r] for d in near[r] if test(c, d)]

    lse = log_sum(
        [
            lse,
            send(lse, [((r, c), (r, c ^ 1)) for r, c in every]),
            send(lse, pairs(lambda c, d: (c - d) % cols in (2, cols - 2))),
            send(lse, pairs(lambda c, d: (c - (d ^ 1)) % cols in (2, cols - 2))),
        ]
    )
    spread = send(lse, [((r, near[r][k]), (r, far[r][k])) for r in range(rows) for k in range(4)])
    blank = jnp.full((8 * rows, 128), nothing, f32)
    near_part = sum_columns(0, lse, blank, heavy)
    col_part = sum_columns(1, spread, near_part, light)
    known = jnp.where(in_far, spread, lse)
    known, near_part = lax.optimization_barrier((known, near_part))
    rest = send(
        known,
        [((r, (near[r] + far[r])[k]), (r, far[r][4 + k])) for r in range(rows) for k in range(8)],
    )
    parts = lax.all_to_all(col_part.reshape(rows, 8, 128), "row", 0, 0)
    top = jnp.max(parts, axis=0)
    col_log = (top + jnp.log2(jnp.sum(jnp.exp2(parts - top), axis=0))).reshape(-1)[:share]

    row_lse = jnp.where(in_near | in_far, known, rest)
    src_potential = jnp.where(
        src_live,
        entropy * (-jnp.log(counted)[:, None] - math.log(all_src) - ln2 * row_lse),
        0.0,
    ).reshape(-1)

    spot = row_here * share + jnp.arange(share, dtype=jnp.int32)
    spot_tile = spot // tile
    spot_count = jnp.sum(
        jnp.where(
            spot_tile[:, None] == jnp.arange(dst_tiles, dtype=jnp.int32)[None, :],
            dst_count[None, :],
            0,
        ),
        axis=1,
    )
    dst_new = jnp.where(
        (spot - spot_tile * tile < spot_count) & (col_log > 0.5 * nothing),
        entropy
        * (-jnp.log(spot_count.astype(f32)) - math.log(dst_tiles * cols) - ln2 * col_log)
        + dst_potential,
        0.0,
    )
    return src_potential, dst_new


def solution(mesh):
    in_specs = (
        P("row", None),
        P(("col", "row"), None),
        P(("col", "row")),
        P("row", None),
        P("row"),
        P("row"),
        P("col"),
    )
    out_specs = (P("row"), P(("col", "row")))
    return jax.shard_map(shards, mesh=mesh, in_specs=in_specs, out_specs=out_specs, check_vma=False)
```

```python
import functools
import math

import jax
import jax.numpy as jnp
from jax import lax
from jax.experimental import pallas as pl
from jax.experimental.pallas import tpu as pltpu
from jax.sharding import PartitionSpec as P

entropy = 0.1
scale = math.log2(math.e) / entropy
ln2 = math.log(2.0)
nothing = -1e30
floor = -1e25
unit_rows = 64
group = 12
span = 8
ring = 4
f32 = jnp.float32
bf16 = jnp.bfloat16


def pieces(a):
    first = a.astype(bf16).astype(f32)
    rest = a - first
    second = rest.astype(bf16).astype(f32)
    return first, second, rest - second


def extra_rows(bias):
    place = lax.broadcasted_iota(jnp.int32, (64, bias.shape[1]), 0)
    block = jnp.where(place < 3, 1.0, 0.0)
    for k, piece in enumerate(pieces(bias)):
        block = jnp.where(place == 3 + k, piece, block)
    return block.astype(bf16)


def pack_targets(
    count_ref, points_ref, potential_ref, wire_ref, square_ref, line_ref, tally_ref, held_ref, level_ref, sems,
):
    copies = [
        pltpu.make_async_copy(source, target, sems.at[k])
        for k, (source, target) in enumerate(
            ((points_ref, held_ref), (potential_ref, level_ref), (count_ref, tally_ref))
        )
    ]
    for copy in copies:
        copy.start()
    share = held_ref.shape[1]
    tile = 256
    mid = share // 2
    begin = lax.axis_index("row") * share
    first_tile = begin // tile
    offset = begin - first_tile * tile
    last_tile = jnp.minimum(first_tile + 1, tally_ref.shape[0] - 1)
    square_ref[...] = jnp.zeros_like(square_ref)
    line_ref[...] = jnp.full_like(line_ref, nothing)
    wire_ref[mid : mid + 8, :] = jnp.zeros((8, 128), f32)
    for copy in copies:
        copy.wait()
    points = held_ref[...]
    square_ref[0:64, 0:share] = points
    turned = square_ref[...].T
    wire_ref[0:mid, :] = scale * (turned[0:mid] + pltpu.roll(turned[mid:share], 64, 1))
    level = level_ref[...].reshape(1, share)
    level = scale * (level - 0.5 * jnp.sum(points * points, axis=0, keepdims=True))
    spot = offset + lax.broadcasted_iota(jnp.int32, (1, share), 1)
    place = jnp.where(spot < tile, spot, spot - tile)
    bound = jnp.where(spot < tile, tally_ref[first_tile], tally_ref[last_tile])
    line_ref[0:1, 0:share] = jnp.where(place < bound, level, nothing)
    for k in range(3):
        wire_ref[mid + k : mid + k + 1, :] = line_ref[0:1, 128 * k : 128 * (k + 1)]


def unpack_targets(wires, operand_ref):
    lane = lax.broadcasted_iota(jnp.int32, (144, 128), 1)
    front = lane < 64
    sublane = lax.broadcasted_iota(jnp.int32, (16, 384), 0)
    pick_row = lax.broadcasted_iota(jnp.int32, (16, 128), 0)
    pick_lane = lax.broadcasted_iota(jnp.int32, (16, 128), 1)
    pick = jnp.where((pick_lane == pick_row + 64) & (pick_row < 6), 1.0, 0.0).astype(bf16)
    row_here = lax.axis_index("row")
    x_here = row_here // ring
    y_here = row_here - x_here * ring
    even = lax.rem(lax.axis_index("col"), 2) == 0
    for k in range(ring):
        for j in range(ring):
            x = lax.rem(x_here + ring - jnp.where(even, k, j), ring)
            y = lax.rem(y_here + ring - jnp.where(even, j, k), ring)
            a = pl.multiple_of((x * ring + y) * 288, 16)
            b = pl.multiple_of((x * ring + y) * 288 + 144, 16)
            both = wires[k][j, 0:144, :]
            high = both.astype(bf16).astype(f32)
            low = both - high
            high_back = pltpu.roll(high, 64, 1)
            low_back = pltpu.roll(low, 64, 1)
            tail = wires[k][j, 144:152, :]
            line = jnp.concatenate([tail[0:1], tail[1:2], tail[2:3]], axis=1)
            stacked = jnp.where(sublane < 6, 1.0, 0.0)
            for i, piece in enumerate(pieces(line)):
                stacked = jnp.where(sublane == i, piece, stacked)
            extra = lax.dot_general(
                stacked.astype(bf16), pick, (((0,), (0,)), ((), ())), preferred_element_type=f32
            )
            operand_ref[pl.ds(a, 144), 0:128] = jnp.where(front, high, low_back).astype(bf16)
            operand_ref[pl.ds(a, 144), 128:256] = jnp.where(front, high, extra[0:144]).astype(bf16)
            operand_ref[pl.ds(b, 144), 0:128] = jnp.where(front, high_back, low).astype(bf16)
            operand_ref[pl.ds(b, 144), 128:256] = jnp.where(
                front, high_back, extra[144:288]
            ).astype(bf16)
    rows = ring * ring * 288
    dummy_lane = lax.broadcasted_iota(jnp.int32, (unit_rows, 256), 1)
    operand_ref[rows : rows + unit_rows, :] = jnp.where(dummy_lane == 192, nothing, 0.0).astype(bf16)


def load_weights(points_ref, weights_ref, shift):
    tiles, depth, tile = weights_ref.shape
    for s in range(tiles):
        x = points_ref[:, s * tile : (s + 1) * tile]
        high = x.astype(bf16)
        low = (x - high.astype(f32)).astype(bf16)
        bias = (-0.5 * scale) * jnp.sum(x * x, axis=0, keepdims=True)
        weights_ref[s, 0:64, :] = high
        weights_ref[s, 64:128, :] = high
        weights_ref[s, 128:192, :] = low
        weights_ref[s, 192:256, :] = extra_rows(bias if shift is None else bias + shift[s : s + 1, :])


def load_all(points_ref, shift, wires, operand_ref, weights_ref):
    load_weights(points_ref, weights_ref, shift)
    unpack_targets(wires, operand_ref)


def plan_work(count_ref, local_ref, plan_ref):
    src_tiles = local_ref.shape[0] - 6
    per_tile = 256 // unit_rows
    units = count_ref.shape[0] * per_tile
    per = units // group
    unit = lax.broadcasted_iota(jnp.int32, (24, 128), 1)
    tile_of = unit // per_tile
    bound = jnp.zeros((24, 128), jnp.int32)
    for t in range(count_ref.shape[0]):
        bound = jnp.where(tile_of == t, count_ref[t], bound)
    live = bound > (unit - tile_of * per_tile) * unit_rows
    hits = jnp.zeros((24, 128), f32)
    for k in range(local_ref.shape[1]):
        hits = jnp.where(local_ref[:, k : k + 1] == tile_of, 1.0, hits)
    active = jnp.where(live, hits, 0.0)
    down = lax.broadcasted_iota(jnp.int32, (128, 128), 0)
    across = lax.broadcasted_iota(jnp.int32, (128, 128), 1)
    upto = jnp.where(down <= across, 1.0, 0.0).astype(bf16)
    rank = jnp.dot(active.astype(bf16), upto, preferred_element_type=f32)
    counts = jnp.broadcast_to(rank[:, 127:128], (24, 128))
    place = jnp.where(active > 0.0, rank - 1.0, -1.0)
    place = jnp.concatenate([place, jnp.full((104, 128), -1.0, f32)], axis=0).T
    position = across.astype(f32)
    value = (down - units).astype(f32)
    plan_ref[...] = jnp.full_like(plan_ref, units)
    last = lax.broadcasted_iota(jnp.int32, (1, 128), 1)
    chunks = jnp.floor((counts + (group - 0.5)) / group).astype(jnp.int32)
    begin = jnp.zeros((1, 128), jnp.int32)
    items = jnp.full((1, 128), src_tiles * per, jnp.int32)
    for s in range(src_tiles):
        listed = jnp.sum(
            jnp.where(place[:, s : s + 1] == position, value, 0.0), axis=0, keepdims=True
        )
        plan_ref[s : s + 1, :] = jnp.where(
            last == 127, counts[s : s + 1], listed + units
        ).astype(jnp.int32)
        along = last - begin
        inside = (along >= 0) & (along < chunks[s : s + 1])
        items = jnp.where(inside, s * per + along, items)
        begin = begin + chunks[s : s + 1]
    plan_ref[src_tiles + 1 : src_tiles + 2, :] = items
    row = lax.axis_index("row")
    apart = lax.axis_index("col") - row + 2 - lax.rem(row, 2) + 16
    near = jnp.where(lax.rem(apart, 16) < 4, 1, 0)
    plan_ref[src_tiles + 2 : src_tiles + 3, :] = begin * jnp.where(last == 0, near, 1 - near)


def pipeline(plan_ref, items, operand_ref, weights_ref, buffers, visit):
    tiles, depth, tile = weights_ref.shape
    per = (operand_ref.shape[0] // unit_rows - 1) // group

    def where(i):
        code = plan_ref[tiles + 1, i]
        s = code // per
        first = (code - s * per) * group
        return jnp.minimum(s, tiles - 1), [plan_ref[s, first + k] for k in range(group)]

    def step(j, carry):
        for k in range(span):
            s, units = where(span * j + k)
            rows = jnp.concatenate(
                [
                    operand_ref[pl.ds(pl.multiple_of(u * unit_rows, unit_rows), unit_rows), :]
                    for u in units
                ],
                axis=0,
            )
            buffers[k][...] = jnp.dot(rows, weights_ref[s], preferred_element_type=f32)
        for k in range(span):
            visit(*where(span * j + k), buffers[k])
        return carry

    lax.fori_loop(0, (items + span - 1) // span, step, 0)


def row_pass(
    which, plan_ref, points_ref, need_ref, w0, w1, w2, w3, lse_ref,
    operand_ref, weights_ref, total_ref, *buffers,
):
    tiles, depth, tile = weights_ref.shape
    items = plan_ref[tiles + 2, which]

    @pl.when(items == 0)
    def _():
        lse_ref[...] = jnp.full_like(lse_ref, nothing)

    @pl.when(items > 0)
    def _():
        load_all(points_ref, None, (w0, w1, w2, w3), operand_ref, weights_ref)
        total_ref[...] = jnp.zeros_like(total_ref)

        def visit(s, units, buffer):
            part = jnp.exp2(buffer[...]).reshape(4, unit_rows * group // 32, 8, tile)
            total_ref[s] += jnp.sum(jnp.sum(part, axis=1), axis=0)

        pipeline(plan_ref, items, operand_ref, weights_ref, buffers, visit)
        total = jnp.sum(total_ref[...], axis=1)
        lse_ref[...] = jnp.where(total > 0.0, jnp.log2(jnp.maximum(total, 1e-37)), nothing)
        fine = (total > 1e-25) & (total < 1e30)
        bad = jnp.where(fine, 0.0, need_ref[...])

        @pl.when(jnp.max(bad) > 0.0)
        def _():
            def one_tile(s, carry):
                weights = weights_ref[s]

                def step(i, state):
                    high, total = state
                    unit = plan_ref[s, i]
                    rows = operand_ref[
                        pl.ds(pl.multiple_of(unit * unit_rows, unit_rows), unit_rows), :
                    ]
                    score = jnp.dot(rows, weights, preferred_element_type=f32)
                    score = score.reshape(unit_rows // 8, 8, tile)
                    new = jnp.maximum(high, jnp.max(score, axis=0))
                    total = total * jnp.exp2(high - new)
                    return new, total + jnp.sum(jnp.exp2(score - new[None]), axis=0)

                start = (jnp.full((8, tile), floor, f32), jnp.zeros((8, tile), f32))
                high, total = lax.fori_loop(0, plan_ref[s, 127], step, start)
                top = jnp.max(high, axis=0, keepdims=True)
                total = jnp.sum(total * jnp.exp2(high - top), axis=0, keepdims=True)
                lse_ref[pl.ds(s, 1), :] = jnp.where(
                    total > 0.0, top + jnp.log2(jnp.maximum(total, 1e-37)), nothing
                )
                return carry

            lax.fori_loop(0, tiles, one_tile, 0)


def column_pass(
    which, plan_ref, points_ref, need_ref, w0, w1, w2, w3, lse_ref, mass_ref, other_ref, out_ref,
    operand_ref, weights_ref, total_ref, high_ref, *buffers,
):
    tiles, depth, tile = weights_ref.shape
    items = plan_ref[tiles + 2, which]

    @pl.when(items == 0)
    def _():
        out_ref[...] = other_ref[...]

    @pl.when(items > 0)
    def _():
        shift = mass_ref[...] - lse_ref[...]
        load_all(points_ref, shift, (w0, w1, w2, w3), operand_ref, weights_ref)
        total_ref[...] = jnp.zeros_like(total_ref)

        def visit(s, units, buffer):
            for k, u in enumerate(units):
                where = pl.ds(pl.multiple_of(u * unit_rows, unit_rows), unit_rows)
                part = jnp.exp2(buffer[k * unit_rows : (k + 1) * unit_rows, :])
                total_ref[where, :] += part[:, 0:128] + part[:, 128:256]

        pipeline(plan_ref, items, operand_ref, weights_ref, buffers, visit)
        eye = lax.broadcasted_iota(jnp.int32, (128, 128), 0) == lax.broadcasted_iota(
            jnp.int32, (128, 128), 1
        )

        def to_row(column):
            return jnp.sum(jnp.where(eye, column, 0.0), axis=0, keepdims=True)

        bad = jnp.zeros((1, 128), f32)
        for u in range(out_ref.shape[0]):
            sums = to_row(jnp.sum(total_ref[u * 128 : (u + 1) * 128, :], axis=1, keepdims=True))
            out_ref[u : u + 1, :] = jnp.where(
                sums > 0.0, jnp.log2(jnp.maximum(sums, 1e-37)), nothing
            )
            bad = jnp.maximum(bad, jnp.where(sums > 1e-25, 0.0, need_ref[u : u + 1, :]))

        @pl.when(jnp.max(bad) > 0.0)
        def _():
            total_ref[...] = jnp.zeros_like(total_ref)
            high_ref[...] = jnp.full_like(high_ref, floor)

            def one_tile(s, carry):
                def step(i, inner):
                    unit = plan_ref[s, i]
                    where = pl.ds(pl.multiple_of(unit * unit_rows, unit_rows), unit_rows)
                    score = jnp.dot(
                        operand_ref[where, :], weights_ref[s], preferred_element_type=f32
                    )
                    a, b = score[:, 0:128], score[:, 128:256]
                    old = high_ref[where, :]
                    new = jnp.maximum(old, jnp.maximum(a, b))
                    high_ref[where, :] = new
                    total_ref[where, :] = (
                        total_ref[where, :] * jnp.exp2(old - new)
                        + jnp.exp2(a - new)
                        + jnp.exp2(b - new)
                    )
                    return inner

                lax.fori_loop(0, plan_ref[s, 127], step, 0)
                return carry

            lax.fori_loop(0, tiles, one_tile, 0)

            def finish(u, carry):
                where = pl.ds(pl.multiple_of(u * 128, 128), 128)
                high = high_ref[where, :]
                top = jnp.max(high, axis=1, keepdims=True)
                rest = total_ref[where, :] * jnp.exp2(high - top)
                sums = to_row(jnp.sum(rest, axis=1, keepdims=True))
                out_ref[pl.ds(u, 1), :] = jnp.where(
                    sums > 0.0, to_row(top) + jnp.log2(jnp.maximum(sums, 1e-37)), nothing
                )
                return carry

            lax.fori_loop(0, out_ref.shape[0], finish, 0)


def log_sum(parts):
    top = functools.reduce(jnp.maximum, parts)
    total = sum(jnp.exp2(p - top) for p in parts)
    return top + jnp.log2(total)


def roles(parity, cols):
    four = [d % cols for d in ((-2, -1, 0, 1), (-1, 0, 1, 2))[parity]]
    lead = [0, (1, -1)[parity] % cols]
    near = lead + [d for d in four if d not in lead]
    out = [(2, -2)[parity] % cols, cols // 2]
    begin = four[0]
    out += [(begin + 5) % cols, (begin + 6) % cols]
    return near, out + [d for d in range(cols) if d not in near and d not in out]


def filled(hops, count, cols):
    found = dict(hops)
    back = {d: s for s, d in hops}
    for rank in range(4):
        free = [d for d in range(count) if d not in back]
        for s in [s for s in range(count) if s not in found]:
            if rank == 0:
                picks = [back[s]] if s in back and back[s] in free else []
            elif rank == 1:
                picks = [s ^ 1] if s ^ 1 in free else []
            else:
                picks = [d for d in free if d != s and (d // cols == s // cols or rank == 3)]
                picks.sort(key=lambda d: min((d - s) % cols, (s - d) % cols))
            if picks:
                found[s] = picks[0]
                back[picks[0]] = s
                free.remove(picks[0])
    return sorted(found.items())


def shards(src_points, dst_points, dst_potential, partners, partner_count, src_count, dst_count):
    src_tiles = src_count.shape[0]
    dst_tiles = dst_count.shape[0]
    tile = src_points.shape[0] // src_tiles
    slots = partners.shape[1]
    rows = lax.axis_size("row")
    cols = lax.axis_size("col")
    row_here = lax.axis_index("row")
    col_here = lax.axis_index("col")
    share = dst_points.shape[0]
    points = dst_tiles * tile
    smem = pl.BlockSpec(memory_space=pltpu.SMEM)
    vmem = pl.BlockSpec(memory_space=pltpu.VMEM)
    anywhere = pl.BlockSpec(memory_space=pl.ANY)
    params = pltpu.CompilerParams(vmem_limit_bytes=24 * 1024 * 1024)
    places = [roles(r % 2, cols) for r in range(rows)]
    near = [[(r + d) % cols for d in places[r][0]] for r in range(rows)]
    far = [[(r + d) % cols for d in places[r][1]] for r in range(rows)]
    parity = lax.rem(row_here, 2)
    apart = lax.rem(col_here - row_here + 2 - parity + cols, cols)
    in_near = apart < 4
    in_far = (
        (apart == 5)
        | (apart == 6)
        | (apart == jnp.where(parity == 0, 4, cols - 1))
        | (apart == jnp.where(parity == 0, 10, 9))
    )

    def send(a, hops, full=True):
        hops = [(s[0] * cols + s[1], d[0] * cols + d[1]) for s, d in hops]
        return lax.ppermute(a, ("row", "col"), filled(hops, rows * cols, cols) if full else hops)

    every = [(r, c) for r in range(rows) for c in range(cols)]

    wire = pl.pallas_call(
        pack_targets,
        out_shape=jax.ShapeDtypeStruct((share // 2 + 8, 128), f32),
        in_specs=[anywhere] * 3,
        out_specs=vmem,
        scratch_shapes=[
            pltpu.VMEM((128, 384), f32),
            pltpu.VMEM((8, 384), f32),
            pltpu.SMEM((dst_tiles,), jnp.int32),
            pltpu.VMEM((64, share), f32),
            pltpu.VMEM((share,), f32),
            pltpu.SemaphoreType.DMA((3,)),
        ],
        compiler_params=pltpu.CompilerParams(vmem_limit_bytes=60 * 1024 * 1024),
    )(dst_count, dst_points.T, dst_potential)

    def around(r, dx, dy):
        return (r // ring + dx) % ring * ring + (r + dy) % ring

    def first_hop(r, c, k):
        return around(r, 0, k) if c % 2 == 0 else around(r, k, 0)

    def second_hop(r, c, k):
        return around(r, k, 0) if c % 2 == 0 else around(r, 0, k)

    bundle = jnp.stack(
        [wire]
        + [send(wire, [((r, c), (first_hop(r, c, k), c)) for r, c in every]) for k in (1, 2, 3)]
    )
    busy = [set(near[r] + far[r][:2]) for r in range(rows)]
    slot_on = jnp.arange(slots, dtype=jnp.int32)[None, :] < partner_count[:, None]
    local = jnp.where(slot_on, partners - col_here * dst_tiles, -1)
    plan = pl.pallas_call(
        plan_work,
        out_shape=jax.ShapeDtypeStruct((24, 128), jnp.int32),
        in_specs=[smem, vmem],
        out_specs=vmem,
        compiler_params=params,
    )(dst_count, jnp.pad(local, ((0, 24 - src_tiles), (0, 0)), constant_values=-1))
    plan, local, dst_count, src_count, bundle = lax.optimization_barrier(
        (plan, local, dst_count, src_count, bundle)
    )
    wires = [bundle] + [
        send(
            bundle,
            [
                ((r, c), (second_hop(r, c, k), c))
                for r, c in every
                if c in busy[second_hop(r, c, k)]
            ],
            full=False,
        )
        for k in (1, 2, 3)
    ]
    place = jnp.arange(tile, dtype=jnp.int32)
    src_live = place[None, :] < src_count[:, None]
    dst_live = place[None, :] < dst_count[:, None]
    wanted = jnp.any(local[:, :, None] == jnp.arange(dst_tiles, dtype=jnp.int32), axis=1)
    src_need = jnp.where(src_live & jnp.any(wanted, axis=1)[:, None], 1.0, 0.0)
    dst_need = jnp.where(dst_live & jnp.any(wanted, axis=0)[:, None], 1.0, 0.0)
    dst_need = dst_need.reshape(points // 128, 128)
    counted = src_count.astype(f32)
    all_src = src_tiles * rows
    mass = jnp.where(src_live, -jnp.log2(counted)[:, None] - math.log2(all_src), nothing)

    scratch = [
        pltpu.VMEM((points + unit_rows, 256), bf16),
        pltpu.VMEM((src_tiles, 256, tile), bf16),
    ]
    buffers = [pltpu.VMEM((unit_rows * group, tile), f32)] * span
    heavy = pl.CostEstimate(flops=8_000_000_000, bytes_accessed=4_000_000, transcendentals=8_000_000)
    light = pl.CostEstimate(flops=100_000_000, bytes_accessed=100_000, transcendentals=100_000)
    turned = src_points.T

    def sum_rows(which, cost):
        return pl.pallas_call(
            functools.partial(row_pass, which),
            out_shape=jax.ShapeDtypeStruct((src_tiles, tile), f32),
            in_specs=[smem] + [vmem] * (2 + ring),
            out_specs=vmem,
            scratch_shapes=scratch + [pltpu.VMEM((src_tiles, 8, tile), f32)] + buffers,
            compiler_params=params,
            cost_estimate=cost,
        )(plan, turned, src_need, *wires)

    def sum_columns(which, lse, other, cost):
        return pl.pallas_call(
            functools.partial(column_pass, which),
            out_shape=jax.ShapeDtypeStruct((points // 128, 128), f32),
            in_specs=[smem] + [vmem] * (5 + ring),
            out_specs=vmem,
            scratch_shapes=scratch + [pltpu.VMEM((points + unit_rows, 128), f32)] * 2 + buffers,
            compiler_params=params,
            cost_estimate=cost,
        )(plan, turned, dst_need, *wires, lse, mass, other)

    far_lse = sum_rows(1, light)
    early = send(
        far_lse,
        [((r, far[r][k]), (r, near[r][k])) for r in range(rows) for k in (0, 1)],
        full=False,
    )
    near_lse = sum_rows(0, heavy)
    got_early = (col_here == row_here) | (col_here == row_here + 1 - 2 * parity)
    lse = log_sum([near_lse, jnp.where(got_early, early, nothing)])

    def pairs(test):
        return [((r, c), (r, d)) for r in range(rows) for c in near[r] for d in near[r] if test(c, d)]

    lse = log_sum(
        [
            lse,
            send(lse, [((r, c), (r, c ^ 1)) for r, c in every]),
            send(lse, pairs(lambda c, d: (c - d) % cols in (2, cols - 2))),
            send(lse, pairs(lambda c, d: (c - (d ^ 1)) % cols in (2, cols - 2))),
        ]
    )
    spread = send(lse, [((r, near[r][k]), (r, far[r][k])) for r in range(rows) for k in range(4)])
    blank = jnp.full((points // 128, 128), nothing, f32)
    near_part = sum_columns(0, lse, blank, heavy)
    col_part = sum_columns(1, spread, near_part, light)
    known = jnp.where(in_far, spread, lse)
    known, near_part = lax.optimization_barrier((known, near_part))
    rest = send(
        known,
        [((r, (near[r] + far[r])[k]), (r, far[r][4 + k])) for r in range(rows) for k in range(8)],
    )
    shared_out = lax.all_to_all(col_part.reshape(rows, share), "row", 0, 0)

    row_lse = jnp.where(in_near | in_far, known, rest)
    src_potential = jnp.where(
        src_live,
        entropy * (-jnp.log(counted)[:, None] - math.log(all_src) - ln2 * row_lse),
        0.0,
    ).reshape(-1)

    spot = row_here * share + jnp.arange(share, dtype=jnp.int32)
    spot_tile = spot // tile
    spot_count = jnp.sum(
        jnp.where(
            spot_tile[:, None] == jnp.arange(dst_tiles, dtype=jnp.int32)[None, :],
            dst_count[None, :],
            0,
        ),
        axis=1,
    )
    top = jnp.max(shared_out, axis=0)
    col_log = top + jnp.log2(jnp.sum(jnp.exp2(shared_out - top[None]), axis=0))
    dst_new = jnp.where(
        (spot - spot_tile * tile < spot_count) & (top > 0.5 * nothing),
        entropy
        * (-jnp.log(spot_count.astype(f32)) - math.log(dst_tiles * cols) - ln2 * col_log)
        + dst_potential,
        0.0,
    )
    return src_potential, dst_new


def solution(mesh):
    in_specs = (
        P("row", None),
        P(("col", "row"), None),
        P(("col", "row")),
        P("row", None),
        P("row"),
        P("row"),
        P("col"),
    )
    out_specs = (P("row"), P(("col", "row")))
    return jax.shard_map(shards, mesh=mesh, in_specs=in_specs, out_specs=out_specs, check_vma=False)
```

```python
import functools
import math

import jax
import jax.numpy as jnp
from jax import lax
from jax.experimental import pallas as pl
from jax.experimental.pallas import tpu as pltpu
from jax.sharding import PartitionSpec as P

entropy = 0.1
scale = math.log2(math.e) / entropy
ln2 = math.log(2.0)
nothing = -1e30
floor = -1e25
unit_rows = 64
group = 12
span = 8
f32 = jnp.float32
bf16 = jnp.bfloat16


def pieces(a):
    first = a.astype(bf16).astype(f32)
    rest = a - first
    second = rest.astype(bf16).astype(f32)
    return first, second, rest - second


def extra_rows(bias):
    place = lax.broadcasted_iota(jnp.int32, (64, bias.shape[1]), 0)
    block = jnp.where(place < 3, 1.0, 0.0)
    for k, piece in enumerate(pieces(bias)):
        block = jnp.where(place == 3 + k, piece, block)
    return block.astype(bf16)


def pack_targets(
    count_ref, points_ref, potential_ref, wire_ref, square_ref, line_ref, tally_ref, held_ref, level_ref, sems,
):
    copies = [
        pltpu.make_async_copy(source, target, sems.at[k])
        for k, (source, target) in enumerate(
            ((points_ref, held_ref), (potential_ref, level_ref), (count_ref, tally_ref))
        )
    ]
    for copy in copies:
        copy.start()
    share = held_ref.shape[1]
    tile = 256
    mid = share // 2
    begin = lax.axis_index("row") * share
    first_tile = begin // tile
    offset = begin - first_tile * tile
    last_tile = jnp.minimum(first_tile + 1, tally_ref.shape[0] - 1)
    square_ref[...] = jnp.zeros_like(square_ref)
    line_ref[...] = jnp.full_like(line_ref, nothing)
    for copy in copies:
        copy.wait()
    points = held_ref[...]
    square_ref[0:64, 0:share] = points
    turned = square_ref[...].T
    packed = scale * (turned[0:mid] + pltpu.roll(turned[mid:share], 64, 1))
    level = level_ref[...].reshape(1, share)
    level = scale * (level - 0.5 * jnp.sum(points * points, axis=0, keepdims=True))
    spot = offset + lax.broadcasted_iota(jnp.int32, (1, share), 1)
    place = jnp.where(spot < tile, spot, spot - tile)
    bound = jnp.where(spot < tile, tally_ref[first_tile], tally_ref[last_tile])
    line_ref[0:1, 0:share] = jnp.where(place < bound, level, nothing)
    lines = [line_ref[0:1, 128 * k : 128 * (k + 1)] for k in range(3)]
    tail = jnp.concatenate(lines + [jnp.zeros((5, 128), f32)], axis=0)
    for r in range(wire_ref.shape[0]):
        wire_ref[r, 0:mid, :] = packed
        wire_ref[r, mid : mid + 8, :] = tail


def unpack_targets(held_ref, operand_ref):
    lane = lax.broadcasted_iota(jnp.int32, (144, 128), 1)
    front = lane < 64
    sublane = lax.broadcasted_iota(jnp.int32, (16, 384), 0)
    pick_row = lax.broadcasted_iota(jnp.int32, (16, 128), 0)
    pick_lane = lax.broadcasted_iota(jnp.int32, (16, 128), 1)
    pick = jnp.where((pick_lane == pick_row + 64) & (pick_row < 6), 1.0, 0.0).astype(bf16)
    for m in range(held_ref.shape[0]):
        a, b, c = m * 288, m * 288 + 144, m * 288 + 288
        both = held_ref[m, 0:144, :]
        high = both.astype(bf16).astype(f32)
        low = both - high
        high_back = pltpu.roll(high, 64, 1)
        low_back = pltpu.roll(low, 64, 1)
        tail = held_ref[m, 144:152, :]
        line = jnp.concatenate([tail[0:1], tail[1:2], tail[2:3]], axis=1)
        stacked = jnp.where(sublane < 6, 1.0, 0.0)
        for i, piece in enumerate(pieces(line)):
            stacked = jnp.where(sublane == i, piece, stacked)
        extra = lax.dot_general(
            stacked.astype(bf16), pick, (((0,), (0,)), ((), ())), preferred_element_type=f32
        )
        operand_ref[a:b, 0:128] = jnp.where(front, high, low_back).astype(bf16)
        operand_ref[a:b, 128:256] = jnp.where(front, high, extra[0:144]).astype(bf16)
        operand_ref[b:c, 0:128] = jnp.where(front, high_back, low).astype(bf16)
        operand_ref[b:c, 128:256] = jnp.where(front, high_back, extra[144:288]).astype(bf16)
    rows = held_ref.shape[0] * 288
    dummy_lane = lax.broadcasted_iota(jnp.int32, (unit_rows, 256), 1)
    operand_ref[rows : rows + unit_rows, :] = jnp.where(dummy_lane == 192, nothing, 0.0).astype(bf16)


def load_weights(points_ref, weights_ref, shift):
    tiles, depth, tile = weights_ref.shape
    for s in range(tiles):
        x = points_ref[:, s * tile : (s + 1) * tile]
        high = x.astype(bf16)
        low = (x - high.astype(f32)).astype(bf16)
        bias = (-0.5 * scale) * jnp.sum(x * x, axis=0, keepdims=True)
        weights_ref[s, 0:64, :] = high
        weights_ref[s, 64:128, :] = high
        weights_ref[s, 128:192, :] = low
        weights_ref[s, 192:256, :] = extra_rows(bias if shift is None else bias + shift[s : s + 1, :])


def load_all(points_ref, shift, wire_ref, held_ref, sem, operand_ref, weights_ref):
    copy = pltpu.make_async_copy(wire_ref, held_ref, sem)
    copy.start()
    load_weights(points_ref, weights_ref, shift)
    copy.wait()
    unpack_targets(held_ref, operand_ref)


def plan_work(count_ref, local_ref, plan_ref):
    src_tiles = local_ref.shape[0] - 6
    per_tile = 256 // unit_rows
    units = count_ref.shape[0] * per_tile
    per = units // group
    unit = lax.broadcasted_iota(jnp.int32, (24, 128), 1)
    tile_of = unit // per_tile
    bound = jnp.zeros((24, 128), jnp.int32)
    for t in range(count_ref.shape[0]):
        bound = jnp.where(tile_of == t, count_ref[t], bound)
    live = bound > (unit - tile_of * per_tile) * unit_rows
    hits = jnp.zeros((24, 128), f32)
    for k in range(local_ref.shape[1]):
        hits = jnp.where(local_ref[:, k : k + 1] == tile_of, 1.0, hits)
    active = jnp.where(live, hits, 0.0)
    down = lax.broadcasted_iota(jnp.int32, (128, 128), 0)
    across = lax.broadcasted_iota(jnp.int32, (128, 128), 1)
    upto = jnp.where(down <= across, 1.0, 0.0).astype(bf16)
    rank = jnp.dot(active.astype(bf16), upto, preferred_element_type=f32)
    counts = jnp.broadcast_to(rank[:, 127:128], (24, 128))
    place = jnp.where(active > 0.0, rank - 1.0, -1.0)
    place = jnp.concatenate([place, jnp.full((104, 128), -1.0, f32)], axis=0).T
    position = across.astype(f32)
    value = (down - units).astype(f32)
    plan_ref[...] = jnp.full_like(plan_ref, units)
    last = lax.broadcasted_iota(jnp.int32, (1, 128), 1)
    chunks = jnp.floor((counts + (group - 0.5)) / group).astype(jnp.int32)
    begin = jnp.zeros((1, 128), jnp.int32)
    items = jnp.full((1, 128), src_tiles * per, jnp.int32)
    for s in range(src_tiles):
        listed = jnp.sum(
            jnp.where(place[:, s : s + 1] == position, value, 0.0), axis=0, keepdims=True
        )
        plan_ref[s : s + 1, :] = jnp.where(
            last == 127, counts[s : s + 1], listed + units
        ).astype(jnp.int32)
        along = last - begin
        inside = (along >= 0) & (along < chunks[s : s + 1])
        items = jnp.where(inside, s * per + along, items)
        begin = begin + chunks[s : s + 1]
    plan_ref[src_tiles + 1 : src_tiles + 2, :] = items
    row = lax.axis_index("row")
    apart = lax.axis_index("col") - row + 2 - lax.rem(row, 2) + 16
    near = jnp.where(lax.rem(apart, 16) < 4, 1, 0)
    plan_ref[src_tiles + 2 : src_tiles + 3, :] = begin * jnp.where(last == 0, near, 1 - near)


def pipeline(plan_ref, items, operand_ref, weights_ref, buffers, visit):
    tiles, depth, tile = weights_ref.shape
    per = (operand_ref.shape[0] // unit_rows - 1) // group

    def where(i):
        code = plan_ref[tiles + 1, i]
        s = code // per
        first = (code - s * per) * group
        return jnp.minimum(s, tiles - 1), [plan_ref[s, first + k] for k in range(group)]

    def step(j, carry):
        for k in range(span):
            s, units = where(span * j + k)
            rows = jnp.concatenate(
                [
                    operand_ref[pl.ds(pl.multiple_of(u * unit_rows, unit_rows), unit_rows), :]
                    for u in units
                ],
                axis=0,
            )
            buffers[k][...] = jnp.dot(rows, weights_ref[s], preferred_element_type=f32)
        for k in range(span):
            visit(*where(span * j + k), buffers[k])
        return carry

    lax.fori_loop(0, (items + span - 1) // span, step, 0)


def row_pass(
    which, plan_ref, points_ref, need_ref, wire_ref, lse_ref,
    held_ref, sem, operand_ref, weights_ref, total_ref, *buffers,
):
    tiles, depth, tile = weights_ref.shape
    items = plan_ref[tiles + 2, which]

    @pl.when(items == 0)
    def _():
        lse_ref[...] = jnp.full_like(lse_ref, nothing)

    @pl.when(items > 0)
    def _():
        load_all(points_ref, None, wire_ref, held_ref, sem, operand_ref, weights_ref)
        total_ref[...] = jnp.zeros_like(total_ref)

        def visit(s, units, buffer):
            part = jnp.exp2(buffer[...]).reshape(4, unit_rows * group // 32, 8, tile)
            total_ref[s] += jnp.sum(jnp.sum(part, axis=1), axis=0)

        pipeline(plan_ref, items, operand_ref, weights_ref, buffers, visit)
        total = jnp.sum(total_ref[...], axis=1)
        lse_ref[...] = jnp.where(total > 0.0, jnp.log2(jnp.maximum(total, 1e-37)), nothing)
        fine = (total > 1e-25) & (total < 1e30)
        bad = jnp.where(fine, 0.0, need_ref[...])

        @pl.when(jnp.max(bad) > 0.0)
        def _():
            def one_tile(s, carry):
                weights = weights_ref[s]

                def step(i, state):
                    high, total = state
                    unit = plan_ref[s, i]
                    rows = operand_ref[
                        pl.ds(pl.multiple_of(unit * unit_rows, unit_rows), unit_rows), :
                    ]
                    score = jnp.dot(rows, weights, preferred_element_type=f32)
                    score = score.reshape(unit_rows // 8, 8, tile)
                    new = jnp.maximum(high, jnp.max(score, axis=0))
                    total = total * jnp.exp2(high - new)
                    return new, total + jnp.sum(jnp.exp2(score - new[None]), axis=0)

                start = (jnp.full((8, tile), floor, f32), jnp.zeros((8, tile), f32))
                high, total = lax.fori_loop(0, plan_ref[s, 127], step, start)
                top = jnp.max(high, axis=0, keepdims=True)
                total = jnp.sum(total * jnp.exp2(high - top), axis=0, keepdims=True)
                lse_ref[pl.ds(s, 1), :] = jnp.where(
                    total > 0.0, top + jnp.log2(jnp.maximum(total, 1e-37)), nothing
                )
                return carry

            lax.fori_loop(0, tiles, one_tile, 0)


def column_pass(
    which, plan_ref, points_ref, need_ref, wire_ref, lse_ref, mass_ref, other_ref, out_ref,
    held_ref, sem, operand_ref, weights_ref, total_ref, high_ref, *buffers,
):
    tiles, depth, tile = weights_ref.shape
    items = plan_ref[tiles + 2, which]

    @pl.when(items == 0)
    def _():
        out_ref[...] = other_ref[...]

    @pl.when(items > 0)
    def _():
        shift = mass_ref[...] - lse_ref[...]
        load_all(points_ref, shift, wire_ref, held_ref, sem, operand_ref, weights_ref)
        total_ref[...] = jnp.zeros_like(total_ref)

        def visit(s, units, buffer):
            for k, u in enumerate(units):
                where = pl.ds(pl.multiple_of(u * unit_rows, unit_rows), unit_rows)
                part = jnp.exp2(buffer[k * unit_rows : (k + 1) * unit_rows, :])
                total_ref[where, :] += part[:, 0:128] + part[:, 128:256]

        pipeline(plan_ref, items, operand_ref, weights_ref, buffers, visit)
        eye = lax.broadcasted_iota(jnp.int32, (128, 128), 0) == lax.broadcasted_iota(
            jnp.int32, (128, 128), 1
        )

        def to_row(column):
            return jnp.sum(jnp.where(eye, column, 0.0), axis=0, keepdims=True)

        bad = jnp.zeros((1, 128), f32)
        for u in range(out_ref.shape[0]):
            sums = to_row(jnp.sum(total_ref[u * 128 : (u + 1) * 128, :], axis=1, keepdims=True))
            out_ref[u : u + 1, :] = jnp.where(
                sums > 0.0, jnp.log2(jnp.maximum(sums, 1e-37)), nothing
            )
            bad = jnp.maximum(bad, jnp.where(sums > 1e-25, 0.0, need_ref[u : u + 1, :]))

        @pl.when(jnp.max(bad) > 0.0)
        def _():
            total_ref[...] = jnp.zeros_like(total_ref)
            high_ref[...] = jnp.full_like(high_ref, floor)

            def one_tile(s, carry):
                def step(i, inner):
                    unit = plan_ref[s, i]
                    where = pl.ds(pl.multiple_of(unit * unit_rows, unit_rows), unit_rows)
                    score = jnp.dot(
                        operand_ref[where, :], weights_ref[s], preferred_element_type=f32
                    )
                    a, b = score[:, 0:128], score[:, 128:256]
                    old = high_ref[where, :]
                    new = jnp.maximum(old, jnp.maximum(a, b))
                    high_ref[where, :] = new
                    total_ref[where, :] = (
                        total_ref[where, :] * jnp.exp2(old - new)
                        + jnp.exp2(a - new)
                        + jnp.exp2(b - new)
                    )
                    return inner

                lax.fori_loop(0, plan_ref[s, 127], step, 0)
                return carry

            lax.fori_loop(0, tiles, one_tile, 0)

            def finish(u, carry):
                where = pl.ds(pl.multiple_of(u * 128, 128), 128)
                high = high_ref[where, :]
                top = jnp.max(high, axis=1, keepdims=True)
                rest = total_ref[where, :] * jnp.exp2(high - top)
                sums = to_row(jnp.sum(rest, axis=1, keepdims=True))
                out_ref[pl.ds(u, 1), :] = jnp.where(
                    sums > 0.0, to_row(top) + jnp.log2(jnp.maximum(sums, 1e-37)), nothing
                )
                return carry

            lax.fori_loop(0, out_ref.shape[0], finish, 0)


def log_sum(parts):
    top = functools.reduce(jnp.maximum, parts)
    total = sum(jnp.exp2(p - top) for p in parts)
    return top + jnp.log2(total)


def roles(parity, cols):
    four = [d % cols for d in ((-2, -1, 0, 1), (-1, 0, 1, 2))[parity]]
    lead = [0, (1, -1)[parity] % cols]
    near = lead + [d for d in four if d not in lead]
    out = [(2, -2)[parity] % cols, cols // 2]
    begin = four[0]
    out += [(begin + 5) % cols, (begin + 6) % cols]
    return near, out + [d for d in range(cols) if d not in near and d not in out]


def filled(hops, count, cols):
    found = dict(hops)
    back = {d: s for s, d in hops}
    for rank in range(4):
        free = [d for d in range(count) if d not in back]
        for s in [s for s in range(count) if s not in found]:
            if rank == 0:
                picks = [back[s]] if s in back and back[s] in free else []
            elif rank == 1:
                picks = [s ^ 1] if s ^ 1 in free else []
            else:
                picks = [d for d in free if d != s and (d // cols == s // cols or rank == 3)]
                picks.sort(key=lambda d: min((d - s) % cols, (s - d) % cols))
            if picks:
                found[s] = picks[0]
                back[picks[0]] = s
                free.remove(picks[0])
    return sorted(found.items())


def shards(src_points, dst_points, dst_potential, partners, partner_count, src_count, dst_count):
    src_tiles = src_count.shape[0]
    dst_tiles = dst_count.shape[0]
    tile = src_points.shape[0] // src_tiles
    slots = partners.shape[1]
    rows = lax.axis_size("row")
    cols = lax.axis_size("col")
    row_here = lax.axis_index("row")
    col_here = lax.axis_index("col")
    share = dst_points.shape[0]
    points = dst_tiles * tile
    smem = pl.BlockSpec(memory_space=pltpu.SMEM)
    vmem = pl.BlockSpec(memory_space=pltpu.VMEM)
    anywhere = pl.BlockSpec(memory_space=pl.ANY)
    params = pltpu.CompilerParams(vmem_limit_bytes=24 * 1024 * 1024)
    places = [roles(r % 2, cols) for r in range(rows)]
    near = [[(r + d) % cols for d in places[r][0]] for r in range(rows)]
    far = [[(r + d) % cols for d in places[r][1]] for r in range(rows)]
    parity = lax.rem(row_here, 2)
    apart = lax.rem(col_here - row_here + 2 - parity + cols, cols)
    in_near = apart < 4
    in_far = (
        (apart == 5)
        | (apart == 6)
        | (apart == jnp.where(parity == 0, 4, cols - 1))
        | (apart == jnp.where(parity == 0, 10, 9))
    )

    def send(a, hops, full=True):
        hops = [(s[0] * cols + s[1], d[0] * cols + d[1]) for s, d in hops]
        return lax.ppermute(a, ("row", "col"), filled(hops, rows * cols, cols) if full else hops)

    every = [(r, c) for r in range(rows) for c in range(cols)]

    wire = pl.pallas_call(
        pack_targets,
        out_shape=jax.ShapeDtypeStruct((rows, share // 2 + 8, 128), f32),
        in_specs=[anywhere] * 3,
        out_specs=vmem,
        scratch_shapes=[
            pltpu.VMEM((128, 384), f32),
            pltpu.VMEM((8, 384), f32),
            pltpu.SMEM((dst_tiles,), jnp.int32),
            pltpu.VMEM((64, share), f32),
            pltpu.VMEM((share,), f32),
            pltpu.SemaphoreType.DMA((3,)),
        ],
        compiler_params=pltpu.CompilerParams(vmem_limit_bytes=60 * 1024 * 1024),
    )(dst_count, dst_points.T, dst_potential)

    wire, partners, partner_count, src_count, dst_count = lax.optimization_barrier(
        (wire, partners, partner_count, src_count, dst_count)
    )
    gathered = lax.all_to_all(wire, "row", 0, 0)
    slot_on = jnp.arange(slots, dtype=jnp.int32)[None, :] < partner_count[:, None]
    local = jnp.where(slot_on, partners - col_here * dst_tiles, -1)
    plan = pl.pallas_call(
        plan_work,
        out_shape=jax.ShapeDtypeStruct((24, 128), jnp.int32),
        in_specs=[smem, vmem],
        out_specs=vmem,
        compiler_params=params,
    )(dst_count, jnp.pad(local, ((0, 24 - src_tiles), (0, 0)), constant_values=-1))
    place = jnp.arange(tile, dtype=jnp.int32)
    src_live = place[None, :] < src_count[:, None]
    dst_live = place[None, :] < dst_count[:, None]
    wanted = jnp.any(local[:, :, None] == jnp.arange(dst_tiles, dtype=jnp.int32), axis=1)
    src_need = jnp.where(src_live & jnp.any(wanted, axis=1)[:, None], 1.0, 0.0)
    dst_need = jnp.where(dst_live & jnp.any(wanted, axis=0)[:, None], 1.0, 0.0)
    dst_need = dst_need.reshape(points // 128, 128)
    counted = src_count.astype(f32)
    all_src = src_tiles * rows
    mass = jnp.where(src_live, -jnp.log2(counted)[:, None] - math.log2(all_src), nothing)

    scratch = [
        pltpu.VMEM(wire.shape, f32),
        pltpu.SemaphoreType.DMA,
        pltpu.VMEM((points + unit_rows, 256), bf16),
        pltpu.VMEM((src_tiles, 256, tile), bf16),
    ]
    buffers = [pltpu.VMEM((unit_rows * group, tile), f32)] * span
    heavy = pl.CostEstimate(flops=8_000_000_000, bytes_accessed=4_000_000, transcendentals=8_000_000)
    light = pl.CostEstimate(flops=100_000_000, bytes_accessed=100_000, transcendentals=100_000)
    turned = src_points.T

    def sum_rows(which, cost):
        return pl.pallas_call(
            functools.partial(row_pass, which),
            out_shape=jax.ShapeDtypeStruct((src_tiles, tile), f32),
            in_specs=[smem, vmem, vmem, anywhere],
            out_specs=vmem,
            scratch_shapes=scratch + [pltpu.VMEM((src_tiles, 8, tile), f32)] + buffers,
            compiler_params=params,
            cost_estimate=cost,
        )(plan, turned, src_need, gathered)

    def sum_columns(which, lse, other, cost):
        return pl.pallas_call(
            functools.partial(column_pass, which),
            out_shape=jax.ShapeDtypeStruct((points // 128, 128), f32),
            in_specs=[smem, vmem, vmem, anywhere, vmem, vmem, vmem],
            out_specs=vmem,
            scratch_shapes=scratch + [pltpu.VMEM((points + unit_rows, 128), f32)] * 2 + buffers,
            compiler_params=params,
            cost_estimate=cost,
        )(plan, turned, dst_need, gathered, lse, mass, other)

    far_lse = sum_rows(1, light)
    early = send(
        far_lse,
        [((r, far[r][k]), (r, near[r][k])) for r in range(rows) for k in (0, 1)],
        full=False,
    )
    near_lse = sum_rows(0, heavy)
    got_early = (col_here == row_here) | (col_here == row_here + 1 - 2 * parity)
    lse = log_sum([near_lse, jnp.where(got_early, early, nothing)])

    def pairs(test):
        return [((r, c), (r, d)) for r in range(rows) for c in near[r] for d in near[r] if test(c, d)]

    lse = log_sum(
        [
            lse,
            send(lse, [((r, c), (r, c ^ 1)) for r, c in every]),
            send(lse, pairs(lambda c, d: (c - d) % cols in (2, cols - 2))),
            send(lse, pairs(lambda c, d: (c - (d ^ 1)) % cols in (2, cols - 2))),
        ]
    )
    spread = send(lse, [((r, near[r][k]), (r, far[r][k])) for r in range(rows) for k in range(4)])
    blank = jnp.full((points // 128, 128), nothing, f32)
    near_part = sum_columns(0, lse, blank, heavy)
    col_part = sum_columns(1, spread, near_part, light)
    known = jnp.where(in_far, spread, lse)
    known, near_part = lax.optimization_barrier((known, near_part))
    rest = send(
        known,
        [((r, (near[r] + far[r])[k]), (r, far[r][4 + k])) for r in range(rows) for k in range(8)],
    )
    shared_out = lax.all_to_all(col_part.reshape(rows, share), "row", 0, 0)

    row_lse = jnp.where(in_near | in_far, known, rest)
    src_potential = jnp.where(
        src_live,
        entropy * (-jnp.log(counted)[:, None] - math.log(all_src) - ln2 * row_lse),
        0.0,
    ).reshape(-1)

    src_potential, shared_out = lax.optimization_barrier((src_potential, shared_out))

    spot = row_here * share + jnp.arange(share, dtype=jnp.int32)
    spot_tile = spot // tile
    spot_count = jnp.sum(
        jnp.where(
            spot_tile[:, None] == jnp.arange(dst_tiles, dtype=jnp.int32)[None, :],
            dst_count[None, :],
            0,
        ),
        axis=1,
    )
    top = jnp.max(shared_out, axis=0)
    col_log = top + jnp.log2(jnp.sum(jnp.exp2(shared_out - top[None]), axis=0))
    dst_new = jnp.where(
        (spot - spot_tile * tile < spot_count) & (top > 0.5 * nothing),
        entropy
        * (-jnp.log(spot_count.astype(f32)) - math.log(dst_tiles * cols) - ln2 * col_log)
        + dst_potential,
        0.0,
    )
    return src_potential, dst_new


def solution(mesh):
    in_specs = (
        P("row", None),
        P(("col", "row"), None),
        P(("col", "row")),
        P("row", None),
        P("row"),
        P("row"),
        P("col"),
    )
    out_specs = (P("row"), P(("col", "row")))
    return jax.shard_map(shards, mesh=mesh, in_specs=in_specs, out_specs=out_specs, check_vma=False)
```

```python
import functools
import math

import jax
import jax.numpy as jnp
from jax import lax
from jax.experimental import pallas as pl
from jax.experimental.pallas import tpu as pltpu
from jax.sharding import PartitionSpec as P

entropy = 0.1
scale = math.log2(math.e) / entropy
ln2 = math.log(2.0)
nothing = -1e30
floor = -1e25
unit_rows = 64
group = 9
span = 10
ring = 4
f32 = jnp.float32
bf16 = jnp.bfloat16


def pieces(a):
    first = a.astype(bf16).astype(f32)
    rest = a - first
    second = rest.astype(bf16).astype(f32)
    return first, second, rest - second


def extra_rows(bias):
    place = lax.broadcasted_iota(jnp.int32, (64, bias.shape[1]), 0)
    block = jnp.where(place < 3, 1.0, 0.0)
    for k, piece in enumerate(pieces(bias)):
        block = jnp.where(place == 3 + k, piece, block)
    return block.astype(bf16)


def pack_targets(
    count_ref, points_ref, potential_ref, wire_ref, square_ref, line_ref, tally_ref, held_ref, level_ref, sems,
):
    copies = [
        pltpu.make_async_copy(source, target, sems.at[k])
        for k, (source, target) in enumerate(
            ((points_ref, held_ref), (potential_ref, level_ref), (count_ref, tally_ref))
        )
    ]
    for copy in copies:
        copy.start()
    share = held_ref.shape[1]
    tile = 256
    mid = share // 2
    begin = lax.axis_index("row") * share
    first_tile = begin // tile
    offset = begin - first_tile * tile
    last_tile = jnp.minimum(first_tile + 1, tally_ref.shape[0] - 1)
    square_ref[...] = jnp.zeros_like(square_ref)
    line_ref[...] = jnp.full_like(line_ref, nothing)
    wire_ref[mid : mid + 8, :] = jnp.zeros((8, 128), f32)
    for copy in copies:
        copy.wait()
    points = held_ref[...]
    square_ref[0:64, 0:share] = points
    turned = square_ref[...].T
    wire_ref[0:mid, :] = scale * (turned[0:mid] + pltpu.roll(turned[mid:share], 64, 1))
    level = level_ref[...].reshape(1, share)
    level = scale * (level - 0.5 * jnp.sum(points * points, axis=0, keepdims=True))
    spot = offset + lax.broadcasted_iota(jnp.int32, (1, share), 1)
    place = jnp.where(spot < tile, spot, spot - tile)
    bound = jnp.where(spot < tile, tally_ref[first_tile], tally_ref[last_tile])
    line_ref[0:1, 0:share] = jnp.where(place < bound, level, nothing)
    for k in range(3):
        wire_ref[mid + k : mid + k + 1, :] = line_ref[0:1, 128 * k : 128 * (k + 1)]


def unpack_targets(wires, operand_ref):
    lane = lax.broadcasted_iota(jnp.int32, (144, 128), 1)
    front = lane < 64
    sublane = lax.broadcasted_iota(jnp.int32, (16, 384), 0)
    pick_row = lax.broadcasted_iota(jnp.int32, (16, 128), 0)
    pick_lane = lax.broadcasted_iota(jnp.int32, (16, 128), 1)
    pick = jnp.where((pick_lane == pick_row + 64) & (pick_row < 6), 1.0, 0.0).astype(bf16)
    row_here = lax.axis_index("row")
    x_here = row_here // ring
    y_here = row_here - x_here * ring
    even = lax.rem(lax.axis_index("col"), 2) == 0
    for k in range(ring):
        for j in range(ring):
            x = lax.rem(x_here + ring - jnp.where(even, k, j), ring)
            y = lax.rem(y_here + ring - jnp.where(even, j, k), ring)
            a = pl.multiple_of((x * ring + y) * 288, 16)
            b = pl.multiple_of((x * ring + y) * 288 + 144, 16)
            both = wires[k][j, 0:144, :]
            high = both.astype(bf16).astype(f32)
            low = both - high
            high_back = pltpu.roll(high, 64, 1)
            low_back = pltpu.roll(low, 64, 1)
            tail = wires[k][j, 144:152, :]
            line = jnp.concatenate([tail[0:1], tail[1:2], tail[2:3]], axis=1)
            stacked = jnp.where(sublane < 6, 1.0, 0.0)
            for i, piece in enumerate(pieces(line)):
                stacked = jnp.where(sublane == i, piece, stacked)
            extra = lax.dot_general(
                stacked.astype(bf16), pick, (((0,), (0,)), ((), ())), preferred_element_type=f32
            )
            operand_ref[pl.ds(a, 144), 0:128] = jnp.where(front, high, low_back).astype(bf16)
            operand_ref[pl.ds(a, 144), 128:256] = jnp.where(front, high, extra[0:144]).astype(bf16)
            operand_ref[pl.ds(b, 144), 0:128] = jnp.where(front, high_back, low).astype(bf16)
            operand_ref[pl.ds(b, 144), 128:256] = jnp.where(
                front, high_back, extra[144:288]
            ).astype(bf16)
    rows = ring * ring * 288
    dummy_lane = lax.broadcasted_iota(jnp.int32, (unit_rows, 256), 1)
    operand_ref[rows : rows + unit_rows, :] = jnp.where(dummy_lane == 192, nothing, 0.0).astype(bf16)


def load_weights(points_ref, weights_ref, shift):
    tiles, depth, tile = weights_ref.shape
    for s in range(tiles):
        x = points_ref[:, s * tile : (s + 1) * tile]
        high = x.astype(bf16)
        low = (x - high.astype(f32)).astype(bf16)
        bias = (-0.5 * scale) * jnp.sum(x * x, axis=0, keepdims=True)
        moved = 0.0
        if shift is not None:
            moved = jnp.concatenate([shift[2 * s : 2 * s + 1], shift[2 * s + 1 : 2 * s + 2]], axis=1)
        weights_ref[s, 0:64, :] = high
        weights_ref[s, 64:128, :] = high
        weights_ref[s, 128:192, :] = low
        weights_ref[s, 192:256, :] = extra_rows(bias + moved)


def plan_work(count_ref, local_ref, plan_ref):
    src_tiles = local_ref.shape[0] - 6
    per_tile = 256 // unit_rows
    units = count_ref.shape[0] * per_tile
    per = units // group
    unit = lax.broadcasted_iota(jnp.int32, (24, 128), 1)
    tile_of = unit // per_tile
    bound = jnp.zeros((24, 128), jnp.int32)
    for t in range(count_ref.shape[0]):
        bound = jnp.where(tile_of == t, count_ref[t], bound)
    live = bound > (unit - tile_of * per_tile) * unit_rows
    hits = jnp.zeros((24, 128), f32)
    for k in range(local_ref.shape[1]):
        hits = jnp.where(local_ref[:, k : k + 1] == tile_of, 1.0, hits)
    active = jnp.where(live, hits, 0.0)
    down = lax.broadcasted_iota(jnp.int32, (128, 128), 0)
    across = lax.broadcasted_iota(jnp.int32, (128, 128), 1)
    upto = jnp.where(down <= across, 1.0, 0.0).astype(bf16)
    rank = jnp.dot(active.astype(bf16), upto, preferred_element_type=f32)
    counts = jnp.broadcast_to(rank[:, 127:128], (24, 128))
    place = jnp.where(active > 0.0, rank - 1.0, -1.0)
    place = jnp.concatenate([place, jnp.full((104, 128), -1.0, f32)], axis=0).T
    position = across.astype(f32)
    value = (down - units).astype(f32)
    plan_ref[...] = jnp.full_like(plan_ref, units)
    last = lax.broadcasted_iota(jnp.int32, (1, 128), 1)
    chunks = jnp.floor((counts + (group - 0.5)) / group).astype(jnp.int32)
    begin = jnp.zeros((1, 128), jnp.int32)
    items = [jnp.full((1, 128), src_tiles * per, jnp.int32)] * 2
    for s in range(src_tiles):
        listed = jnp.sum(
            jnp.where(place[:, s : s + 1] == position, value, 0.0), axis=0, keepdims=True
        )
        plan_ref[s : s + 1, :] = jnp.where(
            last == 127, counts[s : s + 1], listed + units
        ).astype(jnp.int32)
        for k in range(2):
            along = last + 128 * k - begin
            inside = (along >= 0) & (along < chunks[s : s + 1])
            items[k] = jnp.where(inside, s * per + along, items[k])
        begin = begin + chunks[s : s + 1]
    plan_ref[src_tiles + 1 : src_tiles + 2, :] = items[0]
    plan_ref[src_tiles + 2 : src_tiles + 3, :] = items[1]
    plan_ref[src_tiles + 3 : src_tiles + 4, :] = begin


def pipeline(plan_ref, items, operand_ref, weights_ref, buffers, visit):
    tiles, depth, tile = weights_ref.shape
    per = (operand_ref.shape[0] // unit_rows - 1) // group

    def where(i):
        code = plan_ref[tiles + 1 + i // 128, lax.rem(i, 128)]
        s = code // per
        first = (code - s * per) * group
        return jnp.minimum(s, tiles - 1), [plan_ref[s, first + k] for k in range(group)]

    def step(j, carry):
        for k in range(span):
            s, units = where(span * j + k)
            rows = jnp.concatenate(
                [
                    operand_ref[pl.ds(pl.multiple_of(u * unit_rows, unit_rows), unit_rows), :]
                    for u in units
                ],
                axis=0,
            )
            buffers[k][...] = jnp.dot(rows, weights_ref[s], preferred_element_type=f32)
        for k in range(span):
            visit(*where(span * j + k), buffers[k])
        return carry

    lax.fori_loop(0, (items + span - 1) // span, step, 0)


def on_duty(which):
    row = lax.axis_index("row")
    apart = lax.axis_index("col") - row + 2 - lax.rem(row, 2) + 16
    near = lax.rem(apart, 16) < 4
    return near if which == 0 else jnp.logical_not(near)


def row_pass(
    which, sheet_ref, points_ref, need_ref, w0, w1, w2, w3, lse_ref,
    operand_ref, weights_ref, plan_ref, sem, total_ref, *buffers,
):
    tiles, depth, tile = weights_ref.shape
    lse_ref[...] = jnp.full_like(lse_ref, nothing)
    copy = pltpu.make_async_copy(sheet_ref, plan_ref, sem)

    def put(s, line):
        lse_ref[pl.ds(2 * s, 1), :] = line[:, 0:128]
        lse_ref[pl.ds(2 * s + 1, 1), :] = line[:, 128:256]

    def work():
        items = plan_ref[tiles + 3, 0]
        unpack_targets((w0, w1, w2, w3), operand_ref)
        total_ref[...] = jnp.zeros_like(total_ref)

        def visit(s, units, buffer):
            part = jnp.exp2(buffer[...]).reshape(4, unit_rows * group // 32, 8, tile)
            total_ref[s] += jnp.sum(jnp.sum(part, axis=1), axis=0)

        pipeline(plan_ref, items, operand_ref, weights_ref, buffers, visit)
        total = jnp.sum(total_ref[...], axis=1)
        lines = jnp.where(total > 0.0, jnp.log2(jnp.maximum(total, 1e-37)), nothing)
        for s in range(tiles):
            put(s, lines[s : s + 1, :])
        fine = (total > 1e-25) & (total < 1e30)
        bad = jnp.where(fine, 0.0, need_ref[...])

        @pl.when(jnp.max(bad) > 0.0)
        def _():
            def one_tile(s, carry):
                weights = weights_ref[s]

                def step(i, state):
                    high, total = state
                    unit = plan_ref[s, i]
                    rows = operand_ref[
                        pl.ds(pl.multiple_of(unit * unit_rows, unit_rows), unit_rows), :
                    ]
                    score = jnp.dot(rows, weights, preferred_element_type=f32)
                    score = score.reshape(unit_rows // 8, 8, tile)
                    new = jnp.maximum(high, jnp.max(score, axis=0))
                    total = total * jnp.exp2(high - new)
                    return new, total + jnp.sum(jnp.exp2(score - new[None]), axis=0)

                start = (jnp.full((8, tile), floor, f32), jnp.zeros((8, tile), f32))
                high, total = lax.fori_loop(0, plan_ref[s, 127], step, start)
                top = jnp.max(high, axis=0, keepdims=True)
                total = jnp.sum(total * jnp.exp2(high - top), axis=0, keepdims=True)
                put(s, jnp.where(total > 0.0, top + jnp.log2(jnp.maximum(total, 1e-37)), nothing))
                return carry

            lax.fori_loop(0, tiles, one_tile, 0)

    @pl.when(on_duty(which))
    def _():
        copy.start()
        load_weights(points_ref, weights_ref, None)
        copy.wait()
        pl.when(plan_ref[tiles + 3, 0] > 0)(work)


def column_pass(
    which, sheet_ref, points_ref, need_ref, w0, w1, w2, w3, lse_ref, mass_ref, other_ref, out_ref,
    operand_ref, weights_ref, plan_ref, sem, total_ref, high_ref, *buffers,
):
    tiles, depth, tile = weights_ref.shape
    out_ref[...] = other_ref[...]
    copy = pltpu.make_async_copy(sheet_ref, plan_ref, sem)

    def work():
        items = plan_ref[tiles + 3, 0]
        unpack_targets((w0, w1, w2, w3), operand_ref)
        total_ref[...] = jnp.zeros_like(total_ref)

        def visit(s, units, buffer):
            for k, u in enumerate(units):
                where = pl.ds(pl.multiple_of(u * unit_rows, unit_rows), unit_rows)
                part = jnp.exp2(buffer[k * unit_rows : (k + 1) * unit_rows, :])
                total_ref[where, :] += part[:, 0:128] + part[:, 128:256]

        pipeline(plan_ref, items, operand_ref, weights_ref, buffers, visit)
        eye = lax.broadcasted_iota(jnp.int32, (128, 128), 0) == lax.broadcasted_iota(
            jnp.int32, (128, 128), 1
        )

        def to_row(column):
            return jnp.sum(jnp.where(eye, column, 0.0), axis=0, keepdims=True)

        bad = jnp.zeros((1, 128), f32)
        for u in range(out_ref.shape[0]):
            sums = to_row(jnp.sum(total_ref[u * 128 : (u + 1) * 128, :], axis=1, keepdims=True))
            out_ref[u : u + 1, :] = jnp.where(
                sums > 0.0, jnp.log2(jnp.maximum(sums, 1e-37)), nothing
            )
            bad = jnp.maximum(bad, jnp.where(sums > 1e-25, 0.0, need_ref[u : u + 1, :]))

        @pl.when(jnp.max(bad) > 0.0)
        def _():
            total_ref[...] = jnp.zeros_like(total_ref)
            high_ref[...] = jnp.full_like(high_ref, floor)

            def one_tile(s, carry):
                def step(i, inner):
                    unit = plan_ref[s, i]
                    where = pl.ds(pl.multiple_of(unit * unit_rows, unit_rows), unit_rows)
                    score = jnp.dot(
                        operand_ref[where, :], weights_ref[s], preferred_element_type=f32
                    )
                    a, b = score[:, 0:128], score[:, 128:256]
                    old = high_ref[where, :]
                    new = jnp.maximum(old, jnp.maximum(a, b))
                    high_ref[where, :] = new
                    total_ref[where, :] = (
                        total_ref[where, :] * jnp.exp2(old - new)
                        + jnp.exp2(a - new)
                        + jnp.exp2(b - new)
                    )
                    return inner

                lax.fori_loop(0, plan_ref[s, 127], step, 0)
                return carry

            lax.fori_loop(0, tiles, one_tile, 0)

            def finish(u, carry):
                where = pl.ds(pl.multiple_of(u * 128, 128), 128)
                high = high_ref[where, :]
                top = jnp.max(high, axis=1, keepdims=True)
                rest = total_ref[where, :] * jnp.exp2(high - top)
                sums = to_row(jnp.sum(rest, axis=1, keepdims=True))
                out_ref[pl.ds(u, 1), :] = jnp.where(
                    sums > 0.0, to_row(top) + jnp.log2(jnp.maximum(sums, 1e-37)), nothing
                )
                return carry

            lax.fori_loop(0, out_ref.shape[0], finish, 0)

    @pl.when(on_duty(which))
    def _():
        copy.start()
        load_weights(points_ref, weights_ref, mass_ref[...] - lse_ref[...])
        copy.wait()
        pl.when(plan_ref[tiles + 3, 0] > 0)(work)


def log_sum(parts):
    top = functools.reduce(jnp.maximum, parts)
    total = sum(jnp.exp2(p - top) for p in parts)
    return top + jnp.log2(total)


def roles(parity, cols):
    four = [d % cols for d in ((-2, -1, 0, 1), (-1, 0, 1, 2))[parity]]
    lead = [0, (1, -1)[parity] % cols]
    near = lead + [d for d in four if d not in lead]
    out = [(2, -2)[parity] % cols, cols // 2]
    begin = four[0]
    out += [(begin + 5) % cols, (begin + 6) % cols]
    return near, out + [d for d in range(cols) if d not in near and d not in out]


def filled(hops, count, cols):
    found = dict(hops)
    back = {d: s for s, d in hops}
    for rank in range(4):
        free = [d for d in range(count) if d not in back]
        for s in [s for s in range(count) if s not in found]:
            if rank == 0:
                picks = [back[s]] if s in back and back[s] in free else []
            elif rank == 1:
                picks = [s ^ 1] if s ^ 1 in free else []
            else:
                picks = [d for d in free if d != s and (d // cols == s // cols or rank == 3)]
                picks.sort(key=lambda d: min((d - s) % cols, (s - d) % cols))
            if picks:
                found[s] = picks[0]
                back[picks[0]] = s
                free.remove(picks[0])
    return sorted(found.items())


def shards(src_points, dst_points, dst_potential, partners, partner_count, src_count, dst_count):
    src_tiles = src_count.shape[0]
    dst_tiles = dst_count.shape[0]
    tile = src_points.shape[0] // src_tiles
    slots = partners.shape[1]
    rows = lax.axis_size("row")
    cols = lax.axis_size("col")
    row_here = lax.axis_index("row")
    col_here = lax.axis_index("col")
    share = dst_points.shape[0]
    points = dst_tiles * tile
    smem = pl.BlockSpec(memory_space=pltpu.SMEM)
    vmem = pl.BlockSpec(memory_space=pltpu.VMEM)
    anywhere = pl.BlockSpec(memory_space=pl.ANY)
    params = pltpu.CompilerParams(vmem_limit_bytes=24 * 1024 * 1024)
    places = [roles(r % 2, cols) for r in range(rows)]
    near = [[(r + d) % cols for d in places[r][0]] for r in range(rows)]
    far = [[(r + d) % cols for d in places[r][1]] for r in range(rows)]
    parity = lax.rem(row_here, 2)
    apart = lax.rem(col_here - row_here + 2 - parity + cols, cols)
    in_near = apart < 4
    in_far = (
        (apart == 5)
        | (apart == 6)
        | (apart == jnp.where(parity == 0, 4, cols - 1))
        | (apart == jnp.where(parity == 0, 10, 9))
    )

    def send(a, hops, full=True):
        hops = [(s[0] * cols + s[1], d[0] * cols + d[1]) for s, d in hops]
        return lax.ppermute(a, ("row", "col"), filled(hops, rows * cols, cols) if full else hops)

    every = [(r, c) for r in range(rows) for c in range(cols)]

    wire = pl.pallas_call(
        pack_targets,
        out_shape=jax.ShapeDtypeStruct((share // 2 + 8, 128), f32),
        in_specs=[anywhere] * 3,
        out_specs=vmem,
        scratch_shapes=[
            pltpu.VMEM((128, 384), f32),
            pltpu.VMEM((8, 384), f32),
            pltpu.SMEM((dst_tiles,), jnp.int32),
            pltpu.VMEM((64, share), f32),
            pltpu.VMEM((share,), f32),
            pltpu.SemaphoreType.DMA((3,)),
        ],
        compiler_params=pltpu.CompilerParams(vmem_limit_bytes=60 * 1024 * 1024),
    )(dst_count, dst_points.T, dst_potential)

    def around(r, dx, dy):
        return (r // ring + dx) % ring * ring + (r + dy) % ring

    def first_hop(r, c, k):
        return around(r, 0, k) if c % 2 == 0 else around(r, k, 0)

    def second_hop(r, c, k):
        return around(r, k, 0) if c % 2 == 0 else around(r, 0, k)

    bundle = jnp.stack(
        [wire]
        + [send(wire, [((r, c), (first_hop(r, c, k), c)) for r, c in every]) for k in (1, 2, 3)]
    )
    busy = [set(near[r] + far[r][:2]) for r in range(rows)]
    slot_on = jnp.arange(slots, dtype=jnp.int32)[None, :] < partner_count[:, None]
    local = jnp.where(slot_on, partners - col_here * dst_tiles, -1)
    plan = pl.pallas_call(
        plan_work,
        out_shape=jax.ShapeDtypeStruct((24, 128), jnp.int32),
        in_specs=[smem, vmem],
        out_specs=vmem,
        compiler_params=params,
    )(dst_count, jnp.pad(local, ((0, 24 - src_tiles), (0, 0)), constant_values=-1))
    plan, local, dst_count, src_count, bundle = lax.optimization_barrier(
        (plan, local, dst_count, src_count, bundle)
    )
    wires = [bundle] + [
        send(
            bundle,
            [
                ((r, c), (second_hop(r, c, k), c))
                for r, c in every
                if c in busy[second_hop(r, c, k)]
            ],
            full=False,
        )
        for k in (1, 2, 3)
    ]
    place = jnp.arange(tile, dtype=jnp.int32)
    src_live = place[None, :] < src_count[:, None]
    dst_live = place[None, :] < dst_count[:, None]
    wanted = jnp.any(local[:, :, None] == jnp.arange(dst_tiles, dtype=jnp.int32), axis=1)
    src_need = jnp.where(src_live & jnp.any(wanted, axis=1)[:, None], 1.0, 0.0)
    dst_need = jnp.where(dst_live & jnp.any(wanted, axis=0)[:, None], 1.0, 0.0)
    dst_need = dst_need.reshape(points // 128, 128)
    counted = jnp.repeat(src_count.astype(f32), 2)
    half_live = (place[:128][None, :] + 128 * (jnp.arange(2 * src_tiles) % 2)[:, None]) < jnp.repeat(
        src_count, 2
    )[:, None]
    all_src = src_tiles * rows
    mass = jnp.where(half_live, -jnp.log2(counted)[:, None] - math.log2(all_src), nothing)

    scratch = [
        pltpu.VMEM((points + unit_rows, 256), bf16),
        pltpu.VMEM((src_tiles, 256, tile), bf16),
    ]
    buffers = [pltpu.VMEM((unit_rows * group, tile), f32)] * span
    heavy = pl.CostEstimate(flops=8_000_000_000, bytes_accessed=4_000_000, transcendentals=8_000_000)
    light = pl.CostEstimate(flops=100_000_000, bytes_accessed=100_000, transcendentals=100_000)
    turned = src_points.T

    halves = 2 * src_tiles
    scratch += [pltpu.SMEM((24, 128), jnp.int32), pltpu.SemaphoreType.DMA]

    def sum_rows(which, cost):
        return pl.pallas_call(
            functools.partial(row_pass, which),
            out_shape=jax.ShapeDtypeStruct((halves, tile // 2), f32),
            in_specs=[anywhere] + [vmem] * (2 + ring),
            out_specs=vmem,
            scratch_shapes=scratch + [pltpu.VMEM((src_tiles, 8, tile), f32)] + buffers,
            compiler_params=params,
            cost_estimate=cost,
        )(plan, turned, src_need, *wires)

    def sum_columns(which, lse, other, cost):
        return pl.pallas_call(
            functools.partial(column_pass, which),
            out_shape=jax.ShapeDtypeStruct((points // 128, 128), f32),
            in_specs=[anywhere] + [vmem] * (5 + ring),
            out_specs=vmem,
            scratch_shapes=scratch + [pltpu.VMEM((points + unit_rows, 128), f32)] * 2 + buffers,
            compiler_params=params,
            cost_estimate=cost,
        )(plan, turned, dst_need, *wires, lse, mass, other)

    far_lse = sum_rows(1, light)
    early = send(
        far_lse,
        [((r, far[r][k]), (r, near[r][k])) for r in range(rows) for k in (0, 1)],
        full=False,
    )
    near_lse = sum_rows(0, heavy)
    got_early = (col_here == row_here) | (col_here == row_here + 1 - 2 * parity)
    lse = log_sum([near_lse, jnp.where(got_early, early, nothing)])

    def pairs(test):
        return [((r, c), (r, d)) for r in range(rows) for c in near[r] for d in near[r] if test(c, d)]

    lse = log_sum(
        [
            lse,
            send(lse, [((r, c), (r, c ^ 1)) for r, c in every]),
            send(lse, pairs(lambda c, d: (c - d) % cols in (2, cols - 2))),
            send(lse, pairs(lambda c, d: (c - (d ^ 1)) % cols in (2, cols - 2))),
        ]
    )
    spread = send(lse, [((r, near[r][k]), (r, far[r][k])) for r in range(rows) for k in range(4)])
    blank = jnp.full((points // 128, 128), nothing, f32)
    near_part = sum_columns(0, lse, blank, heavy)
    col_part = sum_columns(1, spread, near_part, light)
    known = jnp.where(in_far, spread, lse)
    known, near_part = lax.optimization_barrier((known, near_part))
    rest = send(
        known,
        [((r, (near[r] + far[r])[k]), (r, far[r][4 + k])) for r in range(rows) for k in range(8)],
    )
    shared_out = lax.all_to_all(col_part.reshape(rows, share), "row", 0, 0)

    row_lse = jnp.where(in_near | in_far, known, rest)
    src_potential = jnp.where(
        half_live,
        entropy * (-jnp.log(counted)[:, None] - math.log(all_src) - ln2 * row_lse),
        0.0,
    ).reshape(-1)

    spot = row_here * share + jnp.arange(share, dtype=jnp.int32)
    spot_tile = spot // tile
    spot_count = jnp.sum(
        jnp.where(
            spot_tile[:, None] == jnp.arange(dst_tiles, dtype=jnp.int32)[None, :],
            dst_count[None, :],
            0,
        ),
        axis=1,
    )
    top = jnp.max(shared_out, axis=0)
    col_log = top + jnp.log2(jnp.sum(jnp.exp2(shared_out - top[None]), axis=0))
    dst_new = jnp.where(
        (spot - spot_tile * tile < spot_count) & (top > 0.5 * nothing),
        entropy
        * (-jnp.log(spot_count.astype(f32)) - math.log(dst_tiles * cols) - ln2 * col_log)
        + dst_potential,
        0.0,
    )
    return src_potential, dst_new


def solution(mesh):
    in_specs = (
        P("row", None),
        P(("col", "row"), None),
        P(("col", "row")),
        P("row", None),
        P("row"),
        P("row"),
        P("col"),
    )
    out_specs = (P("row"), P(("col", "row")))
    return jax.shard_map(shards, mesh=mesh, in_specs=in_specs, out_specs=out_specs, check_vma=False)
```

```python
import functools
import math

import jax
import jax.numpy as jnp
from jax import lax
from jax.experimental import pallas as pl
from jax.experimental.pallas import tpu as pltpu
from jax.sharding import PartitionSpec as P

entropy = 0.1
scale = math.log2(math.e) / entropy
ln2 = math.log(2.0)
nothing = -1e30
floor = -1e25
unit_rows = 64
group = 9
span = 10
ring = 4
f32 = jnp.float32
bf16 = jnp.bfloat16


def pieces(a):
    first = a.astype(bf16).astype(f32)
    rest = a - first
    second = rest.astype(bf16).astype(f32)
    return first, second, rest - second


def extra_rows(bias):
    place = lax.broadcasted_iota(jnp.int32, (64, bias.shape[1]), 0)
    block = jnp.where(place < 3, 1.0, 0.0)
    for k, piece in enumerate(pieces(bias)):
        block = jnp.where(place == 3 + k, piece, block)
    return block.astype(bf16)


def pack_targets(
    count_ref, points_ref, potential_ref, wire_ref, square_ref, line_ref, tally_ref, held_ref, level_ref, sems,
):
    copies = [
        pltpu.make_async_copy(source, target, sems.at[k])
        for k, (source, target) in enumerate(
            ((points_ref, held_ref), (potential_ref, level_ref), (count_ref, tally_ref))
        )
    ]
    for copy in copies:
        copy.start()
    share = held_ref.shape[1]
    tile = 256
    mid = share // 2
    begin = lax.axis_index("row") * share
    first_tile = begin // tile
    offset = begin - first_tile * tile
    last_tile = jnp.minimum(first_tile + 1, tally_ref.shape[0] - 1)
    square_ref[...] = jnp.zeros_like(square_ref)
    line_ref[...] = jnp.full_like(line_ref, nothing)
    wire_ref[mid : mid + 8, :] = jnp.zeros((8, 128), f32)
    for copy in copies:
        copy.wait()
    points = held_ref[...]
    square_ref[0:64, 0:share] = points
    turned = square_ref[...].T
    wire_ref[0:mid, :] = scale * (turned[0:mid] + pltpu.roll(turned[mid:share], 64, 1))
    level = level_ref[...].reshape(1, share)
    level = scale * (level - 0.5 * jnp.sum(points * points, axis=0, keepdims=True))
    spot = offset + lax.broadcasted_iota(jnp.int32, (1, share), 1)
    place = jnp.where(spot < tile, spot, spot - tile)
    bound = jnp.where(spot < tile, tally_ref[first_tile], tally_ref[last_tile])
    line_ref[0:1, 0:share] = jnp.where(place < bound, level, nothing)
    for k in range(3):
        wire_ref[mid + k : mid + k + 1, :] = line_ref[0:1, 128 * k : 128 * (k + 1)]


def join(a_ref, b_ref, c_ref, d_ref, out_ref):
    for k, ref in enumerate((a_ref, b_ref, c_ref, d_ref)):
        out_ref[k] = ref[...]


def unpack_targets(wires, operand_ref):
    lane = lax.broadcasted_iota(jnp.int32, (144, 128), 1)
    front = lane < 64
    sublane = lax.broadcasted_iota(jnp.int32, (16, 384), 0)
    pick_row = lax.broadcasted_iota(jnp.int32, (16, 128), 0)
    pick_lane = lax.broadcasted_iota(jnp.int32, (16, 128), 1)
    pick = jnp.where((pick_lane == pick_row + 64) & (pick_row < 6), 1.0, 0.0).astype(bf16)
    row_here = lax.axis_index("row")
    x_here = row_here // ring
    y_here = row_here - x_here * ring
    even = lax.rem(lax.axis_index("col"), 2) == 0
    for k in range(ring):
        for j in range(ring):
            x = lax.rem(x_here + ring - jnp.where(even, k, j), ring)
            y = lax.rem(y_here + ring - jnp.where(even, j, k), ring)
            a = pl.multiple_of((x * ring + y) * 288, 16)
            b = pl.multiple_of((x * ring + y) * 288 + 144, 16)
            both = wires[k][j, 0:144, :]
            high = both.astype(bf16).astype(f32)
            low = both - high
            high_back = pltpu.roll(high, 64, 1)
            low_back = pltpu.roll(low, 64, 1)
            tail = wires[k][j, 144:152, :]
            line = jnp.concatenate([tail[0:1], tail[1:2], tail[2:3]], axis=1)
            stacked = jnp.where(sublane < 6, 1.0, 0.0)
            for i, piece in enumerate(pieces(line)):
                stacked = jnp.where(sublane == i, piece, stacked)
            extra = lax.dot_general(
                stacked.astype(bf16), pick, (((0,), (0,)), ((), ())), preferred_element_type=f32
            )
            operand_ref[pl.ds(a, 144), 0:128] = jnp.where(front, high, low_back).astype(bf16)
            operand_ref[pl.ds(a, 144), 128:256] = jnp.where(front, high, extra[0:144]).astype(bf16)
            operand_ref[pl.ds(b, 144), 0:128] = jnp.where(front, high_back, low).astype(bf16)
            operand_ref[pl.ds(b, 144), 128:256] = jnp.where(
                front, high_back, extra[144:288]
            ).astype(bf16)
    rows = ring * ring * 288
    dummy_lane = lax.broadcasted_iota(jnp.int32, (unit_rows, 256), 1)
    operand_ref[rows : rows + unit_rows, :] = jnp.where(dummy_lane == 192, nothing, 0.0).astype(bf16)


def load_weights(points_ref, weights_ref, shift):
    tiles, depth, tile = weights_ref.shape
    for s in range(tiles):
        x = points_ref[:, s * tile : (s + 1) * tile]
        high = x.astype(bf16)
        low = (x - high.astype(f32)).astype(bf16)
        bias = (-0.5 * scale) * jnp.sum(x * x, axis=0, keepdims=True)
        moved = 0.0
        if shift is not None:
            moved = jnp.concatenate([shift[2 * s : 2 * s + 1], shift[2 * s + 1 : 2 * s + 2]], axis=1)
        weights_ref[s, 0:64, :] = high
        weights_ref[s, 64:128, :] = high
        weights_ref[s, 128:192, :] = low
        weights_ref[s, 192:256, :] = extra_rows(bias + moved)


def plan_work(count_ref, local_ref, plan_ref):
    src_tiles = local_ref.shape[0] - 6
    per_tile = 256 // unit_rows
    units = count_ref.shape[0] * per_tile
    per = units // group
    unit = lax.broadcasted_iota(jnp.int32, (24, 128), 1)
    tile_of = unit // per_tile
    bound = jnp.zeros((24, 128), jnp.int32)
    for t in range(count_ref.shape[0]):
        bound = jnp.where(tile_of == t, count_ref[t], bound)
    live = bound > (unit - tile_of * per_tile) * unit_rows
    hits = jnp.zeros((24, 128), f32)
    for k in range(local_ref.shape[1]):
        hits = jnp.where(local_ref[:, k : k + 1] == tile_of, 1.0, hits)
    active = jnp.where(live, hits, 0.0)
    down = lax.broadcasted_iota(jnp.int32, (128, 128), 0)
    across = lax.broadcasted_iota(jnp.int32, (128, 128), 1)
    upto = jnp.where(down <= across, 1.0, 0.0).astype(bf16)
    rank = jnp.dot(active.astype(bf16), upto, preferred_element_type=f32)
    counts = jnp.broadcast_to(rank[:, 127:128], (24, 128))
    place = jnp.where(active > 0.0, rank - 1.0, -1.0)
    place = jnp.concatenate([place, jnp.full((104, 128), -1.0, f32)], axis=0).T
    position = across.astype(f32)
    value = (down - units).astype(f32)
    plan_ref[...] = jnp.full_like(plan_ref, units)
    last = lax.broadcasted_iota(jnp.int32, (1, 128), 1)
    chunks = jnp.floor((counts + (group - 0.5)) / group).astype(jnp.int32)
    begin = jnp.zeros((1, 128), jnp.int32)
    items = [jnp.full((1, 128), src_tiles * per, jnp.int32)] * 2
    for s in range(src_tiles):
        listed = jnp.sum(
            jnp.where(place[:, s : s + 1] == position, value, 0.0), axis=0, keepdims=True
        )
        plan_ref[s : s + 1, :] = jnp.where(
            last == 127, counts[s : s + 1], listed + units
        ).astype(jnp.int32)
        for k in range(2):
            along = last + 128 * k - begin
            inside = (along >= 0) & (along < chunks[s : s + 1])
            items[k] = jnp.where(inside, s * per + along, items[k])
        begin = begin + chunks[s : s + 1]
    plan_ref[src_tiles + 1 : src_tiles + 2, :] = items[0]
    plan_ref[src_tiles + 2 : src_tiles + 3, :] = items[1]
    plan_ref[src_tiles + 3 : src_tiles + 4, :] = begin


def pipeline(plan_ref, items, operand_ref, weights_ref, buffers, visit):
    tiles, depth, tile = weights_ref.shape
    per = (operand_ref.shape[0] // unit_rows - 1) // group

    def where(i):
        code = plan_ref[tiles + 1 + i // 128, lax.rem(i, 128)]
        s = code // per
        first = (code - s * per) * group
        return jnp.minimum(s, tiles - 1), [plan_ref[s, first + k] for k in range(group)]

    def step(j, carry):
        for k in range(span):
            s, units = where(span * j + k)
            rows = jnp.concatenate(
                [
                    operand_ref[pl.ds(pl.multiple_of(u * unit_rows, unit_rows), unit_rows), :]
                    for u in units
                ],
                axis=0,
            )
            buffers[k][...] = jnp.dot(rows, weights_ref[s], preferred_element_type=f32)
        for k in range(span):
            visit(*where(span * j + k), buffers[k])
        return carry

    lax.fori_loop(0, (items + span - 1) // span, step, 0)


def on_duty(which):
    row = lax.axis_index("row")
    apart = lax.axis_index("col") - row + 2 - lax.rem(row, 2) + 16
    near = lax.rem(apart, 16) < 4
    return near if which == 0 else jnp.logical_not(near)


def row_pass(
    which, sheet_ref, points_ref, need_ref, w0, w1, w2, w3, lse_ref,
    operand_ref, weights_ref, plan_ref, sem, total_ref, *buffers,
):
    tiles, depth, tile = weights_ref.shape
    lse_ref[...] = jnp.full_like(lse_ref, nothing)
    copy = pltpu.make_async_copy(sheet_ref, plan_ref, sem)

    def put(s, line):
        lse_ref[pl.ds(2 * s, 1), :] = line[:, 0:128]
        lse_ref[pl.ds(2 * s + 1, 1), :] = line[:, 128:256]

    def work():
        items = plan_ref[tiles + 3, 0]
        unpack_targets((w0, w1, w2, w3), operand_ref)
        total_ref[...] = jnp.zeros_like(total_ref)

        def visit(s, units, buffer):
            part = jnp.exp2(buffer[...]).reshape(4, unit_rows * group // 32, 8, tile)
            total_ref[s] += jnp.sum(jnp.sum(part, axis=1), axis=0)

        pipeline(plan_ref, items, operand_ref, weights_ref, buffers, visit)
        total = jnp.sum(total_ref[...], axis=1)
        lines = jnp.where(total > 0.0, jnp.log2(jnp.maximum(total, 1e-37)), nothing)
        for s in range(tiles):
            put(s, lines[s : s + 1, :])
        fine = (total > 1e-25) & (total < 1e30)
        bad = jnp.where(fine, 0.0, need_ref[...])

        @pl.when(jnp.max(bad) > 0.0)
        def _():
            def one_tile(s, carry):
                weights = weights_ref[s]

                def step(i, state):
                    high, total = state
                    unit = plan_ref[s, i]
                    rows = operand_ref[
                        pl.ds(pl.multiple_of(unit * unit_rows, unit_rows), unit_rows), :
                    ]
                    score = jnp.dot(rows, weights, preferred_element_type=f32)
                    score = score.reshape(unit_rows // 8, 8, tile)
                    new = jnp.maximum(high, jnp.max(score, axis=0))
                    total = total * jnp.exp2(high - new)
                    return new, total + jnp.sum(jnp.exp2(score - new[None]), axis=0)

                start = (jnp.full((8, tile), floor, f32), jnp.zeros((8, tile), f32))
                high, total = lax.fori_loop(0, plan_ref[s, 127], step, start)
                top = jnp.max(high, axis=0, keepdims=True)
                total = jnp.sum(total * jnp.exp2(high - top), axis=0, keepdims=True)
                put(s, jnp.where(total > 0.0, top + jnp.log2(jnp.maximum(total, 1e-37)), nothing))
                return carry

            lax.fori_loop(0, tiles, one_tile, 0)

    @pl.when(on_duty(which))
    def _():
        copy.start()
        load_weights(points_ref, weights_ref, None)
        copy.wait()
        pl.when(plan_ref[tiles + 3, 0] > 0)(work)


def column_pass(
    which, sheet_ref, points_ref, need_ref, w0, w1, w2, w3, lse_ref, mass_ref, other_ref, out_ref,
    operand_ref, weights_ref, plan_ref, sem, total_ref, high_ref, *buffers,
):
    tiles, depth, tile = weights_ref.shape
    out_ref[...] = other_ref[...]
    copy = pltpu.make_async_copy(sheet_ref, plan_ref, sem)

    def work():
        items = plan_ref[tiles + 3, 0]
        unpack_targets((w0, w1, w2, w3), operand_ref)
        total_ref[...] = jnp.zeros_like(total_ref)

        def visit(s, units, buffer):
            for k, u in enumerate(units):
                where = pl.ds(pl.multiple_of(u * unit_rows, unit_rows), unit_rows)
                part = jnp.exp2(buffer[k * unit_rows : (k + 1) * unit_rows, :])
                total_ref[where, :] += part[:, 0:128] + part[:, 128:256]

        pipeline(plan_ref, items, operand_ref, weights_ref, buffers, visit)
        eye = lax.broadcasted_iota(jnp.int32, (128, 128), 0) == lax.broadcasted_iota(
            jnp.int32, (128, 128), 1
        )

        def to_row(column):
            return jnp.sum(jnp.where(eye, column, 0.0), axis=0, keepdims=True)

        bad = jnp.zeros((1, 128), f32)
        for u in range(out_ref.shape[0]):
            sums = to_row(jnp.sum(total_ref[u * 128 : (u + 1) * 128, :], axis=1, keepdims=True))
            out_ref[u : u + 1, :] = jnp.where(
                sums > 0.0, jnp.log2(jnp.maximum(sums, 1e-37)), nothing
            )
            bad = jnp.maximum(bad, jnp.where(sums > 1e-25, 0.0, need_ref[u : u + 1, :]))

        @pl.when(jnp.max(bad) > 0.0)
        def _():
            total_ref[...] = jnp.zeros_like(total_ref)
            high_ref[...] = jnp.full_like(high_ref, floor)

            def one_tile(s, carry):
                def step(i, inner):
                    unit = plan_ref[s, i]
                    where = pl.ds(pl.multiple_of(unit * unit_rows, unit_rows), unit_rows)
                    score = jnp.dot(
                        operand_ref[where, :], weights_ref[s], preferred_element_type=f32
                    )
                    a, b = score[:, 0:128], score[:, 128:256]
                    old = high_ref[where, :]
                    new = jnp.maximum(old, jnp.maximum(a, b))
                    high_ref[where, :] = new
                    total_ref[where, :] = (
                        total_ref[where, :] * jnp.exp2(old - new)
                        + jnp.exp2(a - new)
                        + jnp.exp2(b - new)
                    )
                    return inner

                lax.fori_loop(0, plan_ref[s, 127], step, 0)
                return carry

            lax.fori_loop(0, tiles, one_tile, 0)

            def finish(u, carry):
                where = pl.ds(pl.multiple_of(u * 128, 128), 128)
                high = high_ref[where, :]
                top = jnp.max(high, axis=1, keepdims=True)
                rest = total_ref[where, :] * jnp.exp2(high - top)
                sums = to_row(jnp.sum(rest, axis=1, keepdims=True))
                out_ref[pl.ds(u, 1), :] = jnp.where(
                    sums > 0.0, to_row(top) + jnp.log2(jnp.maximum(sums, 1e-37)), nothing
                )
                return carry

            lax.fori_loop(0, out_ref.shape[0], finish, 0)

    @pl.when(on_duty(which))
    def _():
        copy.start()
        load_weights(points_ref, weights_ref, mass_ref[...] - lse_ref[...])
        copy.wait()
        pl.when(plan_ref[tiles + 3, 0] > 0)(work)


def log_sum(parts):
    top = functools.reduce(jnp.maximum, parts)
    total = sum(jnp.exp2(p - top) for p in parts)
    return top + jnp.log2(total)


def roles(parity, cols):
    four = [d % cols for d in ((-2, -1, 0, 1), (-1, 0, 1, 2))[parity]]
    lead = [0, (1, -1)[parity] % cols]
    near = lead + [d for d in four if d not in lead]
    out = [(2, -2)[parity] % cols, cols // 2]
    begin = four[0]
    out += [(begin + 5) % cols, (begin + 6) % cols]
    return near, out + [d for d in range(cols) if d not in near and d not in out]


def filled(hops, count, cols):
    found = dict(hops)
    back = {d: s for s, d in hops}
    for rank in range(4):
        free = [d for d in range(count) if d not in back]
        for s in [s for s in range(count) if s not in found]:
            if rank == 0:
                picks = [back[s]] if s in back and back[s] in free else []
            elif rank == 1:
                picks = [s ^ 1] if s ^ 1 in free else []
            else:
                picks = [d for d in free if d != s and (d // cols == s // cols or rank == 3)]
                picks.sort(key=lambda d: min((d - s) % cols, (s - d) % cols))
            if picks:
                found[s] = picks[0]
                back[picks[0]] = s
                free.remove(picks[0])
    return sorted(found.items())


def shards(src_points, dst_points, dst_potential, partners, partner_count, src_count, dst_count):
    src_tiles = src_count.shape[0]
    dst_tiles = dst_count.shape[0]
    tile = src_points.shape[0] // src_tiles
    slots = partners.shape[1]
    rows = lax.axis_size("row")
    cols = lax.axis_size("col")
    row_here = lax.axis_index("row")
    col_here = lax.axis_index("col")
    share = dst_points.shape[0]
    points = dst_tiles * tile
    smem = pl.BlockSpec(memory_space=pltpu.SMEM)
    vmem = pl.BlockSpec(memory_space=pltpu.VMEM)
    anywhere = pl.BlockSpec(memory_space=pl.ANY)
    params = pltpu.CompilerParams(vmem_limit_bytes=24 * 1024 * 1024)
    places = [roles(r % 2, cols) for r in range(rows)]
    near = [[(r + d) % cols for d in places[r][0]] for r in range(rows)]
    far = [[(r + d) % cols for d in places[r][1]] for r in range(rows)]
    parity = lax.rem(row_here, 2)
    apart = lax.rem(col_here - row_here + 2 - parity + cols, cols)
    in_near = apart < 4
    in_far = (
        (apart == 5)
        | (apart == 6)
        | (apart == jnp.where(parity == 0, 4, cols - 1))
        | (apart == jnp.where(parity == 0, 10, 9))
    )

    def send(a, hops, full=True):
        hops = [(s[0] * cols + s[1], d[0] * cols + d[1]) for s, d in hops]
        return lax.ppermute(a, ("row", "col"), filled(hops, rows * cols, cols) if full else hops)

    every = [(r, c) for r in range(rows) for c in range(cols)]

    wire = pl.pallas_call(
        pack_targets,
        out_shape=jax.ShapeDtypeStruct((share // 2 + 8, 128), f32),
        in_specs=[anywhere] * 3,
        out_specs=vmem,
        scratch_shapes=[
            pltpu.VMEM((128, 384), f32),
            pltpu.VMEM((8, 384), f32),
            pltpu.SMEM((dst_tiles,), jnp.int32),
            pltpu.VMEM((64, share), f32),
            pltpu.VMEM((share,), f32),
            pltpu.SemaphoreType.DMA((3,)),
        ],
        compiler_params=pltpu.CompilerParams(vmem_limit_bytes=60 * 1024 * 1024),
    )(dst_count, dst_points.T, dst_potential)

    def around(r, dx, dy):
        return (r // ring + dx) % ring * ring + (r + dy) % ring

    def first_hop(r, c, k):
        return around(r, 0, k) if c % 2 == 0 else around(r, k, 0)

    def second_hop(r, c, k):
        return around(r, k, 0) if c % 2 == 0 else around(r, 0, k)

    bundle = pl.pallas_call(
        join,
        out_shape=jax.ShapeDtypeStruct((ring,) + wire.shape, f32),
        in_specs=[vmem] * ring,
        out_specs=vmem,
        compiler_params=params,
    )(wire, *[send(wire, [((r, c), (first_hop(r, c, k), c)) for r, c in every]) for k in (1, 2, 3)])
    busy = [set(near[r] + far[r][:2]) for r in range(rows)]
    slot_on = jnp.arange(slots, dtype=jnp.int32)[None, :] < partner_count[:, None]
    local = jnp.where(slot_on, partners - col_here * dst_tiles, -1)
    plan = pl.pallas_call(
        plan_work,
        out_shape=jax.ShapeDtypeStruct((24, 128), jnp.int32),
        in_specs=[smem, vmem],
        out_specs=vmem,
        compiler_params=params,
    )(dst_count, jnp.pad(local, ((0, 24 - src_tiles), (0, 0)), constant_values=-1))
    plan, local, dst_count, src_count, bundle = lax.optimization_barrier(
        (plan, local, dst_count, src_count, bundle)
    )
    wires = [bundle] + [
        send(
            bundle,
            [
                ((r, c), (second_hop(r, c, k), c))
                for r, c in every
                if c in busy[second_hop(r, c, k)]
            ],
            full=False,
        )
        for k in (1, 2, 3)
    ]
    place = jnp.arange(tile, dtype=jnp.int32)
    src_live = place[None, :] < src_count[:, None]
    dst_live = place[None, :] < dst_count[:, None]
    wanted = jnp.any(local[:, :, None] == jnp.arange(dst_tiles, dtype=jnp.int32), axis=1)
    src_need = jnp.where(src_live & jnp.any(wanted, axis=1)[:, None], 1.0, 0.0)
    dst_need = jnp.where(dst_live & jnp.any(wanted, axis=0)[:, None], 1.0, 0.0)
    dst_need = dst_need.reshape(points // 128, 128)
    counted = jnp.repeat(src_count.astype(f32), 2)
    half_live = (place[:128][None, :] + 128 * (jnp.arange(2 * src_tiles) % 2)[:, None]) < jnp.repeat(
        src_count, 2
    )[:, None]
    all_src = src_tiles * rows
    mass = jnp.where(half_live, -jnp.log2(counted)[:, None] - math.log2(all_src), nothing)

    scratch = [
        pltpu.VMEM((points + unit_rows, 256), bf16),
        pltpu.VMEM((src_tiles, 256, tile), bf16),
    ]
    buffers = [pltpu.VMEM((unit_rows * group, tile), f32)] * span
    heavy = pl.CostEstimate(flops=8_000_000_000, bytes_accessed=4_000_000, transcendentals=8_000_000)
    light = pl.CostEstimate(flops=100_000_000, bytes_accessed=100_000, transcendentals=100_000)
    turned = src_points.T

    halves = 2 * src_tiles
    scratch += [pltpu.SMEM((24, 128), jnp.int32), pltpu.SemaphoreType.DMA]

    def sum_rows(which, cost):
        return pl.pallas_call(
            functools.partial(row_pass, which),
            out_shape=jax.ShapeDtypeStruct((halves, tile // 2), f32),
            in_specs=[anywhere] + [vmem] * (2 + ring),
            out_specs=vmem,
            scratch_shapes=scratch + [pltpu.VMEM((src_tiles, 8, tile), f32)] + buffers,
            compiler_params=params,
            cost_estimate=cost,
        )(plan, turned, src_need, *wires)

    def sum_columns(which, lse, other, cost):
        return pl.pallas_call(
            functools.partial(column_pass, which),
            out_shape=jax.ShapeDtypeStruct((points // 128, 128), f32),
            in_specs=[anywhere] + [vmem] * (5 + ring),
            out_specs=vmem,
            scratch_shapes=scratch + [pltpu.VMEM((points + unit_rows, 128), f32)] * 2 + buffers,
            compiler_params=params,
            cost_estimate=cost,
        )(plan, turned, dst_need, *wires, lse, mass, other)

    far_lse = sum_rows(1, light)
    loops = [
        [(r, c) for c in (far[r][k], near[r][k], far[r][k] ^ 1)] for r in range(rows) for k in (0, 1)
    ]
    early = send(far_lse, [(loop[i], loop[(i + 1) % 3]) for loop in loops for i in range(3)])
    near_lse = sum_rows(0, heavy)
    got_early = (col_here == row_here) | (col_here == row_here + 1 - 2 * parity)
    lse = log_sum([near_lse, jnp.where(got_early, early, nothing)])

    def pairs(test):
        return [((r, c), (r, d)) for r in range(rows) for c in near[r] for d in near[r] if test(c, d)]

    lse = log_sum(
        [
            lse,
            send(lse, [((r, c), (r, c ^ 1)) for r, c in every]),
            send(lse, pairs(lambda c, d: (c - d) % cols in (2, cols - 2))),
            send(lse, pairs(lambda c, d: (c - (d ^ 1)) % cols in (2, cols - 2))),
        ]
    )
    spread = send(lse, [((r, near[r][k]), (r, far[r][k])) for r in range(rows) for k in range(4)])
    blank = jnp.full((points // 128, 128), nothing, f32)
    near_part = sum_columns(0, lse, blank, heavy)
    col_part = sum_columns(1, spread, near_part, light)
    known = jnp.where(in_far, spread, lse)
    known, near_part = lax.optimization_barrier((known, near_part))
    rest = send(
        known,
        [((r, (near[r] + far[r])[k]), (r, far[r][4 + k])) for r in range(rows) for k in range(8)],
    )
    shared_out = lax.all_to_all(col_part.reshape(rows, share), "row", 0, 0)

    row_lse = jnp.where(in_near | in_far, known, rest)
    src_potential = jnp.where(
        half_live,
        entropy * (-jnp.log(counted)[:, None] - math.log(all_src) - ln2 * row_lse),
        0.0,
    ).reshape(-1)

    spot = row_here * share + jnp.arange(share, dtype=jnp.int32)
    spot_tile = spot // tile
    spot_count = jnp.sum(
        jnp.where(
            spot_tile[:, None] == jnp.arange(dst_tiles, dtype=jnp.int32)[None, :],
            dst_count[None, :],
            0,
        ),
        axis=1,
    )
    top = jnp.max(shared_out, axis=0)
    col_log = top + jnp.log2(jnp.sum(jnp.exp2(shared_out - top[None]), axis=0))
    dst_new = jnp.where(
        (spot - spot_tile * tile < spot_count) & (top > 0.5 * nothing),
        entropy
        * (-jnp.log(spot_count.astype(f32)) - math.log(dst_tiles * cols) - ln2 * col_log)
        + dst_potential,
        0.0,
    )
    return src_potential, dst_new


def solution(mesh):
    in_specs = (
        P("row", None),
        P(("col", "row"), None),
        P(("col", "row")),
        P("row", None),
        P("row"),
        P("row"),
        P("col"),
    )
    out_specs = (P("row"), P(("col", "row")))
    return jax.shard_map(shards, mesh=mesh, in_specs=in_specs, out_specs=out_specs, check_vma=False)
```

```python
import functools
import math

import jax
import jax.numpy as jnp
from jax import lax
from jax.experimental import pallas as pl
from jax.experimental.pallas import tpu as pltpu
from jax.sharding import PartitionSpec as P

entropy = 0.1
scale = math.log2(math.e) / entropy
ln2 = math.log(2.0)
nothing = -1e30
floor = -1e25
unit_rows = 64
group = 9
span = 10
ring = 4
f32 = jnp.float32
bf16 = jnp.bfloat16


def pieces(a):
    first = a.astype(bf16).astype(f32)
    rest = a - first
    second = rest.astype(bf16).astype(f32)
    return first, second, rest - second


def extra_rows(bias):
    place = lax.broadcasted_iota(jnp.int32, (64, bias.shape[1]), 0)
    block = jnp.where(place < 3, 1.0, 0.0)
    for k, piece in enumerate(pieces(bias)):
        block = jnp.where(place == 3 + k, piece, block)
    return block.astype(bf16)


def pack_targets(
    count_ref, points_ref, potential_ref, wire_ref, square_ref, line_ref, tally_ref, held_ref, level_ref, sems,
):
    copies = [
        pltpu.make_async_copy(source, target, sems.at[k])
        for k, (source, target) in enumerate(
            ((points_ref, held_ref), (potential_ref, level_ref), (count_ref, tally_ref))
        )
    ]
    for copy in copies:
        copy.start()
    share = held_ref.shape[1]
    tile = 256
    mid = share // 2
    begin = lax.axis_index("row") * share
    first_tile = begin // tile
    offset = begin - first_tile * tile
    last_tile = jnp.minimum(first_tile + 1, tally_ref.shape[0] - 1)
    square_ref[...] = jnp.zeros_like(square_ref)
    line_ref[...] = jnp.full_like(line_ref, nothing)
    wire_ref[mid : mid + 8, :] = jnp.zeros((8, 128), f32)
    for copy in copies:
        copy.wait()
    points = held_ref[...]
    square_ref[0:64, 0:share] = points
    turned = square_ref[...].T
    wire_ref[0:mid, :] = scale * (turned[0:mid] + pltpu.roll(turned[mid:share], 64, 1))
    level = level_ref[...].reshape(1, share)
    level = scale * (level - 0.5 * jnp.sum(points * points, axis=0, keepdims=True))
    spot = offset + lax.broadcasted_iota(jnp.int32, (1, share), 1)
    place = jnp.where(spot < tile, spot, spot - tile)
    bound = jnp.where(spot < tile, tally_ref[first_tile], tally_ref[last_tile])
    line_ref[0:1, 0:share] = jnp.where(place < bound, level, nothing)
    for k in range(3):
        wire_ref[mid + k : mid + k + 1, :] = line_ref[0:1, 128 * k : 128 * (k + 1)]


def join(a_ref, b_ref, c_ref, d_ref, out_ref):
    for k, ref in enumerate((a_ref, b_ref, c_ref, d_ref)):
        out_ref[k] = ref[...]


def unpack_targets(wires, operand_ref):
    lane = lax.broadcasted_iota(jnp.int32, (144, 128), 1)
    front = lane < 64
    sublane = lax.broadcasted_iota(jnp.int32, (16, 384), 0)
    pick_row = lax.broadcasted_iota(jnp.int32, (16, 128), 0)
    pick_lane = lax.broadcasted_iota(jnp.int32, (16, 128), 1)
    pick = jnp.where((pick_lane == pick_row + 64) & (pick_row < 6), 1.0, 0.0).astype(bf16)
    row_here = lax.axis_index("row")
    x_here = row_here // ring
    y_here = row_here - x_here * ring
    even = lax.rem(lax.axis_index("col"), 2) == 0
    for k in range(ring):
        for j in range(ring):
            x = lax.rem(x_here + ring - jnp.where(even, k, j), ring)
            y = lax.rem(y_here + ring - jnp.where(even, j, k), ring)
            a = pl.multiple_of((x * ring + y) * 288, 16)
            b = pl.multiple_of((x * ring + y) * 288 + 144, 16)
            both = wires[k][j, 0:144, :]
            high = both.astype(bf16).astype(f32)
            low = both - high
            high_back = pltpu.roll(high, 64, 1)
            low_back = pltpu.roll(low, 64, 1)
            tail = wires[k][j, 144:152, :]
            line = jnp.concatenate([tail[0:1], tail[1:2], tail[2:3]], axis=1)
            stacked = jnp.where(sublane < 6, 1.0, 0.0)
            for i, piece in enumerate(pieces(line)):
                stacked = jnp.where(sublane == i, piece, stacked)
            extra = lax.dot_general(
                stacked.astype(bf16), pick, (((0,), (0,)), ((), ())), preferred_element_type=f32
            )
            operand_ref[pl.ds(a, 144), 0:128] = jnp.where(front, high, low_back).astype(bf16)
            operand_ref[pl.ds(a, 144), 128:256] = jnp.where(front, high, extra[0:144]).astype(bf16)
            operand_ref[pl.ds(b, 144), 0:128] = jnp.where(front, high_back, low).astype(bf16)
            operand_ref[pl.ds(b, 144), 128:256] = jnp.where(
                front, high_back, extra[144:288]
            ).astype(bf16)
    rows = ring * ring * 288
    dummy_lane = lax.broadcasted_iota(jnp.int32, (unit_rows, 256), 1)
    operand_ref[rows : rows + unit_rows, :] = jnp.where(dummy_lane == 192, nothing, 0.0).astype(bf16)


def load_weights(points_ref, weights_ref, shift):
    tiles, depth, tile = weights_ref.shape
    for s in range(tiles):
        x = points_ref[:, s * tile : (s + 1) * tile]
        high = x.astype(bf16)
        low = (x - high.astype(f32)).astype(bf16)
        bias = (-0.5 * scale) * jnp.sum(x * x, axis=0, keepdims=True)
        moved = 0.0
        if shift is not None:
            moved = jnp.concatenate([shift[2 * s : 2 * s + 1], shift[2 * s + 1 : 2 * s + 2]], axis=1)
        weights_ref[s, 0:64, :] = high
        weights_ref[s, 64:128, :] = high
        weights_ref[s, 128:192, :] = low
        weights_ref[s, 192:256, :] = extra_rows(bias + moved)


def plan_work(count_ref, local_ref, wire_ref, plan_ref, near_wire_ref, sem):
    copy = pltpu.make_async_copy(wire_ref, near_wire_ref, sem)
    copy.start()
    src_tiles = local_ref.shape[0] - 6
    per_tile = 256 // unit_rows
    units = count_ref.shape[0] * per_tile
    per = units // group
    unit = lax.broadcasted_iota(jnp.int32, (24, 128), 1)
    tile_of = unit // per_tile
    bound = jnp.zeros((24, 128), jnp.int32)
    for t in range(count_ref.shape[0]):
        bound = jnp.where(tile_of == t, count_ref[t], bound)
    live = bound > (unit - tile_of * per_tile) * unit_rows
    hits = jnp.zeros((24, 128), f32)
    for k in range(local_ref.shape[1]):
        hits = jnp.where(local_ref[:, k : k + 1] == tile_of, 1.0, hits)
    active = jnp.where(live, hits, 0.0)
    down = lax.broadcasted_iota(jnp.int32, (128, 128), 0)
    across = lax.broadcasted_iota(jnp.int32, (128, 128), 1)
    upto = jnp.where(down <= across, 1.0, 0.0).astype(bf16)
    rank = jnp.dot(active.astype(bf16), upto, preferred_element_type=f32)
    counts = jnp.broadcast_to(rank[:, 127:128], (24, 128))
    place = jnp.where(active > 0.0, rank - 1.0, -1.0)
    place = jnp.concatenate([place, jnp.full((104, 128), -1.0, f32)], axis=0).T
    position = across.astype(f32)
    value = (down - units).astype(f32)
    plan_ref[...] = jnp.full_like(plan_ref, units)
    last = lax.broadcasted_iota(jnp.int32, (1, 128), 1)
    chunks = jnp.floor((counts + (group - 0.5)) / group).astype(jnp.int32)
    begin = jnp.zeros((1, 128), jnp.int32)
    items = [jnp.full((1, 128), src_tiles * per, jnp.int32)] * 2
    for s in range(src_tiles):
        listed = jnp.sum(
            jnp.where(place[:, s : s + 1] == position, value, 0.0), axis=0, keepdims=True
        )
        plan_ref[s : s + 1, :] = jnp.where(
            last == 127, counts[s : s + 1], listed + units
        ).astype(jnp.int32)
        for k in range(2):
            along = last + 128 * k - begin
            inside = (along >= 0) & (along < chunks[s : s + 1])
            items[k] = jnp.where(inside, s * per + along, items[k])
        begin = begin + chunks[s : s + 1]
    plan_ref[src_tiles + 1 : src_tiles + 2, :] = items[0]
    plan_ref[src_tiles + 2 : src_tiles + 3, :] = items[1]
    plan_ref[src_tiles + 3 : src_tiles + 4, :] = begin
    copy.wait()


def pipeline(plan_ref, items, operand_ref, weights_ref, buffers, visit):
    tiles, depth, tile = weights_ref.shape
    per = (operand_ref.shape[0] // unit_rows - 1) // group

    def where(i):
        code = plan_ref[tiles + 1 + i // 128, lax.rem(i, 128)]
        s = code // per
        first = (code - s * per) * group
        return jnp.minimum(s, tiles - 1), [plan_ref[s, first + k] for k in range(group)]

    def step(j, carry):
        for k in range(span):
            s, units = where(span * j + k)
            rows = jnp.concatenate(
                [
                    operand_ref[pl.ds(pl.multiple_of(u * unit_rows, unit_rows), unit_rows), :]
                    for u in units
                ],
                axis=0,
            )
            buffers[k][...] = jnp.dot(rows, weights_ref[s], preferred_element_type=f32)
        for k in range(span):
            visit(*where(span * j + k), buffers[k])
        return carry

    lax.fori_loop(0, (items + span - 1) // span, step, 0)


def distance():
    row = lax.axis_index("row")
    return lax.rem(lax.axis_index("col") - row + 2 - lax.rem(row, 2) + 16, 16)


def on_duty(which):
    near = distance() < 4
    return near if which == 0 else jnp.logical_not(near)


def finish_sources(known_ref, rest_ref, mass_ref, live_ref, out_ref):
    apart = distance()
    odd = lax.rem(lax.axis_index("row"), 2) == 1
    here = (apart < 4) | (apart == 5) | (apart == 6)
    here |= (apart == jnp.where(odd, 15, 4)) | (apart == jnp.where(odd, 9, 10))
    total = jnp.where(here, known_ref[...], rest_ref[...])
    out_ref[...] = jnp.where(
        live_ref[...] > 0.0, (entropy * ln2) * (mass_ref[...] - total), 0.0
    )


def row_pass(
    which, sheet_ref, points_ref, need_ref, w0, w1, w2, w3, lse_ref,
    operand_ref, weights_ref, plan_ref, sem, total_ref, *buffers,
):
    tiles, depth, tile = weights_ref.shape
    lse_ref[...] = jnp.full_like(lse_ref, nothing)
    copy = pltpu.make_async_copy(sheet_ref, plan_ref, sem)

    def put(s, line):
        lse_ref[pl.ds(2 * s, 1), :] = line[:, 0:128]
        lse_ref[pl.ds(2 * s + 1, 1), :] = line[:, 128:256]

    def work():
        items = plan_ref[tiles + 3, 0]
        unpack_targets((w0, w1, w2, w3), operand_ref)
        total_ref[...] = jnp.zeros_like(total_ref)

        def visit(s, units, buffer):
            part = jnp.exp2(buffer[...]).reshape(4, unit_rows * group // 32, 8, tile)
            total_ref[s] += jnp.sum(jnp.sum(part, axis=1), axis=0)

        pipeline(plan_ref, items, operand_ref, weights_ref, buffers, visit)
        total = jnp.sum(total_ref[...], axis=1)
        lines = jnp.where(total > 0.0, jnp.log2(jnp.maximum(total, 1e-37)), nothing)
        for s in range(tiles):
            put(s, lines[s : s + 1, :])
        fine = (total > 1e-25) & (total < 1e30)
        bad = jnp.where(fine, 0.0, need_ref[...])

        @pl.when(jnp.max(bad) > 0.0)
        def _():
            def one_tile(s, carry):
                weights = weights_ref[s]

                def step(i, state):
                    high, total = state
                    unit = plan_ref[s, i]
                    rows = operand_ref[
                        pl.ds(pl.multiple_of(unit * unit_rows, unit_rows), unit_rows), :
                    ]
                    score = jnp.dot(rows, weights, preferred_element_type=f32)
                    score = score.reshape(unit_rows // 8, 8, tile)
                    new = jnp.maximum(high, jnp.max(score, axis=0))
                    total = total * jnp.exp2(high - new)
                    return new, total + jnp.sum(jnp.exp2(score - new[None]), axis=0)

                start = (jnp.full((8, tile), floor, f32), jnp.zeros((8, tile), f32))
                high, total = lax.fori_loop(0, plan_ref[s, 127], step, start)
                top = jnp.max(high, axis=0, keepdims=True)
                total = jnp.sum(total * jnp.exp2(high - top), axis=0, keepdims=True)
                put(s, jnp.where(total > 0.0, top + jnp.log2(jnp.maximum(total, 1e-37)), nothing))
                return carry

            lax.fori_loop(0, tiles, one_tile, 0)

    @pl.when(on_duty(which))
    def _():
        copy.start()
        load_weights(points_ref, weights_ref, None)
        copy.wait()
        pl.when(plan_ref[tiles + 3, 0] > 0)(work)


def column_pass(
    which, sheet_ref, points_ref, need_ref, w0, w1, w2, w3, lse_ref, mass_ref, other_ref, out_ref,
    operand_ref, weights_ref, plan_ref, sem, total_ref, high_ref, *buffers,
):
    tiles, depth, tile = weights_ref.shape
    out_ref[...] = other_ref[...]
    copy = pltpu.make_async_copy(sheet_ref, plan_ref, sem)

    def work():
        items = plan_ref[tiles + 3, 0]
        unpack_targets((w0, w1, w2, w3), operand_ref)
        total_ref[...] = jnp.zeros_like(total_ref)

        def visit(s, units, buffer):
            for k, u in enumerate(units):
                where = pl.ds(pl.multiple_of(u * unit_rows, unit_rows), unit_rows)
                part = jnp.exp2(buffer[k * unit_rows : (k + 1) * unit_rows, :])
                total_ref[where, :] += part[:, 0:128] + part[:, 128:256]

        pipeline(plan_ref, items, operand_ref, weights_ref, buffers, visit)
        eye = lax.broadcasted_iota(jnp.int32, (128, 128), 0) == lax.broadcasted_iota(
            jnp.int32, (128, 128), 1
        )

        def to_row(column):
            return jnp.sum(jnp.where(eye, column, 0.0), axis=0, keepdims=True)

        bad = jnp.zeros((1, 128), f32)
        for u in range(out_ref.shape[0]):
            sums = to_row(jnp.sum(total_ref[u * 128 : (u + 1) * 128, :], axis=1, keepdims=True))
            out_ref[u : u + 1, :] = jnp.where(
                sums > 0.0, jnp.log2(jnp.maximum(sums, 1e-37)), nothing
            )
            bad = jnp.maximum(bad, jnp.where(sums > 1e-25, 0.0, need_ref[u : u + 1, :]))

        @pl.when(jnp.max(bad) > 0.0)
        def _():
            total_ref[...] = jnp.zeros_like(total_ref)
            high_ref[...] = jnp.full_like(high_ref, floor)

            def one_tile(s, carry):
                def step(i, inner):
                    unit = plan_ref[s, i]
                    where = pl.ds(pl.multiple_of(unit * unit_rows, unit_rows), unit_rows)
                    score = jnp.dot(
                        operand_ref[where, :], weights_ref[s], preferred_element_type=f32
                    )
                    a, b = score[:, 0:128], score[:, 128:256]
                    old = high_ref[where, :]
                    new = jnp.maximum(old, jnp.maximum(a, b))
                    high_ref[where, :] = new
                    total_ref[where, :] = (
                        total_ref[where, :] * jnp.exp2(old - new)
                        + jnp.exp2(a - new)
                        + jnp.exp2(b - new)
                    )
                    return inner

                lax.fori_loop(0, plan_ref[s, 127], step, 0)
                return carry

            lax.fori_loop(0, tiles, one_tile, 0)

            def finish(u, carry):
                where = pl.ds(pl.multiple_of(u * 128, 128), 128)
                high = high_ref[where, :]
                top = jnp.max(high, axis=1, keepdims=True)
                rest = total_ref[where, :] * jnp.exp2(high - top)
                sums = to_row(jnp.sum(rest, axis=1, keepdims=True))
                out_ref[pl.ds(u, 1), :] = jnp.where(
                    sums > 0.0, to_row(top) + jnp.log2(jnp.maximum(sums, 1e-37)), nothing
                )
                return carry

            lax.fori_loop(0, out_ref.shape[0], finish, 0)

    @pl.when(on_duty(which))
    def _():
        copy.start()
        load_weights(points_ref, weights_ref, mass_ref[...] - lse_ref[...])
        copy.wait()
        pl.when(plan_ref[tiles + 3, 0] > 0)(work)


def log_sum(parts):
    top = functools.reduce(jnp.maximum, parts)
    total = sum(jnp.exp2(p - top) for p in parts)
    return top + jnp.log2(total)


def roles(parity, cols):
    four = [d % cols for d in ((-2, -1, 0, 1), (-1, 0, 1, 2))[parity]]
    lead = [0, (1, -1)[parity] % cols]
    near = lead + [d for d in four if d not in lead]
    out = [(2, -2)[parity] % cols, cols // 2]
    begin = four[0]
    out += [(begin + 5) % cols, (begin + 6) % cols]
    return near, out + [d for d in range(cols) if d not in near and d not in out]


def filled(hops, count, cols):
    found = dict(hops)
    back = {d: s for s, d in hops}
    for rank in range(4):
        free = [d for d in range(count) if d not in back]
        for s in [s for s in range(count) if s not in found]:
            if rank == 0:
                picks = [back[s]] if s in back and back[s] in free else []
            elif rank == 1:
                picks = [s ^ 1] if s ^ 1 in free else []
            else:
                picks = [d for d in free if d != s and (d // cols == s // cols or rank == 3)]
                picks.sort(key=lambda d: min((d - s) % cols, (s - d) % cols))
            if picks:
                found[s] = picks[0]
                back[picks[0]] = s
                free.remove(picks[0])
    return sorted(found.items())


def shards(src_points, dst_points, dst_potential, partners, partner_count, src_count, dst_count):
    src_tiles = src_count.shape[0]
    dst_tiles = dst_count.shape[0]
    tile = src_points.shape[0] // src_tiles
    slots = partners.shape[1]
    rows = lax.axis_size("row")
    cols = lax.axis_size("col")
    row_here = lax.axis_index("row")
    col_here = lax.axis_index("col")
    share = dst_points.shape[0]
    points = dst_tiles * tile
    smem = pl.BlockSpec(memory_space=pltpu.SMEM)
    vmem = pl.BlockSpec(memory_space=pltpu.VMEM)
    anywhere = pl.BlockSpec(memory_space=pl.ANY)
    params = pltpu.CompilerParams(vmem_limit_bytes=24 * 1024 * 1024)
    places = [roles(r % 2, cols) for r in range(rows)]
    near = [[(r + d) % cols for d in places[r][0]] for r in range(rows)]
    far = [[(r + d) % cols for d in places[r][1]] for r in range(rows)]
    parity = lax.rem(row_here, 2)
    apart = lax.rem(col_here - row_here + 2 - parity + cols, cols)
    in_near = apart < 4
    in_far = (
        (apart == 5)
        | (apart == 6)
        | (apart == jnp.where(parity == 0, 4, cols - 1))
        | (apart == jnp.where(parity == 0, 10, 9))
    )

    def send(a, hops, full=True):
        hops = [(s[0] * cols + s[1], d[0] * cols + d[1]) for s, d in hops]
        return lax.ppermute(a, ("row", "col"), filled(hops, rows * cols, cols) if full else hops)

    every = [(r, c) for r in range(rows) for c in range(cols)]

    wire = pl.pallas_call(
        pack_targets,
        out_shape=jax.ShapeDtypeStruct((share // 2 + 8, 128), f32),
        in_specs=[anywhere] * 3,
        out_specs=vmem,
        scratch_shapes=[
            pltpu.VMEM((128, 384), f32),
            pltpu.VMEM((8, 384), f32),
            pltpu.SMEM((dst_tiles,), jnp.int32),
            pltpu.VMEM((64, share), f32),
            pltpu.VMEM((share,), f32),
            pltpu.SemaphoreType.DMA((3,)),
        ],
        compiler_params=pltpu.CompilerParams(vmem_limit_bytes=60 * 1024 * 1024),
    )(dst_count, dst_points.T, dst_potential)

    def around(r, dx, dy):
        return (r // ring + dx) % ring * ring + (r + dy) % ring

    def first_hop(r, c, k):
        return around(r, 0, k) if c % 2 == 0 else around(r, k, 0)

    def second_hop(r, c, k):
        return around(r, k, 0) if c % 2 == 0 else around(r, 0, k)

    slot_on = jnp.arange(slots, dtype=jnp.int32)[None, :] < partner_count[:, None]
    local = jnp.where(slot_on, partners - col_here * dst_tiles, -1)
    plan, near_wire = pl.pallas_call(
        plan_work,
        out_shape=(
            jax.ShapeDtypeStruct((24, 128), jnp.int32),
            jax.ShapeDtypeStruct(wire.shape, f32),
        ),
        in_specs=[smem, vmem, anywhere],
        out_specs=(vmem, vmem),
        scratch_shapes=[pltpu.SemaphoreType.DMA],
        compiler_params=params,
    )(dst_count, jnp.pad(local, ((0, 24 - src_tiles), (0, 0)), constant_values=-1), wire)
    bundle = pl.pallas_call(
        join,
        out_shape=jax.ShapeDtypeStruct((ring,) + wire.shape, f32),
        in_specs=[vmem] * ring,
        out_specs=vmem,
        compiler_params=params,
    )(near_wire, *[send(wire, [((r, c), (first_hop(r, c, k), c)) for r, c in every]) for k in (1, 2, 3)])
    busy = [set(near[r] + far[r][:2]) for r in range(rows)]
    plan, local, dst_count, src_count, bundle = lax.optimization_barrier(
        (plan, local, dst_count, src_count, bundle)
    )
    wires = [bundle] + [
        send(
            bundle,
            [
                ((r, c), (second_hop(r, c, k), c))
                for r, c in every
                if c in busy[second_hop(r, c, k)]
            ],
            full=False,
        )
        for k in (1, 2, 3)
    ]
    place = jnp.arange(tile, dtype=jnp.int32)
    src_live = place[None, :] < src_count[:, None]
    dst_live = place[None, :] < dst_count[:, None]
    wanted = jnp.any(local[:, :, None] == jnp.arange(dst_tiles, dtype=jnp.int32), axis=1)
    src_need = jnp.where(src_live & jnp.any(wanted, axis=1)[:, None], 1.0, 0.0)
    dst_need = jnp.where(dst_live & jnp.any(wanted, axis=0)[:, None], 1.0, 0.0)
    dst_need = dst_need.reshape(points // 128, 128)
    counted = jnp.repeat(src_count.astype(f32), 2)
    half_live = (place[:128][None, :] + 128 * (jnp.arange(2 * src_tiles) % 2)[:, None]) < jnp.repeat(
        src_count, 2
    )[:, None]
    all_src = src_tiles * rows
    mass = jnp.where(half_live, -jnp.log2(counted)[:, None] - math.log2(all_src), nothing)

    scratch = [
        pltpu.VMEM((points + unit_rows, 256), bf16),
        pltpu.VMEM((src_tiles, 256, tile), bf16),
    ]
    buffers = [pltpu.VMEM((unit_rows * group, tile), f32)] * span
    heavy = pl.CostEstimate(flops=8_000_000_000, bytes_accessed=4_000_000, transcendentals=8_000_000)
    light = pl.CostEstimate(flops=100_000_000, bytes_accessed=100_000, transcendentals=100_000)
    turned = src_points.T

    halves = 2 * src_tiles
    scratch += [pltpu.SMEM((24, 128), jnp.int32), pltpu.SemaphoreType.DMA]

    def sum_rows(which, cost):
        return pl.pallas_call(
            functools.partial(row_pass, which),
            out_shape=jax.ShapeDtypeStruct((halves, tile // 2), f32),
            in_specs=[anywhere] + [vmem] * (2 + ring),
            out_specs=vmem,
            scratch_shapes=scratch + [pltpu.VMEM((src_tiles, 8, tile), f32)] + buffers,
            compiler_params=params,
            cost_estimate=cost,
        )(plan, turned, src_need, *wires)

    def sum_columns(which, lse, other, cost):
        return pl.pallas_call(
            functools.partial(column_pass, which),
            out_shape=jax.ShapeDtypeStruct((points // 128, 128), f32),
            in_specs=[anywhere] + [vmem] * (5 + ring),
            out_specs=vmem,
            scratch_shapes=scratch + [pltpu.VMEM((points + unit_rows, 128), f32)] * 2 + buffers,
            compiler_params=params,
            cost_estimate=cost,
        )(plan, turned, dst_need, *wires, lse, mass, other)

    far_lse = sum_rows(1, light)
    loops = [
        [(r, c) for c in (far[r][k], near[r][k], far[r][k] ^ 1)] for r in range(rows) for k in (0, 1)
    ]
    hops = [(loop[i], loop[(i + 1) % 3]) for loop in loops for i in range(3)]
    for r in range(rows):
        taken = near[r] + far[r][:2] + [c ^ 1 for c in far[r][:2]]
        spare = [c for c in range(cols) if c not in taken][:2]
        for a, c in zip(near[r][2:], spare):
            hops += [((r, a), (r, c)), ((r, c), (r, a))]
    early = send(far_lse, hops)
    near_lse = sum_rows(0, heavy)
    got_early = (col_here == row_here) | (col_here == row_here + 1 - 2 * parity)
    lse = log_sum([near_lse, jnp.where(got_early, early, nothing)])

    def pairs(test):
        return [((r, c), (r, d)) for r in range(rows) for c in near[r] for d in near[r] if test(c, d)]

    lse = log_sum(
        [
            lse,
            send(lse, [((r, c), (r, c ^ 1)) for r, c in every]),
            send(lse, pairs(lambda c, d: (c - d) % cols in (2, cols - 2))),
            send(lse, pairs(lambda c, d: (c - (d ^ 1)) % cols in (2, cols - 2))),
        ]
    )
    spread = send(lse, [((r, near[r][k]), (r, far[r][k])) for r in range(rows) for k in range(4)])
    blank = jnp.full((points // 128, 128), nothing, f32)
    near_part = sum_columns(0, lse, blank, heavy)
    col_part = sum_columns(1, spread, near_part, light)
    known = jnp.where(in_far, spread, lse)
    known, near_part = lax.optimization_barrier((known, near_part))
    rest = send(
        known,
        [((r, (near[r] + far[r])[k]), (r, far[r][4 + k])) for r in range(rows) for k in range(8)],
    )
    shared_out = lax.all_to_all(col_part.reshape(rows, share), "row", 0, 0)

    src_potential = pl.pallas_call(
        finish_sources,
        out_shape=jax.ShapeDtypeStruct((halves, tile // 2), f32),
        in_specs=[vmem] * 4,
        out_specs=vmem,
        compiler_params=params,
        cost_estimate=heavy,
    )(known, rest, mass, half_live.astype(f32)).reshape(-1)

    spot = row_here * share + jnp.arange(share, dtype=jnp.int32)
    spot_tile = spot // tile
    spot_count = jnp.sum(
        jnp.where(
            spot_tile[:, None] == jnp.arange(dst_tiles, dtype=jnp.int32)[None, :],
            dst_count[None, :],
            0,
        ),
        axis=1,
    )
    top = jnp.max(shared_out, axis=0)
    col_log = top + jnp.log2(jnp.sum(jnp.exp2(shared_out - top[None]), axis=0))
    dst_new = jnp.where(
        (spot - spot_tile * tile < spot_count) & (top > 0.5 * nothing),
        entropy
        * (-jnp.log(spot_count.astype(f32)) - math.log(dst_tiles * cols) - ln2 * col_log)
        + dst_potential,
        0.0,
    )
    return src_potential, dst_new


def solution(mesh):
    in_specs = (
        P("row", None),
        P(("col", "row"), None),
        P(("col", "row")),
        P("row", None),
        P("row"),
        P("row"),
        P("col"),
    )
    out_specs = (P("row"), P(("col", "row")))
    return jax.shard_map(shards, mesh=mesh, in_specs=in_specs, out_specs=out_specs, check_vma=False)
```

```python
import functools
import math

import jax
import jax.numpy as jnp
from jax import lax
from jax.experimental import pallas as pl
from jax.experimental.pallas import tpu as pltpu
from jax.sharding import PartitionSpec as P

entropy = 0.1
scale = math.log2(math.e) / entropy
ln2 = math.log(2.0)
nothing = -1e30
floor = -1e25
unit_rows = 64
group = 9
span = 10
ring = 4
f32 = jnp.float32
bf16 = jnp.bfloat16


def pieces(a):
    first = a.astype(bf16).astype(f32)
    rest = a - first
    second = rest.astype(bf16).astype(f32)
    return first, second, rest - second


def extra_rows(bias):
    place = lax.broadcasted_iota(jnp.int32, (64, bias.shape[1]), 0)
    block = jnp.where(place < 3, 1.0, 0.0)
    for k, piece in enumerate(pieces(bias)):
        block = jnp.where(place == 3 + k, piece, block)
    return block.astype(bf16)


def pack_targets(
    count_ref, points_ref, potential_ref, wire_ref, square_ref, line_ref, tally_ref, held_ref, level_ref, sems,
):
    copies = [
        pltpu.make_async_copy(source, target, sems.at[k])
        for k, (source, target) in enumerate(
            ((points_ref, held_ref), (potential_ref, level_ref), (count_ref, tally_ref))
        )
    ]
    for copy in copies:
        copy.start()
    share = held_ref.shape[1]
    tile = 256
    mid = share // 2
    begin = lax.axis_index("row") * share
    first_tile = begin // tile
    offset = begin - first_tile * tile
    last_tile = jnp.minimum(first_tile + 1, tally_ref.shape[0] - 1)
    square_ref[...] = jnp.zeros_like(square_ref)
    line_ref[...] = jnp.full_like(line_ref, nothing)
    wire_ref[mid : mid + 8, :] = jnp.zeros((8, 128), f32)
    for copy in copies:
        copy.wait()
    points = held_ref[...]
    square_ref[0:64, 0:share] = points
    turned = square_ref[...].T
    wire_ref[0:mid, :] = scale * (turned[0:mid] + pltpu.roll(turned[mid:share], 64, 1))
    level = level_ref[...].reshape(1, share)
    level = scale * (level - 0.5 * jnp.sum(points * points, axis=0, keepdims=True))
    spot = offset + lax.broadcasted_iota(jnp.int32, (1, share), 1)
    place = jnp.where(spot < tile, spot, spot - tile)
    bound = jnp.where(spot < tile, tally_ref[first_tile], tally_ref[last_tile])
    line_ref[0:1, 0:share] = jnp.where(place < bound, level, nothing)
    for k in range(3):
        wire_ref[mid + k : mid + k + 1, :] = line_ref[0:1, 128 * k : 128 * (k + 1)]


def join(a_ref, b_ref, c_ref, d_ref, out_ref):
    for k, ref in enumerate((a_ref, b_ref, c_ref, d_ref)):
        out_ref[k] = ref[...]


def unpack_targets(wires, operand_ref):
    lane = lax.broadcasted_iota(jnp.int32, (144, 128), 1)
    front = lane < 64
    sublane = lax.broadcasted_iota(jnp.int32, (16, 384), 0)
    pick_row = lax.broadcasted_iota(jnp.int32, (16, 128), 0)
    pick_lane = lax.broadcasted_iota(jnp.int32, (16, 128), 1)
    pick = jnp.where((pick_lane == pick_row + 64) & (pick_row < 6), 1.0, 0.0).astype(bf16)
    row_here = lax.axis_index("row")
    x_here = row_here // ring
    y_here = row_here - x_here * ring
    even = lax.rem(lax.axis_index("col"), 2) == 0
    for k in range(ring):
        for j in range(ring):
            x = lax.rem(x_here + ring - jnp.where(even, k, j), ring)
            y = lax.rem(y_here + ring - jnp.where(even, j, k), ring)
            a = pl.multiple_of((x * ring + y) * 288, 16)
            b = pl.multiple_of((x * ring + y) * 288 + 144, 16)
            both = wires[k][j, 0:144, :]
            high = both.astype(bf16).astype(f32)
            low = both - high
            high_back = pltpu.roll(high, 64, 1)
            low_back = pltpu.roll(low, 64, 1)
            tail = wires[k][j, 144:152, :]
            line = jnp.concatenate([tail[0:1], tail[1:2], tail[2:3]], axis=1)
            stacked = jnp.where(sublane < 6, 1.0, 0.0)
            for i, piece in enumerate(pieces(line)):
                stacked = jnp.where(sublane == i, piece, stacked)
            extra = lax.dot_general(
                stacked.astype(bf16), pick, (((0,), (0,)), ((), ())), preferred_element_type=f32
            )
            operand_ref[pl.ds(a, 144), 0:128] = jnp.where(front, high, low_back).astype(bf16)
            operand_ref[pl.ds(a, 144), 128:256] = jnp.where(front, high, extra[0:144]).astype(bf16)
            operand_ref[pl.ds(b, 144), 0:128] = jnp.where(front, high_back, low).astype(bf16)
            operand_ref[pl.ds(b, 144), 128:256] = jnp.where(
                front, high_back, extra[144:288]
            ).astype(bf16)
    rows = ring * ring * 288
    dummy_lane = lax.broadcasted_iota(jnp.int32, (unit_rows, 256), 1)
    operand_ref[rows : rows + unit_rows, :] = jnp.where(dummy_lane == 192, nothing, 0.0).astype(bf16)


def load_weights(points_ref, weights_ref, shift):
    tiles, depth, tile = weights_ref.shape
    for s in range(tiles):
        x = points_ref[:, s * tile : (s + 1) * tile]
        high = x.astype(bf16)
        low = (x - high.astype(f32)).astype(bf16)
        bias = (-0.5 * scale) * jnp.sum(x * x, axis=0, keepdims=True)
        moved = 0.0
        if shift is not None:
            moved = jnp.concatenate([shift[2 * s : 2 * s + 1], shift[2 * s + 1 : 2 * s + 2]], axis=1)
        weights_ref[s, 0:64, :] = high
        weights_ref[s, 64:128, :] = high
        weights_ref[s, 128:192, :] = low
        weights_ref[s, 192:256, :] = extra_rows(bias + moved)


def plan_work(count_ref, local_ref, wire_ref, plan_ref, near_wire_ref, sem):
    copy = pltpu.make_async_copy(wire_ref, near_wire_ref, sem)
    copy.start()
    src_tiles = local_ref.shape[0] - 6
    per_tile = 256 // unit_rows
    units = count_ref.shape[0] * per_tile
    per = units // group
    unit = lax.broadcasted_iota(jnp.int32, (24, 128), 1)
    tile_of = unit // per_tile
    bound = jnp.zeros((24, 128), jnp.int32)
    for t in range(count_ref.shape[0]):
        bound = jnp.where(tile_of == t, count_ref[t], bound)
    live = bound > (unit - tile_of * per_tile) * unit_rows
    hits = jnp.zeros((24, 128), f32)
    for k in range(local_ref.shape[1]):
        hits = jnp.where(local_ref[:, k : k + 1] == tile_of, 1.0, hits)
    active = jnp.where(live, hits, 0.0)
    down = lax.broadcasted_iota(jnp.int32, (128, 128), 0)
    across = lax.broadcasted_iota(jnp.int32, (128, 128), 1)
    upto = jnp.where(down <= across, 1.0, 0.0).astype(bf16)
    rank = jnp.dot(active.astype(bf16), upto, preferred_element_type=f32)
    counts = jnp.broadcast_to(rank[:, 127:128], (24, 128))
    place = jnp.where(active > 0.0, rank - 1.0, -1.0)
    place = jnp.concatenate([place, jnp.full((104, 128), -1.0, f32)], axis=0).T
    position = across.astype(f32)
    value = (down - units).astype(f32)
    plan_ref[...] = jnp.full_like(plan_ref, units)
    last = lax.broadcasted_iota(jnp.int32, (1, 128), 1)
    chunks = jnp.floor((counts + (group - 0.5)) / group).astype(jnp.int32)
    begin = jnp.zeros((1, 128), jnp.int32)
    items = [jnp.full((1, 128), src_tiles * per, jnp.int32)] * 2
    for s in range(src_tiles):
        listed = jnp.sum(
            jnp.where(place[:, s : s + 1] == position, value, 0.0), axis=0, keepdims=True
        )
        plan_ref[s : s + 1, :] = jnp.where(
            last == 127, counts[s : s + 1], listed + units
        ).astype(jnp.int32)
        for k in range(2):
            along = last + 128 * k - begin
            inside = (along >= 0) & (along < chunks[s : s + 1])
            items[k] = jnp.where(inside, s * per + along, items[k])
        begin = begin + chunks[s : s + 1]
    plan_ref[src_tiles + 1 : src_tiles + 2, :] = items[0]
    plan_ref[src_tiles + 2 : src_tiles + 3, :] = items[1]
    plan_ref[src_tiles + 3 : src_tiles + 4, :] = begin
    copy.wait()


def pipeline(plan_ref, items, operand_ref, weights_ref, buffers, visit):
    tiles, depth, tile = weights_ref.shape
    per = (operand_ref.shape[0] // unit_rows - 1) // group

    def where(i):
        code = plan_ref[tiles + 1 + i // 128, lax.rem(i, 128)]
        s = code // per
        first = (code - s * per) * group
        return jnp.minimum(s, tiles - 1), [plan_ref[s, first + k] for k in range(group)]

    def step(j, carry):
        for k in range(span):
            s, units = where(span * j + k)
            rows = jnp.concatenate(
                [
                    operand_ref[pl.ds(pl.multiple_of(u * unit_rows, unit_rows), unit_rows), :]
                    for u in units
                ],
                axis=0,
            )
            buffers[k][...] = jnp.dot(rows, weights_ref[s], preferred_element_type=f32)
        for k in range(span):
            visit(*where(span * j + k), buffers[k])
        return carry

    lax.fori_loop(0, (items + span - 1) // span, step, 0)


def distance():
    row = lax.axis_index("row")
    return lax.rem(lax.axis_index("col") - row + 2 - lax.rem(row, 2) + 16, 16)


def on_duty(which):
    near = distance() < 4
    return near if which == 0 else jnp.logical_not(near)


def finish_sources(known_ref, rest_ref, mass_ref, live_ref, out_ref):
    apart = distance()
    odd = lax.rem(lax.axis_index("row"), 2) == 1
    here = (apart < 4) | (apart == 5) | (apart == 6)
    here |= (apart == jnp.where(odd, 15, 4)) | (apart == jnp.where(odd, 9, 10))
    total = jnp.where(here, known_ref[...], rest_ref[...])
    out_ref[...] = jnp.where(
        live_ref[...] > 0.0, (entropy * ln2) * (mass_ref[...] - total), 0.0
    )


def row_pass(
    which, sheet_ref, points_ref, need_ref, w0, w1, w2, w3, lse_ref,
    operand_ref, weights_ref, plan_ref, sem, total_ref, *buffers,
):
    tiles, depth, tile = weights_ref.shape
    lse_ref[...] = jnp.full_like(lse_ref, nothing)
    copy = pltpu.make_async_copy(sheet_ref, plan_ref, sem)

    def put(s, line):
        lse_ref[pl.ds(2 * s, 1), :] = line[:, 0:128]
        lse_ref[pl.ds(2 * s + 1, 1), :] = line[:, 128:256]

    def work():
        items = plan_ref[tiles + 3, 0]
        unpack_targets((w0, w1, w2, w3), operand_ref)
        total_ref[...] = jnp.zeros_like(total_ref)

        def visit(s, units, buffer):
            part = jnp.exp2(buffer[...]).reshape(4, unit_rows * group // 32, 8, tile)
            total_ref[s] += jnp.sum(jnp.sum(part, axis=1), axis=0)

        pipeline(plan_ref, items, operand_ref, weights_ref, buffers, visit)
        total = jnp.sum(total_ref[...], axis=1)
        lines = jnp.where(total > 0.0, jnp.log2(jnp.maximum(total, 1e-37)), nothing)
        for s in range(tiles):
            put(s, lines[s : s + 1, :])
        fine = (total > 1e-25) & (total < 1e30)
        bad = jnp.where(fine, 0.0, need_ref[...])

        @pl.when(jnp.max(bad) > 0.0)
        def _():
            def one_tile(s, carry):
                weights = weights_ref[s]

                def step(i, state):
                    high, total = state
                    unit = plan_ref[s, i]
                    rows = operand_ref[
                        pl.ds(pl.multiple_of(unit * unit_rows, unit_rows), unit_rows), :
                    ]
                    score = jnp.dot(rows, weights, preferred_element_type=f32)
                    score = score.reshape(unit_rows // 8, 8, tile)
                    new = jnp.maximum(high, jnp.max(score, axis=0))
                    total = total * jnp.exp2(high - new)
                    return new, total + jnp.sum(jnp.exp2(score - new[None]), axis=0)

                start = (jnp.full((8, tile), floor, f32), jnp.zeros((8, tile), f32))
                high, total = lax.fori_loop(0, plan_ref[s, 127], step, start)
                top = jnp.max(high, axis=0, keepdims=True)
                total = jnp.sum(total * jnp.exp2(high - top), axis=0, keepdims=True)
                put(s, jnp.where(total > 0.0, top + jnp.log2(jnp.maximum(total, 1e-37)), nothing))
                return carry

            lax.fori_loop(0, tiles, one_tile, 0)

    @pl.when(on_duty(which))
    def _():
        copy.start()
        load_weights(points_ref, weights_ref, None)
        copy.wait()
        pl.when(plan_ref[tiles + 3, 0] > 0)(work)


def column_pass(
    which, sheet_ref, points_ref, need_ref, w0, w1, w2, w3, lse_ref, mass_ref, other_ref, out_ref,
    operand_ref, weights_ref, plan_ref, sem, total_ref, high_ref, *buffers,
):
    tiles, depth, tile = weights_ref.shape
    out_ref[...] = other_ref[...]
    copy = pltpu.make_async_copy(sheet_ref, plan_ref, sem)

    def work():
        items = plan_ref[tiles + 3, 0]
        unpack_targets((w0, w1, w2, w3), operand_ref)
        total_ref[...] = jnp.zeros_like(total_ref)

        def visit(s, units, buffer):
            for k, u in enumerate(units):
                where = pl.ds(pl.multiple_of(u * unit_rows, unit_rows), unit_rows)
                part = jnp.exp2(buffer[k * unit_rows : (k + 1) * unit_rows, :])
                total_ref[where, :] += part[:, 0:128] + part[:, 128:256]

        pipeline(plan_ref, items, operand_ref, weights_ref, buffers, visit)
        eye = lax.broadcasted_iota(jnp.int32, (128, 128), 0) == lax.broadcasted_iota(
            jnp.int32, (128, 128), 1
        )

        def to_row(column):
            return jnp.sum(
                jnp.where(eye[0 : column.shape[0]], column, 0.0), axis=0, keepdims=True
            )

        blocks = [
            (shard, slice(128 * i, 128 * i + size), slice(shard * 288 + 128 * i, shard * 288 + 128 * i + size))
            for shard in range(out_ref.shape[0])
            for i, size in enumerate((128, 128, 32))
        ]
        bad = jnp.zeros((1, 128), f32)
        for shard, lanes, where in blocks:
            sums = to_row(jnp.sum(total_ref[where, :], axis=1, keepdims=True))
            size = lanes.stop - lanes.start
            out_ref[shard, :, lanes] = jnp.where(
                sums > 0.0, jnp.log2(jnp.maximum(sums, 1e-37)), nothing
            )[:, 0:size]
            needed = need_ref[3 * shard + lanes.start // 128 : 3 * shard + lanes.start // 128 + 1, :]
            bad = jnp.maximum(bad, jnp.where(sums > 1e-25, 0.0, needed))

        @pl.when(jnp.max(bad) > 0.0)
        def _():
            total_ref[...] = jnp.zeros_like(total_ref)
            high_ref[...] = jnp.full_like(high_ref, floor)

            def one_tile(s, carry):
                def step(i, inner):
                    unit = plan_ref[s, i]
                    where = pl.ds(pl.multiple_of(unit * unit_rows, unit_rows), unit_rows)
                    score = jnp.dot(
                        operand_ref[where, :], weights_ref[s], preferred_element_type=f32
                    )
                    a, b = score[:, 0:128], score[:, 128:256]
                    old = high_ref[where, :]
                    new = jnp.maximum(old, jnp.maximum(a, b))
                    high_ref[where, :] = new
                    total_ref[where, :] = (
                        total_ref[where, :] * jnp.exp2(old - new)
                        + jnp.exp2(a - new)
                        + jnp.exp2(b - new)
                    )
                    return inner

                lax.fori_loop(0, plan_ref[s, 127], step, 0)
                return carry

            lax.fori_loop(0, tiles, one_tile, 0)

            for shard, lanes, where in blocks:
                high = high_ref[where, :]
                top = jnp.max(high, axis=1, keepdims=True)
                rest = total_ref[where, :] * jnp.exp2(high - top)
                sums = to_row(jnp.sum(rest, axis=1, keepdims=True))
                size = lanes.stop - lanes.start
                out_ref[shard, :, lanes] = jnp.where(
                    sums > 0.0, to_row(top) + jnp.log2(jnp.maximum(sums, 1e-37)), nothing
                )[:, 0:size]

    @pl.when(on_duty(which))
    def _():
        copy.start()
        load_weights(points_ref, weights_ref, mass_ref[...] - lse_ref[...])
        copy.wait()
        pl.when(plan_ref[tiles + 3, 0] > 0)(work)


def log_sum(parts):
    top = functools.reduce(jnp.maximum, parts)
    total = sum(jnp.exp2(p - top) for p in parts)
    return top + jnp.log2(total)


def roles(parity, cols):
    four = [d % cols for d in ((-2, -1, 0, 1), (-1, 0, 1, 2))[parity]]
    lead = [0, (1, -1)[parity] % cols]
    near = lead + [d for d in four if d not in lead]
    out = [(2, -2)[parity] % cols, cols // 2]
    begin = four[0]
    out += [(begin + 5) % cols, (begin + 6) % cols]
    return near, out + [d for d in range(cols) if d not in near and d not in out]


def filled(hops, count, cols):
    found = dict(hops)
    back = {d: s for s, d in hops}
    for rank in range(4):
        free = [d for d in range(count) if d not in back]
        for s in [s for s in range(count) if s not in found]:
            if rank == 0:
                picks = [back[s]] if s in back and back[s] in free else []
            elif rank == 1:
                picks = [s ^ 1] if s ^ 1 in free else []
            else:
                picks = [d for d in free if d != s and (d // cols == s // cols or rank == 3)]
                picks.sort(key=lambda d: min((d - s) % cols, (s - d) % cols))
            if picks:
                found[s] = picks[0]
                back[picks[0]] = s
                free.remove(picks[0])
    return sorted(found.items())


def shards(src_points, dst_points, dst_potential, partners, partner_count, src_count, dst_count):
    src_tiles = src_count.shape[0]
    dst_tiles = dst_count.shape[0]
    tile = src_points.shape[0] // src_tiles
    slots = partners.shape[1]
    rows = lax.axis_size("row")
    cols = lax.axis_size("col")
    row_here = lax.axis_index("row")
    col_here = lax.axis_index("col")
    share = dst_points.shape[0]
    points = dst_tiles * tile
    smem = pl.BlockSpec(memory_space=pltpu.SMEM)
    vmem = pl.BlockSpec(memory_space=pltpu.VMEM)
    anywhere = pl.BlockSpec(memory_space=pl.ANY)
    params = pltpu.CompilerParams(vmem_limit_bytes=24 * 1024 * 1024)
    places = [roles(r % 2, cols) for r in range(rows)]
    near = [[(r + d) % cols for d in places[r][0]] for r in range(rows)]
    far = [[(r + d) % cols for d in places[r][1]] for r in range(rows)]
    parity = lax.rem(row_here, 2)
    apart = lax.rem(col_here - row_here + 2 - parity + cols, cols)
    in_near = apart < 4
    in_far = (
        (apart == 5)
        | (apart == 6)
        | (apart == jnp.where(parity == 0, 4, cols - 1))
        | (apart == jnp.where(parity == 0, 10, 9))
    )

    def send(a, hops, full=True):
        hops = [(s[0] * cols + s[1], d[0] * cols + d[1]) for s, d in hops]
        return lax.ppermute(a, ("row", "col"), filled(hops, rows * cols, cols) if full else hops)

    every = [(r, c) for r in range(rows) for c in range(cols)]

    wire = pl.pallas_call(
        pack_targets,
        out_shape=jax.ShapeDtypeStruct((share // 2 + 8, 128), f32),
        in_specs=[anywhere] * 3,
        out_specs=vmem,
        scratch_shapes=[
            pltpu.VMEM((128, 384), f32),
            pltpu.VMEM((8, 384), f32),
            pltpu.SMEM((dst_tiles,), jnp.int32),
            pltpu.VMEM((64, share), f32),
            pltpu.VMEM((share,), f32),
            pltpu.SemaphoreType.DMA((3,)),
        ],
        compiler_params=pltpu.CompilerParams(vmem_limit_bytes=60 * 1024 * 1024),
    )(dst_count, dst_points.T, dst_potential)

    def around(r, dx, dy):
        return (r // ring + dx) % ring * ring + (r + dy) % ring

    def first_hop(r, c, k):
        return around(r, 0, k) if c % 2 == 0 else around(r, k, 0)

    def second_hop(r, c, k):
        return around(r, k, 0) if c % 2 == 0 else around(r, 0, k)

    slot_on = jnp.arange(slots, dtype=jnp.int32)[None, :] < partner_count[:, None]
    local = jnp.where(slot_on, partners - col_here * dst_tiles, -1)
    plan, near_wire = pl.pallas_call(
        plan_work,
        out_shape=(
            jax.ShapeDtypeStruct((24, 128), jnp.int32),
            jax.ShapeDtypeStruct(wire.shape, f32),
        ),
        in_specs=[smem, vmem, anywhere],
        out_specs=(vmem, vmem),
        scratch_shapes=[pltpu.SemaphoreType.DMA],
        compiler_params=params,
    )(dst_count, jnp.pad(local, ((0, 24 - src_tiles), (0, 0)), constant_values=-1), wire)
    bundle = pl.pallas_call(
        join,
        out_shape=jax.ShapeDtypeStruct((ring,) + wire.shape, f32),
        in_specs=[vmem] * ring,
        out_specs=vmem,
        compiler_params=params,
    )(near_wire, *[send(wire, [((r, c), (first_hop(r, c, k), c)) for r, c in every]) for k in (1, 2, 3)])
    busy = [set(near[r] + far[r][:2]) for r in range(rows)]
    plan, local, dst_count, src_count, bundle = lax.optimization_barrier(
        (plan, local, dst_count, src_count, bundle)
    )
    wires = [bundle] + [
        send(
            bundle,
            [
                ((r, c), (second_hop(r, c, k), c))
                for r, c in every
                if c in busy[second_hop(r, c, k)]
            ],
            full=False,
        )
        for k in (1, 2, 3)
    ]
    place = jnp.arange(tile, dtype=jnp.int32)
    src_live = place[None, :] < src_count[:, None]
    dst_live = place[None, :] < dst_count[:, None]
    wanted = jnp.any(local[:, :, None] == jnp.arange(dst_tiles, dtype=jnp.int32), axis=1)
    src_need = jnp.where(src_live & jnp.any(wanted, axis=1)[:, None], 1.0, 0.0)
    dst_need = jnp.where(dst_live & jnp.any(wanted, axis=0)[:, None], 1.0, 0.0)
    dst_need = jnp.pad(dst_need.reshape(rows, share), ((0, 0), (0, 384 - share)))
    dst_need = dst_need.reshape(rows * 3, 128)
    counted = jnp.repeat(src_count.astype(f32), 2)
    half_live = (place[:128][None, :] + 128 * (jnp.arange(2 * src_tiles) % 2)[:, None]) < jnp.repeat(
        src_count, 2
    )[:, None]
    all_src = src_tiles * rows
    mass = jnp.where(half_live, -jnp.log2(counted)[:, None] - math.log2(all_src), nothing)

    scratch = [
        pltpu.VMEM((points + unit_rows, 256), bf16),
        pltpu.VMEM((src_tiles, 256, tile), bf16),
    ]
    buffers = [pltpu.VMEM((unit_rows * group, tile), f32)] * span
    heavy = pl.CostEstimate(flops=8_000_000_000, bytes_accessed=4_000_000, transcendentals=8_000_000)
    light = pl.CostEstimate(flops=100_000_000, bytes_accessed=100_000, transcendentals=100_000)
    turned = src_points.T

    halves = 2 * src_tiles
    scratch += [pltpu.SMEM((24, 128), jnp.int32), pltpu.SemaphoreType.DMA]

    def sum_rows(which, cost):
        return pl.pallas_call(
            functools.partial(row_pass, which),
            out_shape=jax.ShapeDtypeStruct((halves, tile // 2), f32),
            in_specs=[anywhere] + [vmem] * (2 + ring),
            out_specs=vmem,
            scratch_shapes=scratch + [pltpu.VMEM((src_tiles, 8, tile), f32)] + buffers,
            compiler_params=params,
            cost_estimate=cost,
        )(plan, turned, src_need, *wires)

    def sum_columns(which, lse, other, cost):
        return pl.pallas_call(
            functools.partial(column_pass, which),
            out_shape=jax.ShapeDtypeStruct((rows, 1, share), f32),
            in_specs=[anywhere] + [vmem] * (5 + ring),
            out_specs=vmem,
            scratch_shapes=scratch + [pltpu.VMEM((points + unit_rows, 128), f32)] * 2 + buffers,
            compiler_params=params,
            cost_estimate=cost,
        )(plan, turned, dst_need, *wires, lse, mass, other)

    far_lse = sum_rows(1, light)
    loops = [
        [(r, c) for c in (far[r][k], near[r][k], far[r][k] ^ 1)] for r in range(rows) for k in (0, 1)
    ]
    hops = [(loop[i], loop[(i + 1) % 3]) for loop in loops for i in range(3)]
    for r in range(rows):
        taken = near[r] + far[r][:2] + [c ^ 1 for c in far[r][:2]]
        spare = [c for c in range(cols) if c not in taken][:2]
        for a, c in zip(near[r][2:], spare):
            hops += [((r, a), (r, c)), ((r, c), (r, a))]
    early = send(far_lse, hops)
    near_lse = sum_rows(0, heavy)
    got_early = (col_here == row_here) | (col_here == row_here + 1 - 2 * parity)
    lse = log_sum([near_lse, jnp.where(got_early, early, nothing)])

    def pairs(test):
        return [((r, c), (r, d)) for r in range(rows) for c in near[r] for d in near[r] if test(c, d)]

    lse = log_sum(
        [
            lse,
            send(lse, [((r, c), (r, c ^ 1)) for r, c in every]),
            send(lse, pairs(lambda c, d: (c - d) % cols in (2, cols - 2))),
            send(lse, pairs(lambda c, d: (c - (d ^ 1)) % cols in (2, cols - 2))),
        ]
    )
    spread = send(lse, [((r, near[r][k]), (r, far[r][k])) for r in range(rows) for k in range(4)])
    blank = jnp.full((rows, 1, share), nothing, f32)
    near_part = sum_columns(0, lse, blank, heavy)
    col_part = sum_columns(1, spread, near_part, light)
    known = jnp.where(in_far, spread, lse)
    known, near_part = lax.optimization_barrier((known, near_part))
    rest = send(
        known,
        [((r, (near[r] + far[r])[k]), (r, far[r][4 + k])) for r in range(rows) for k in range(8)],
    )
    shared_out = lax.all_to_all(col_part, "row", 0, 0)[:, 0]

    src_potential = pl.pallas_call(
        finish_sources,
        out_shape=jax.ShapeDtypeStruct((halves, tile // 2), f32),
        in_specs=[vmem] * 4,
        out_specs=vmem,
        compiler_params=params,
        cost_estimate=heavy,
    )(known, rest, mass, half_live.astype(f32)).reshape(-1)

    src_potential, dst_potential = lax.optimization_barrier((src_potential, dst_potential))
    spot = row_here * share + jnp.arange(share, dtype=jnp.int32)
    spot_tile = spot // tile
    spot_count = jnp.sum(
        jnp.where(
            spot_tile[:, None] == jnp.arange(dst_tiles, dtype=jnp.int32)[None, :],
            dst_count[None, :],
            0,
        ),
        axis=1,
    )
    top = jnp.max(shared_out, axis=0)
    col_log = top + jnp.log2(jnp.sum(jnp.exp2(shared_out - top[None]), axis=0))
    dst_new = jnp.where(
        (spot - spot_tile * tile < spot_count) & (top > 0.5 * nothing),
        entropy
        * (-jnp.log(spot_count.astype(f32)) - math.log(dst_tiles * cols) - ln2 * col_log)
        + dst_potential,
        0.0,
    )
    return src_potential, dst_new


def solution(mesh):
    in_specs = (
        P("row", None),
        P(("col", "row"), None),
        P(("col", "row")),
        P("row", None),
        P("row"),
        P("row"),
        P("col"),
    )
    out_specs = (P("row"), P(("col", "row")))
    return jax.shard_map(shards, mesh=mesh, in_specs=in_specs, out_specs=out_specs, check_vma=False)
```

```python
import functools
import math

import jax
import jax.numpy as jnp
from jax import lax
from jax.experimental import pallas as pl
from jax.experimental.pallas import tpu as pltpu
from jax.sharding import PartitionSpec as P

entropy = 0.1
scale = math.log2(math.e) / entropy
ln2 = math.log(2.0)
nothing = -1e30
floor = -1e25
unit_rows = 64
group = 9
span = 10
ring = 4
f32 = jnp.float32
bf16 = jnp.bfloat16


def pieces(a):
    first = a.astype(bf16).astype(f32)
    rest = a - first
    second = rest.astype(bf16).astype(f32)
    return first, second, rest - second


def extra_rows(bias):
    place = lax.broadcasted_iota(jnp.int32, (64, bias.shape[1]), 0)
    block = jnp.where(place < 3, 1.0, 0.0)
    for k, piece in enumerate(pieces(bias)):
        block = jnp.where(place == 3 + k, piece, block)
    return block.astype(bf16)


def pack_targets(
    count_ref, points_ref, potential_ref, wire_ref, square_ref, line_ref, tally_ref, held_ref, level_ref, sems,
):
    copies = [
        pltpu.make_async_copy(source, target, sems.at[k])
        for k, (source, target) in enumerate(
            ((points_ref, held_ref), (potential_ref, level_ref), (count_ref, tally_ref))
        )
    ]
    for copy in copies:
        copy.start()
    share = held_ref.shape[1]
    tile = 256
    mid = share // 2
    begin = lax.axis_index("row") * share
    first_tile = begin // tile
    offset = begin - first_tile * tile
    last_tile = jnp.minimum(first_tile + 1, tally_ref.shape[0] - 1)
    square_ref[...] = jnp.zeros_like(square_ref)
    line_ref[...] = jnp.full_like(line_ref, nothing)
    wire_ref[mid : mid + 8, :] = jnp.zeros((8, 128), f32)
    for copy in copies:
        copy.wait()
    points = held_ref[...]
    square_ref[0:64, 0:share] = points
    turned = square_ref[...].T
    wire_ref[0:mid, :] = scale * (turned[0:mid] + pltpu.roll(turned[mid:share], 64, 1))
    level = level_ref[...].reshape(1, share)
    level = scale * (level - 0.5 * jnp.sum(points * points, axis=0, keepdims=True))
    spot = offset + lax.broadcasted_iota(jnp.int32, (1, share), 1)
    place = jnp.where(spot < tile, spot, spot - tile)
    bound = jnp.where(spot < tile, tally_ref[first_tile], tally_ref[last_tile])
    line_ref[0:1, 0:share] = jnp.where(place < bound, level, nothing)
    for k in range(3):
        wire_ref[mid + k : mid + k + 1, :] = line_ref[0:1, 128 * k : 128 * (k + 1)]


def join(a_ref, b_ref, c_ref, d_ref, out_ref):
    for k, ref in enumerate((a_ref, b_ref, c_ref, d_ref)):
        out_ref[k] = ref[...]


def unpack_targets(wires, operand_ref):
    lane = lax.broadcasted_iota(jnp.int32, (144, 128), 1)
    front = lane < 64
    sublane = lax.broadcasted_iota(jnp.int32, (16, 384), 0)
    pick_row = lax.broadcasted_iota(jnp.int32, (16, 128), 0)
    pick_lane = lax.broadcasted_iota(jnp.int32, (16, 128), 1)
    pick = jnp.where((pick_lane == pick_row + 64) & (pick_row < 6), 1.0, 0.0).astype(bf16)
    row_here = lax.axis_index("row")
    x_here = row_here // ring
    y_here = row_here - x_here * ring
    even = lax.rem(lax.axis_index("col"), 2) == 0
    for k in range(ring):
        for j in range(ring):
            x = lax.rem(x_here + ring - jnp.where(even, k, j), ring)
            y = lax.rem(y_here + ring - jnp.where(even, j, k), ring)
            a = pl.multiple_of((x * ring + y) * 288, 16)
            b = pl.multiple_of((x * ring + y) * 288 + 144, 16)
            both = wires[k][j, 0:144, :]
            high = both.astype(bf16).astype(f32)
            low = both - high
            high_back = pltpu.roll(high, 64, 1)
            low_back = pltpu.roll(low, 64, 1)
            tail = wires[k][j, 144:152, :]
            line = jnp.concatenate([tail[0:1], tail[1:2], tail[2:3]], axis=1)
            stacked = jnp.where(sublane < 6, 1.0, 0.0)
            for i, piece in enumerate(pieces(line)):
                stacked = jnp.where(sublane == i, piece, stacked)
            extra = lax.dot_general(
                stacked.astype(bf16), pick, (((0,), (0,)), ((), ())), preferred_element_type=f32
            )
            operand_ref[pl.ds(a, 144), 0:128] = jnp.where(front, high, low_back).astype(bf16)
            operand_ref[pl.ds(a, 144), 128:256] = jnp.where(front, high, extra[0:144]).astype(bf16)
            operand_ref[pl.ds(b, 144), 0:128] = jnp.where(front, high_back, low).astype(bf16)
            operand_ref[pl.ds(b, 144), 128:256] = jnp.where(
                front, high_back, extra[144:288]
            ).astype(bf16)
    rows = ring * ring * 288
    dummy_lane = lax.broadcasted_iota(jnp.int32, (unit_rows, 256), 1)
    operand_ref[rows : rows + unit_rows, :] = jnp.where(dummy_lane == 192, nothing, 0.0).astype(bf16)


def load_weights(points_ref, weights_ref, shift):
    tiles, depth, tile = weights_ref.shape
    for s in range(tiles):
        x = points_ref[:, s * tile : (s + 1) * tile]
        high = x.astype(bf16)
        low = (x - high.astype(f32)).astype(bf16)
        bias = (-0.5 * scale) * jnp.sum(x * x, axis=0, keepdims=True)
        moved = 0.0
        if shift is not None:
            moved = jnp.concatenate([shift[2 * s : 2 * s + 1], shift[2 * s + 1 : 2 * s + 2]], axis=1)
        weights_ref[s, 0:64, :] = high
        weights_ref[s, 64:128, :] = high
        weights_ref[s, 128:192, :] = low
        weights_ref[s, 192:256, :] = extra_rows(bias + moved)


def plan_work(count_ref, local_ref, wire_ref, plan_ref, near_wire_ref, sem):
    copy = pltpu.make_async_copy(wire_ref, near_wire_ref, sem)
    copy.start()
    src_tiles = local_ref.shape[0] - 6
    per_tile = 256 // unit_rows
    units = count_ref.shape[0] * per_tile
    per = units // group
    unit = lax.broadcasted_iota(jnp.int32, (24, 128), 1)
    tile_of = unit // per_tile
    bound = jnp.zeros((24, 128), jnp.int32)
    for t in range(count_ref.shape[0]):
        bound = jnp.where(tile_of == t, count_ref[t], bound)
    live = bound > (unit - tile_of * per_tile) * unit_rows
    hits = jnp.zeros((24, 128), f32)
    for k in range(local_ref.shape[1]):
        hits = jnp.where(local_ref[:, k : k + 1] == tile_of, 1.0, hits)
    active = jnp.where(live, hits, 0.0)
    down = lax.broadcasted_iota(jnp.int32, (128, 128), 0)
    across = lax.broadcasted_iota(jnp.int32, (128, 128), 1)
    upto = jnp.where(down <= across, 1.0, 0.0).astype(bf16)
    rank = jnp.dot(active.astype(bf16), upto, preferred_element_type=f32)
    counts = jnp.broadcast_to(rank[:, 127:128], (24, 128))
    place = jnp.where(active > 0.0, rank - 1.0, -1.0)
    place = jnp.concatenate([place, jnp.full((104, 128), -1.0, f32)], axis=0).T
    position = across.astype(f32)
    value = (down - units).astype(f32)
    plan_ref[...] = jnp.full_like(plan_ref, units)
    last = lax.broadcasted_iota(jnp.int32, (1, 128), 1)
    chunks = jnp.floor((counts + (group - 0.5)) / group).astype(jnp.int32)
    begin = jnp.zeros((1, 128), jnp.int32)
    items = [jnp.full((1, 128), src_tiles * per, jnp.int32)] * 2
    for s in range(src_tiles):
        listed = jnp.sum(
            jnp.where(place[:, s : s + 1] == position, value, 0.0), axis=0, keepdims=True
        )
        plan_ref[s : s + 1, :] = jnp.where(
            last == 127, counts[s : s + 1], listed + units
        ).astype(jnp.int32)
        for k in range(2):
            along = last + 128 * k - begin
            inside = (along >= 0) & (along < chunks[s : s + 1])
            items[k] = jnp.where(inside, s * per + along, items[k])
        begin = begin + chunks[s : s + 1]
    plan_ref[src_tiles + 1 : src_tiles + 2, :] = items[0]
    plan_ref[src_tiles + 2 : src_tiles + 3, :] = items[1]
    plan_ref[src_tiles + 3 : src_tiles + 4, :] = begin
    copy.wait()


def pipeline(plan_ref, items, operand_ref, weights_ref, buffers, visit):
    tiles, depth, tile = weights_ref.shape
    per = (operand_ref.shape[0] // unit_rows - 1) // group

    def where(i):
        code = plan_ref[tiles + 1 + i // 128, lax.rem(i, 128)]
        s = code // per
        first = (code - s * per) * group
        return jnp.minimum(s, tiles - 1), [plan_ref[s, first + k] for k in range(group)]

    def step(j, carry):
        for k in range(span):
            s, units = where(span * j + k)
            rows = jnp.concatenate(
                [
                    operand_ref[pl.ds(pl.multiple_of(u * unit_rows, unit_rows), unit_rows), :]
                    for u in units
                ],
                axis=0,
            )
            buffers[k][...] = jnp.dot(rows, weights_ref[s], preferred_element_type=f32)
        for k in range(span):
            visit(*where(span * j + k), buffers[k])
        return carry

    lax.fori_loop(0, (items + span - 1) // span, step, 0)


def distance():
    row = lax.axis_index("row")
    return lax.rem(lax.axis_index("col") - row + 2 - lax.rem(row, 2) + 16, 16)


def on_duty(which):
    near = distance() < 4
    return near if which == 0 else jnp.logical_not(near)


def finish(
    known_ref, rest_ref, mass_ref, live_ref, parts_ref, base_ref, valid_ref, out_ref, new_ref
):
    apart = distance()
    odd = lax.rem(lax.axis_index("row"), 2) == 1
    here = (apart < 4) | (apart == 5) | (apart == 6)
    here |= (apart == jnp.where(odd, 15, 4)) | (apart == jnp.where(odd, 9, 10))
    total = jnp.where(here, known_ref[...], rest_ref[...])
    out_ref[...] = jnp.where(
        live_ref[...] > 0.0, (entropy * ln2) * (mass_ref[...] - total), 0.0
    )
    parts = [parts_ref[k] for k in range(parts_ref.shape[0])]
    top = functools.reduce(jnp.maximum, parts)
    log = top + jnp.log2(sum(jnp.exp2(p - top) for p in parts))
    new = base_ref[...] - (entropy * ln2) * log
    fine = (valid_ref[...] > 0.0) & (log > 0.5 * nothing)
    new_ref[...] = jnp.where(fine, new, 0.0).reshape(new_ref.shape)


def row_pass(
    which, sheet_ref, points_ref, need_ref, w0, w1, w2, w3, lse_ref,
    operand_ref, weights_ref, plan_ref, sem, total_ref, *buffers,
):
    tiles, depth, tile = weights_ref.shape
    lse_ref[...] = jnp.full_like(lse_ref, nothing)
    copy = pltpu.make_async_copy(sheet_ref, plan_ref, sem)

    def put(s, line):
        lse_ref[pl.ds(2 * s, 1), :] = line[:, 0:128]
        lse_ref[pl.ds(2 * s + 1, 1), :] = line[:, 128:256]

    def work():
        items = plan_ref[tiles + 3, 0]
        unpack_targets((w0, w1, w2, w3), operand_ref)
        total_ref[...] = jnp.zeros_like(total_ref)

        def visit(s, units, buffer):
            part = jnp.exp2(buffer[...]).reshape(4, unit_rows * group // 32, 8, tile)
            total_ref[s] += jnp.sum(jnp.sum(part, axis=1), axis=0)

        pipeline(plan_ref, items, operand_ref, weights_ref, buffers, visit)
        total = jnp.sum(total_ref[...], axis=1)
        lines = jnp.where(total > 0.0, jnp.log2(jnp.maximum(total, 1e-37)), nothing)
        for s in range(tiles):
            put(s, lines[s : s + 1, :])
        fine = (total > 1e-25) & (total < 1e30)
        bad = jnp.where(fine, 0.0, need_ref[...])

        @pl.when(jnp.max(bad) > 0.0)
        def _():
            def one_tile(s, carry):
                weights = weights_ref[s]

                def step(i, state):
                    high, total = state
                    unit = plan_ref[s, i]
                    rows = operand_ref[
                        pl.ds(pl.multiple_of(unit * unit_rows, unit_rows), unit_rows), :
                    ]
                    score = jnp.dot(rows, weights, preferred_element_type=f32)
                    score = score.reshape(unit_rows // 8, 8, tile)
                    new = jnp.maximum(high, jnp.max(score, axis=0))
                    total = total * jnp.exp2(high - new)
                    return new, total + jnp.sum(jnp.exp2(score - new[None]), axis=0)

                start = (jnp.full((8, tile), floor, f32), jnp.zeros((8, tile), f32))
                high, total = lax.fori_loop(0, plan_ref[s, 127], step, start)
                top = jnp.max(high, axis=0, keepdims=True)
                total = jnp.sum(total * jnp.exp2(high - top), axis=0, keepdims=True)
                put(s, jnp.where(total > 0.0, top + jnp.log2(jnp.maximum(total, 1e-37)), nothing))
                return carry

            lax.fori_loop(0, tiles, one_tile, 0)

    @pl.when(on_duty(which))
    def _():
        copy.start()
        load_weights(points_ref, weights_ref, None)
        copy.wait()
        pl.when(plan_ref[tiles + 3, 0] > 0)(work)


def column_pass(
    which, sheet_ref, points_ref, need_ref, w0, w1, w2, w3, lse_ref, mass_ref, other_ref, out_ref,
    operand_ref, weights_ref, plan_ref, sem, total_ref, high_ref, *buffers,
):
    tiles, depth, tile = weights_ref.shape
    out_ref[...] = other_ref[...]
    copy = pltpu.make_async_copy(sheet_ref, plan_ref, sem)

    def work():
        items = plan_ref[tiles + 3, 0]
        unpack_targets((w0, w1, w2, w3), operand_ref)
        total_ref[...] = jnp.zeros_like(total_ref)

        def visit(s, units, buffer):
            for k, u in enumerate(units):
                where = pl.ds(pl.multiple_of(u * unit_rows, unit_rows), unit_rows)
                part = jnp.exp2(buffer[k * unit_rows : (k + 1) * unit_rows, :])
                total_ref[where, :] += part[:, 0:128] + part[:, 128:256]

        pipeline(plan_ref, items, operand_ref, weights_ref, buffers, visit)
        eye = lax.broadcasted_iota(jnp.int32, (128, 128), 0) == lax.broadcasted_iota(
            jnp.int32, (128, 128), 1
        )

        def to_row(column):
            return jnp.sum(
                jnp.where(eye[0 : column.shape[0]], column, 0.0), axis=0, keepdims=True
            )

        blocks = [
            (shard, slice(128 * i, 128 * i + size), slice(shard * 288 + 128 * i, shard * 288 + 128 * i + size))
            for shard in range(out_ref.shape[0])
            for i, size in enumerate((128, 128, 32))
        ]
        bad = jnp.zeros((1, 128), f32)
        for shard, lanes, where in blocks:
            sums = to_row(jnp.sum(total_ref[where, :], axis=1, keepdims=True))
            size = lanes.stop - lanes.start
            out_ref[shard, :, lanes] = jnp.where(
                sums > 0.0, jnp.log2(jnp.maximum(sums, 1e-37)), nothing
            )[:, 0:size]
            needed = need_ref[3 * shard + lanes.start // 128 : 3 * shard + lanes.start // 128 + 1, :]
            bad = jnp.maximum(bad, jnp.where(sums > 1e-25, 0.0, needed))

        @pl.when(jnp.max(bad) > 0.0)
        def _():
            total_ref[...] = jnp.zeros_like(total_ref)
            high_ref[...] = jnp.full_like(high_ref, floor)

            def one_tile(s, carry):
                def step(i, inner):
                    unit = plan_ref[s, i]
                    where = pl.ds(pl.multiple_of(unit * unit_rows, unit_rows), unit_rows)
                    score = jnp.dot(
                        operand_ref[where, :], weights_ref[s], preferred_element_type=f32
                    )
                    a, b = score[:, 0:128], score[:, 128:256]
                    old = high_ref[where, :]
                    new = jnp.maximum(old, jnp.maximum(a, b))
                    high_ref[where, :] = new
                    total_ref[where, :] = (
                        total_ref[where, :] * jnp.exp2(old - new)
                        + jnp.exp2(a - new)
                        + jnp.exp2(b - new)
                    )
                    return inner

                lax.fori_loop(0, plan_ref[s, 127], step, 0)
                return carry

            lax.fori_loop(0, tiles, one_tile, 0)

            for shard, lanes, where in blocks:
                high = high_ref[where, :]
                top = jnp.max(high, axis=1, keepdims=True)
                rest = total_ref[where, :] * jnp.exp2(high - top)
                sums = to_row(jnp.sum(rest, axis=1, keepdims=True))
                size = lanes.stop - lanes.start
                out_ref[shard, :, lanes] = jnp.where(
                    sums > 0.0, to_row(top) + jnp.log2(jnp.maximum(sums, 1e-37)), nothing
                )[:, 0:size]

    @pl.when(on_duty(which))
    def _():
        copy.start()
        load_weights(points_ref, weights_ref, mass_ref[...] - lse_ref[...])
        copy.wait()
        pl.when(plan_ref[tiles + 3, 0] > 0)(work)


def log_sum(parts):
    top = functools.reduce(jnp.maximum, parts)
    total = sum(jnp.exp2(p - top) for p in parts)
    return top + jnp.log2(total)


def roles(parity, cols):
    four = [d % cols for d in ((-2, -1, 0, 1), (-1, 0, 1, 2))[parity]]
    lead = [0, (1, -1)[parity] % cols]
    near = lead + [d for d in four if d not in lead]
    out = [(2, -2)[parity] % cols, cols // 2]
    begin = four[0]
    out += [(begin + 5) % cols, (begin + 6) % cols]
    return near, out + [d for d in range(cols) if d not in near and d not in out]


def filled(hops, count, cols):
    found = dict(hops)
    back = {d: s for s, d in hops}
    for rank in range(4):
        free = [d for d in range(count) if d not in back]
        for s in [s for s in range(count) if s not in found]:
            if rank == 0:
                picks = [back[s]] if s in back and back[s] in free else []
            elif rank == 1:
                picks = [s ^ 1] if s ^ 1 in free else []
            else:
                picks = [d for d in free if d != s and (d // cols == s // cols or rank == 3)]
                picks.sort(key=lambda d: min((d - s) % cols, (s - d) % cols))
            if picks:
                found[s] = picks[0]
                back[picks[0]] = s
                free.remove(picks[0])
    return sorted(found.items())


def shards(src_points, dst_points, dst_potential, partners, partner_count, src_count, dst_count):
    src_tiles = src_count.shape[0]
    dst_tiles = dst_count.shape[0]
    tile = src_points.shape[0] // src_tiles
    slots = partners.shape[1]
    rows = lax.axis_size("row")
    cols = lax.axis_size("col")
    row_here = lax.axis_index("row")
    col_here = lax.axis_index("col")
    share = dst_points.shape[0]
    points = dst_tiles * tile
    smem = pl.BlockSpec(memory_space=pltpu.SMEM)
    vmem = pl.BlockSpec(memory_space=pltpu.VMEM)
    anywhere = pl.BlockSpec(memory_space=pl.ANY)
    params = pltpu.CompilerParams(vmem_limit_bytes=24 * 1024 * 1024)
    places = [roles(r % 2, cols) for r in range(rows)]
    near = [[(r + d) % cols for d in places[r][0]] for r in range(rows)]
    far = [[(r + d) % cols for d in places[r][1]] for r in range(rows)]
    parity = lax.rem(row_here, 2)
    apart = lax.rem(col_here - row_here + 2 - parity + cols, cols)
    in_near = apart < 4
    in_far = (
        (apart == 5)
        | (apart == 6)
        | (apart == jnp.where(parity == 0, 4, cols - 1))
        | (apart == jnp.where(parity == 0, 10, 9))
    )

    def send(a, hops, full=True):
        hops = [(s[0] * cols + s[1], d[0] * cols + d[1]) for s, d in hops]
        return lax.ppermute(a, ("row", "col"), filled(hops, rows * cols, cols) if full else hops)

    every = [(r, c) for r in range(rows) for c in range(cols)]

    wire = pl.pallas_call(
        pack_targets,
        out_shape=jax.ShapeDtypeStruct((share // 2 + 8, 128), f32),
        in_specs=[anywhere] * 3,
        out_specs=vmem,
        scratch_shapes=[
            pltpu.VMEM((128, 384), f32),
            pltpu.VMEM((8, 384), f32),
            pltpu.SMEM((dst_tiles,), jnp.int32),
            pltpu.VMEM((64, share), f32),
            pltpu.VMEM((share,), f32),
            pltpu.SemaphoreType.DMA((3,)),
        ],
        compiler_params=pltpu.CompilerParams(vmem_limit_bytes=60 * 1024 * 1024),
    )(dst_count, dst_points.T, dst_potential)

    def around(r, dx, dy):
        return (r // ring + dx) % ring * ring + (r + dy) % ring

    def first_hop(r, c, k):
        return around(r, 0, k) if c % 2 == 0 else around(r, k, 0)

    def second_hop(r, c, k):
        return around(r, k, 0) if c % 2 == 0 else around(r, 0, k)

    slot_on = jnp.arange(slots, dtype=jnp.int32)[None, :] < partner_count[:, None]
    local = jnp.where(slot_on, partners - col_here * dst_tiles, -1)
    plan, near_wire = pl.pallas_call(
        plan_work,
        out_shape=(
            jax.ShapeDtypeStruct((24, 128), jnp.int32),
            jax.ShapeDtypeStruct(wire.shape, f32),
        ),
        in_specs=[smem, vmem, anywhere],
        out_specs=(vmem, vmem),
        scratch_shapes=[pltpu.SemaphoreType.DMA],
        compiler_params=params,
    )(dst_count, jnp.pad(local, ((0, 24 - src_tiles), (0, 0)), constant_values=-1), wire)
    bundle = pl.pallas_call(
        join,
        out_shape=jax.ShapeDtypeStruct((ring,) + wire.shape, f32),
        in_specs=[vmem] * ring,
        out_specs=vmem,
        compiler_params=params,
    )(near_wire, *[send(wire, [((r, c), (first_hop(r, c, k), c)) for r, c in every]) for k in (1, 2, 3)])
    busy = [set(near[r] + far[r][:2]) for r in range(rows)]
    plan, local, dst_count, src_count, bundle = lax.optimization_barrier(
        (plan, local, dst_count, src_count, bundle)
    )
    wires = [bundle] + [
        send(
            bundle,
            [
                ((r, c), (second_hop(r, c, k), c))
                for r, c in every
                if c in busy[second_hop(r, c, k)]
            ],
            full=False,
        )
        for k in (1, 2, 3)
    ]
    place = jnp.arange(tile, dtype=jnp.int32)
    src_live = place[None, :] < src_count[:, None]
    dst_live = place[None, :] < dst_count[:, None]
    wanted = jnp.any(local[:, :, None] == jnp.arange(dst_tiles, dtype=jnp.int32), axis=1)
    src_need = jnp.where(src_live & jnp.any(wanted, axis=1)[:, None], 1.0, 0.0)
    dst_need = jnp.where(dst_live & jnp.any(wanted, axis=0)[:, None], 1.0, 0.0)
    dst_need = jnp.pad(dst_need.reshape(rows, share), ((0, 0), (0, 384 - share)))
    dst_need = dst_need.reshape(rows * 3, 128)
    counted = jnp.repeat(src_count.astype(f32), 2)
    half_live = (place[:128][None, :] + 128 * (jnp.arange(2 * src_tiles) % 2)[:, None]) < jnp.repeat(
        src_count, 2
    )[:, None]
    all_src = src_tiles * rows
    mass = jnp.where(half_live, -jnp.log2(counted)[:, None] - math.log2(all_src), nothing)

    scratch = [
        pltpu.VMEM((points + unit_rows, 256), bf16),
        pltpu.VMEM((src_tiles, 256, tile), bf16),
    ]
    buffers = [pltpu.VMEM((unit_rows * group, tile), f32)] * span
    heavy = pl.CostEstimate(flops=8_000_000_000, bytes_accessed=4_000_000, transcendentals=8_000_000)
    light = pl.CostEstimate(flops=100_000_000, bytes_accessed=100_000, transcendentals=100_000)
    turned = src_points.T

    halves = 2 * src_tiles
    scratch += [pltpu.SMEM((24, 128), jnp.int32), pltpu.SemaphoreType.DMA]

    def sum_rows(which, cost):
        return pl.pallas_call(
            functools.partial(row_pass, which),
            out_shape=jax.ShapeDtypeStruct((halves, tile // 2), f32),
            in_specs=[anywhere] + [vmem] * (2 + ring),
            out_specs=vmem,
            scratch_shapes=scratch + [pltpu.VMEM((src_tiles, 8, tile), f32)] + buffers,
            compiler_params=params,
            cost_estimate=cost,
        )(plan, turned, src_need, *wires)

    def sum_columns(which, lse, other, cost):
        return pl.pallas_call(
            functools.partial(column_pass, which),
            out_shape=jax.ShapeDtypeStruct((rows, 1, share), f32),
            in_specs=[anywhere] + [vmem] * (5 + ring),
            out_specs=vmem,
            scratch_shapes=scratch + [pltpu.VMEM((points + unit_rows, 128), f32)] * 2 + buffers,
            compiler_params=params,
            cost_estimate=cost,
        )(plan, turned, dst_need, *wires, lse, mass, other)

    far_lse = sum_rows(1, light)
    loops = [
        [(r, c) for c in (far[r][k], near[r][k], far[r][k] ^ 1)] for r in range(rows) for k in (0, 1)
    ]
    hops = [(loop[i], loop[(i + 1) % 3]) for loop in loops for i in range(3)]
    for r in range(rows):
        taken = near[r] + far[r][:2] + [c ^ 1 for c in far[r][:2]]
        spare = [c for c in range(cols) if c not in taken][:2]
        for a, c in zip(near[r][2:], spare):
            hops += [((r, a), (r, c)), ((r, c), (r, a))]
    early = send(far_lse, hops)
    near_lse = sum_rows(0, heavy)
    got_early = (col_here == row_here) | (col_here == row_here + 1 - 2 * parity)
    lse = log_sum([near_lse, jnp.where(got_early, early, nothing)])

    def pairs(test):
        return [((r, c), (r, d)) for r in range(rows) for c in near[r] for d in near[r] if test(c, d)]

    lse = log_sum(
        [
            lse,
            send(lse, [((r, c), (r, c ^ 1)) for r, c in every]),
            send(lse, pairs(lambda c, d: (c - d) % cols in (2, cols - 2))),
            send(lse, pairs(lambda c, d: (c - (d ^ 1)) % cols in (2, cols - 2))),
        ]
    )
    spread = send(lse, [((r, near[r][k]), (r, far[r][k])) for r in range(rows) for k in range(4)])
    blank = jnp.full((rows, 1, share), nothing, f32)
    near_part = sum_columns(0, lse, blank, heavy)
    col_part = sum_columns(1, spread, near_part, light)
    known = jnp.where(in_far, spread, lse)
    known, near_part = lax.optimization_barrier((known, near_part))
    rest = send(
        known,
        [((r, (near[r] + far[r])[k]), (r, far[r][4 + k])) for r in range(rows) for k in range(8)],
    )
    parts = lax.all_to_all(col_part, "row", 0, 0)
    spot = row_here * share + jnp.arange(share, dtype=jnp.int32)
    spot_tile = spot // tile
    spot_count = jnp.sum(
        jnp.where(
            spot_tile[:, None] == jnp.arange(dst_tiles, dtype=jnp.int32)[None, :],
            dst_count[None, :],
            0,
        ),
        axis=1,
    )
    valid = jnp.where(spot - spot_tile * tile < spot_count, 1.0, 0.0)[None, :]
    base = dst_potential - entropy * (
        jnp.log(spot_count.astype(f32)) + math.log(dst_tiles * cols)
    )
    src_potential, dst_new = pl.pallas_call(
        finish,
        out_shape=(
            jax.ShapeDtypeStruct((halves, tile // 2), f32),
            jax.ShapeDtypeStruct((share,), f32),
        ),
        in_specs=[vmem] * 7,
        out_specs=(vmem, vmem),
        compiler_params=params,
    )(known, rest, mass, half_live.astype(f32), parts, base[None, :], valid)
    src_potential = src_potential.reshape(-1)
    return src_potential, dst_new


def solution(mesh):
    in_specs = (
        P("row", None),
        P(("col", "row"), None),
        P(("col", "row")),
        P("row", None),
        P("row"),
        P("row"),
        P("col"),
    )
    out_specs = (P("row"), P(("col", "row")))
    return jax.shard_map(shards, mesh=mesh, in_specs=in_specs, out_specs=out_specs, check_vma=False)
```
